32 devices in a mesh: groups: 2 (over y), dp: 2 (over core), tensor: 8 (over z, x).
Axes of the slice: x: 2, y: 2, z: 4, core: 2. Of those that a mesh axis runs over, the one named last changes fastest.
Arguments:
- attended: bfloat16 [256, 8192], P(('groups', 'dp'), 'tensor'), parts along dimension 0, may hold values from -12 to 12
- out_weight: bfloat16 [8192, 16384], P('tensor'), may hold values from -0.09375 to 0.09375
- residual: bfloat16 [256, 16384], P(('groups', 'dp'), 'tensor'), parts along dimension 0, may hold values from -40 to 40
- norm_gain: bfloat16 [16384], P('tensor'), may hold values from 0.099609375 to 1.8984375
- norm_bias: bfloat16 [16384], P('tensor'), may hold values from -3 to 3
Outputs:
- stream_out: bfloat16 [256, 16384], P(('groups', 'dp'), 'tensor'), parts along dimension 0
- normed: bfloat16 [256, 16384], P(('groups', 'dp')), parts along dimension 0
The draws below stay inside these ranges and needn't reach their ends.
There are 2 independent parts, one for each index of `groups`. The reference program is written for one: setup_inputs(seed, part) draws one part's arguments, and reference() takes and returns one part's arrays. A program takes and returns all parts, laid end to end along the dimension named above; an argument that names none is the same for every part. Nothing has to cross between parts.
All inputs are finite; a program needn't handle non-finite values.
Results may differ from the reference program's by a relative error of at most 0.008.
Values may be sent and summed in bfloat16 or wider, within the bound.
No kernel may reach another device: no remote copies, remote signals or barrier semaphores. Data moves between devices by JAX's collectives and lax.ppermute only.
A program may use at most 128 MiB of HBM per device.

```python
import math
import jax
import jax.numpy as jnp
from jax import lax

MODEL_DIM = 16384
HEAD_DIM = 128
HEADS = 64
BLOCK_LEN = 128
ROWS = 128


def draw_residual(key, part):
    key = jax.random.fold_in(key, 7)
    row_key, entry_key = jax.random.split(key)
    columns = jnp.arange(MODEL_DIM, dtype=jnp.float32) / MODEL_DIM
    row_scale = jnp.exp(jax.random.uniform(row_key, (ROWS, 1), jnp.float32, math.log(0.3), math.log(3.0)))
    entries = jnp.clip(jax.random.normal(entry_key, (ROWS, MODEL_DIM), jnp.float32), -4.0, 4.0)
    column_scale = 10.0 ** (columns - 0.5)
    values = row_scale * entries * column_scale[None, :]
    return values.astype(jnp.bfloat16)


def spiked(drawn, own_key, source, target, shards_of, factor):
    owner, partner = [(jnp.arange(drawn.shape[dim]) // (drawn.shape[dim] // shards_of)).reshape([-1 if axis == dim else 1 for axis in range(drawn.ndim)]) for dim in (source, target)]
    chosen = jax.random.permutation(own_key, shards_of)[partner]
    strong = (owner == chosen) | (owner == (partner + shards_of // 2) % shards_of)
    return jnp.where(strong, factor * drawn, drawn)


def steps_of(own_key, dims, pieces, smallest, high):
    loudness = 1.0
    for dim, parts in pieces:
        draws = jax.random.uniform(jax.random.fold_in(jax.random.fold_in(own_key, 6), dim), (parts,), jnp.float32, smallest / len(pieces), high / len(pieces))
        loudness = loudness * jnp.repeat(jnp.exp(draws), dims[dim] // parts).reshape((-1,) + (1,) * (len(dims) - 1 - dim))
    return loudness


def centred(rng, shape, deviation, reach, cuts=(), kind=jnp.bfloat16):
    gain = steps_of(rng, shape, cuts, -0.22, 0.18) if cuts else 1.0
    values = jax.random.normal(rng, shape, jnp.float32) * deviation * gain
    return jnp.minimum(jnp.maximum(values, -reach), reach).astype(kind)


def heavy_noise(own_key, dims, scale, most, shards, heavy, kind=jnp.bfloat16):
    result = scale * jax.random.normal(own_key, dims, jnp.float32)
    if shards:
        result = result * steps_of(own_key, dims, shards, -0.22, 0.18)
    return jnp.clip(spiked(result, jax.random.fold_in(own_key, 3), *heavy), -most, most).astype(kind)


def setup_inputs(seed: int = 0, part: int = 0) -> dict:
    key_list = jax.random.split(jax.random.key(seed), 6)
    part_keys = jax.random.split(jax.random.fold_in(key_list[5], part), 6)
    return {
        "attended": centred(part_keys[0], (ROWS, HEADS * HEAD_DIM), 2.0, 12.0, ((0, 2), (1, 8))),
        "out_weight": heavy_noise(key_list[1], (HEADS * HEAD_DIM, MODEL_DIM), (HEADS * HEAD_DIM) ** -0.5, 0.09375, ((0, 8),), (0, 1, 8, 2.0)),
        "residual": draw_residual(jax.random.fold_in(jax.random.fold_in(key_list[5], part), 71), part),
        "norm_gain": jnp.clip(1.0 + 0.18 * jax.random.normal(key_list[3], (MODEL_DIM,), jnp.float32), 0.099609375, 1.8984375).astype(jnp.bfloat16),
        "norm_bias": centred(key_list[4], (MODEL_DIM,), 0.5, 3.0, ((0, 8),)),
    }


def hadamard(length):
    indices = lax.iota(jnp.int32, length)
    parity = jnp.zeros((length, length), jnp.int32)
    for bit_index in range(length.bit_length() - 1):
        column = jnp.bitwise_and(jnp.right_shift(indices, bit_index), 1)
        parity = parity + column[:, None] * column[None, :]
    sign_table = 1 - 2 * jnp.bitwise_and(parity, 1)
    return sign_table.astype(jnp.float32) / math.sqrt(length)

def rotate(values, rotation):
    length = rotation.shape[0]
    flat = jnp.dot(values.reshape(-1, length), rotation, precision=lax.Precision.HIGHEST)
    return flat.reshape(values.shape)

def encode(values, length):
    blocks = values.reshape(values.shape[0], -1, length)
    largest = lax.optimization_barrier(jnp.max(jnp.abs(blocks), axis=2))
    scales = (largest / 448.0 + 1e-06).astype(jnp.bfloat16)
    quanta = (blocks / scales.astype(jnp.float32)[:, :, None]).astype(jnp.bfloat16)
    return (quanta.reshape(values.shape), scales)

def decode(quanta, scales, rotation):
    length = rotation.shape[0]
    blocks = quanta.astype(jnp.float32).reshape(quanta.shape[0], -1, length)
    blocks = blocks * scales.astype(jnp.float32)[:, :, None]
    return rotate(blocks.reshape(quanta.shape), rotation).astype(jnp.bfloat16)

def reference(attended, out_weight, residual, norm_gain, norm_bias):
    rotation = hadamard(BLOCK_LEN)
    projected = jnp.dot(attended, out_weight, preferred_element_type=jnp.float32)
    stream = residual.astype(jnp.float32) + projected
    centre = lax.optimization_barrier(jnp.mean(stream, axis=1, keepdims=True))
    offsets = stream - centre
    spread = lax.optimization_barrier(jnp.mean(offsets * offsets, axis=1, keepdims=True))
    normal_rows = offsets * lax.rsqrt(spread + 1e-05) * norm_gain.astype(jnp.float32) + norm_bias.astype(jnp.float32)
    quanta, scales = encode(rotate(normal_rows, rotation), BLOCK_LEN)
    return (stream.astype(jnp.bfloat16), decode(quanta, scales, rotation))
```

```python
import math

import jax
import jax.numpy as jnp
from jax import lax
from jax.sharding import PartitionSpec as P

BLOCK_LEN = 128


def hadamard(length):
    indices = lax.iota(jnp.int32, length)
    parity = jnp.zeros((length, length), jnp.int32)
    for bit_index in range(length.bit_length() - 1):
        column = jnp.bitwise_and(jnp.right_shift(indices, bit_index), 1)
        parity = parity + column[:, None] * column[None, :]
    sign_table = 1 - 2 * jnp.bitwise_and(parity, 1)
    return sign_table.astype(jnp.float32) / math.sqrt(length)


def rotate(values, rotation):
    length = rotation.shape[0]
    flat = jnp.dot(values.reshape(-1, length), rotation, precision=lax.Precision.HIGHEST)
    return flat.reshape(values.shape)


def encode(values, length):
    blocks = values.reshape(values.shape[0], -1, length)
    largest = jnp.max(jnp.abs(blocks), axis=2)
    scales = (largest / 448.0 + 1e-06).astype(jnp.bfloat16)
    quanta = (blocks / scales.astype(jnp.float32)[:, :, None]).astype(jnp.bfloat16)
    return (quanta.reshape(values.shape), scales)


def decode(quanta, scales, rotation):
    length = rotation.shape[0]
    blocks = quanta.astype(jnp.float32).reshape(quanta.shape[0], -1, length)
    blocks = blocks * scales.astype(jnp.float32)[:, :, None]
    return rotate(blocks.reshape(quanta.shape), rotation).astype(jnp.bfloat16)


def body(attended, out_weight, residual, norm_gain, norm_bias):
    rotation = hadamard(BLOCK_LEN)
    n = lax.axis_size("tensor")
    width = out_weight.shape[1]
    projected = jnp.dot(attended, out_weight, preferred_element_type=jnp.float32)
    own = lax.psum_scatter(
        projected.astype(jnp.bfloat16), "tensor", scatter_dimension=1, tiled=True
    )
    stream = residual.astype(jnp.float32) + own.astype(jnp.float32)
    total = jnp.sum(stream, axis=1, keepdims=True)
    local_mean = total / stream.shape[1]
    local_square = jnp.sum((stream - local_mean) ** 2, axis=1, keepdims=True)
    stats = jnp.concatenate([local_mean, local_square], axis=1)
    parts = [stats]
    for k in range(1, n):
        parts.append(
            lax.ppermute(stats, "tensor", [(i, (i + k) % n) for i in range(n)])
        )
    means = jnp.stack([p[:, 0] for p in parts])
    squares = jnp.stack([p[:, 1] for p in parts])
    centre = jnp.mean(means, axis=0)
    spread = (
        jnp.sum(squares, axis=0)
        + stream.shape[1] * jnp.sum((means - centre) ** 2, axis=0)
    ) / width
    offsets = stream - centre[:, None]
    normal_rows = offsets * lax.rsqrt(spread + 1e-05)[:, None] * norm_gain.astype(
        jnp.float32
    ) + norm_bias.astype(jnp.float32)
    quanta, scales = encode(rotate(normal_rows, rotation), BLOCK_LEN)
    normed = decode(quanta, scales, rotation)
    normed = lax.all_gather(normed, "tensor", axis=1, tiled=True)
    return (stream.astype(jnp.bfloat16), normed)


def solution(mesh):
    placed = (
        P(("groups", "dp"), "tensor"),
        P("tensor", None),
        P(("groups", "dp"), "tensor"),
        P("tensor"),
        P("tensor"),
    )
    return jax.shard_map(
        body,
        mesh=mesh,
        in_specs=placed,
        out_specs=(P(("groups", "dp"), "tensor"), P(("groups", "dp"), None)),
        check_vma=False,
    )
```

```python
import functools
import math

import jax
import jax.numpy as jnp
from jax import lax
from jax.experimental import pallas as pl
from jax.experimental.pallas import tpu as pltpu
from jax.sharding import PartitionSpec as P

BLOCK_LEN = 128
VMEM_BYTES = 40 * 1024 * 1024


def factors(n):
    inner = 1 << ((n.bit_length() - 1) // 2)
    return n // inner, inner


def tile_width(width):
    for tile in (1024, 512, 256, 128):
        if width % tile == 0:
            return tile
    return width


def signs(length):
    rows = lax.broadcasted_iota(jnp.int32, (length, length), 0)
    columns = lax.broadcasted_iota(jnp.int32, (length, length), 1)
    common = jnp.bitwise_and(rows, columns)
    parity = jnp.zeros((length, length), jnp.int32)
    for bit_index in range(length.bit_length() - 1):
        parity = parity + jnp.bitwise_and(jnp.right_shift(common, bit_index), 1)
    return (1 - 2 * jnp.bitwise_and(parity, 1)).astype(jnp.bfloat16)


def product_kernel(which, rows_ref, weight_ref, out_ref):
    del which
    out_ref[0] = jnp.dot(
        rows_ref[...], weight_ref[...], preferred_element_type=jnp.float32
    ).astype(out_ref.dtype)


def product(attended, weight, inner, nz, nx, halves, half, dtype):
    rows, depth = attended.shape
    part = weight.shape[1] // (nz * nx * halves)
    tile = tile_width(part)
    per = part // tile

    def weight_index(z, j, which):
        return (0, ((z * nx + which[0]) * halves + half) * per + j)

    return pl.pallas_call(
        product_kernel,
        out_shape=jax.ShapeDtypeStruct((nz, rows, part), dtype),
        grid_spec=pltpu.PrefetchScalarGridSpec(
            num_scalar_prefetch=1,
            grid=(nz, per),
            in_specs=[
                pl.BlockSpec((rows, depth), lambda z, j, which: (0, 0)),
                pl.BlockSpec((depth, tile), weight_index),
            ],
            out_specs=pl.BlockSpec((1, rows, tile), lambda z, j, which: (z, 0, j)),
        ),
        compiler_params=pltpu.CompilerParams(vmem_limit_bytes=VMEM_BYTES),
        cost_estimate=pl.CostEstimate(
            flops=2 * rows * depth * part * nz,
            bytes_accessed=2 * depth * part * nz,
            transcendentals=0,
        ),
    )(inner.reshape(1), attended, weight)


def rows_kernel(stream_ref, centre_ref, inverse_ref, gain_ref, bias_ref, out_ref):
    rows, width = stream_ref.shape
    blocks = width // BLOCK_LEN
    table = signs(BLOCK_LEN)
    unit = 1.0 / math.sqrt(BLOCK_LEN)
    gain = gain_ref[...].astype(jnp.float32)
    bias = bias_ref[...].astype(jnp.float32)
    normal = (stream_ref[...] - centre_ref[...]) * inverse_ref[...] * gain + bias
    normal = jnp.concatenate(
        [normal[:, b * BLOCK_LEN : (b + 1) * BLOCK_LEN] for b in range(blocks)], axis=0
    )
    coded = jnp.zeros(normal.shape, jnp.float32)
    rest = normal
    for _ in range(3):
        piece = rest.astype(jnp.bfloat16)
        coded = coded + jnp.dot(piece, table, preferred_element_type=jnp.float32)
        rest = rest - piece.astype(jnp.float32)
    coded = coded * unit
    largest = jnp.max(jnp.abs(coded), axis=1, keepdims=True)
    scales = (largest / 448.0 + 1e-06).astype(jnp.bfloat16).astype(jnp.float32)
    quanta = (coded / scales).astype(jnp.bfloat16)
    back = jnp.dot(quanta, table, preferred_element_type=jnp.float32) * (scales * unit)
    back = back.astype(out_ref.dtype)
    for b in range(blocks):
        out_ref[:, b * BLOCK_LEN : (b + 1) * BLOCK_LEN] = back[b * rows : (b + 1) * rows]


def row_work(stream, centre, inverse, gain, bias):
    rows, width = stream.shape
    return pl.pallas_call(
        rows_kernel,
        out_shape=jax.ShapeDtypeStruct((rows, width), jnp.bfloat16),
        compiler_params=pltpu.CompilerParams(vmem_limit_bytes=VMEM_BYTES),
    )(stream, centre, inverse, gain.reshape(1, width), bias.reshape(1, width))


def place_kernel(which, piece_ref, *refs):
    del which
    refs[-1][...] = piece_ref[0]


def place(whole, pieces, inner, nx, halves, half):
    nz, rows, part = pieces.shape
    earlier = [] if whole is None else [whole]
    return pl.pallas_call(
        place_kernel,
        out_shape=jax.ShapeDtypeStruct((rows, nz * nx * halves * part), pieces.dtype),
        grid_spec=pltpu.PrefetchScalarGridSpec(
            num_scalar_prefetch=1,
            grid=(nz,),
            in_specs=[
                pl.BlockSpec((1, rows, part), lambda z, which: (z, 0, 0)),
            ]
            + [pl.BlockSpec(memory_space=pl.ANY)] * len(earlier),
            out_specs=pl.BlockSpec(
                (rows, part), lambda z, which: (0, (z * nx + which[0]) * halves + half)
            ),
        ),
        input_output_aliases={2: 0} if earlier else {},
        cost_estimate=pl.CostEstimate(
            flops=0, bytes_accessed=4 * nz * rows * part, transcendentals=0
        ),
    )(inner.reshape(1), pieces, *earlier)


def body(attended, out_weight, residual, norm_gain, norm_bias):
    n = lax.axis_size("tensor")
    nz, nx = factors(n)
    width = out_weight.shape[1]
    local = width // n
    halves = 2 if local % (2 * BLOCK_LEN) == 0 else 1
    part = local // halves
    me = lax.axis_index("tensor")
    inner = me % nx
    along_z = [[z * nx + x for z in range(nz)] for x in range(nx)]
    swap = [
        [(z * nx + x, z * nx + (x ^ j)) for z in range(nz) for x in range(nx)]
        for j in range(nx)
    ]

    own = []
    for half in range(halves):
        sent = []
        for j in range(1, nx):
            piece = product(attended, out_weight, inner ^ j, nz, nx, halves, half, jnp.bfloat16)
            sent.append(lax.ppermute(piece, "tensor", swap[j]))
        kept = product(attended, out_weight, inner, nz, nx, halves, half, jnp.float32)
        for piece in sent:
            kept = kept + piece.astype(jnp.float32)
        arrived = lax.all_to_all(
            kept.astype(jnp.bfloat16), "tensor", 0, 0, axis_index_groups=along_z, tiled=True
        )
        base = residual[:, half * part : (half + 1) * part].astype(jnp.float32)
        own.append(base + jnp.sum(arrived.astype(jnp.float32), axis=0))
    stream = jnp.concatenate(own, axis=1)

    mean = jnp.mean(stream, axis=1)
    square = jnp.sum((stream - mean[:, None]) ** 2, axis=1)
    stats = jnp.stack([mean, square])
    stats = lax.all_to_all(
        jnp.broadcast_to(stats[None], (n,) + stats.shape), "tensor", 0, 0, tiled=True
    )
    centre = jnp.mean(stats[:, 0], axis=0)
    spread = (
        jnp.sum(stats[:, 1], axis=0) + local * jnp.sum((stats[:, 0] - centre) ** 2, axis=0)
    ) / width
    inverse = lax.rsqrt(spread + 1e-05)

    normed = row_work(stream, centre[:, None], inverse[:, None], norm_gain, norm_bias)
    whole = None
    for half in range(halves):
        piece = normed[:, half * part : (half + 1) * part]
        line = lax.all_to_all(
            jnp.broadcast_to(piece[None], (nz,) + piece.shape),
            "tensor",
            0,
            0,
            axis_index_groups=along_z,
            tiled=True,
        )
        whole = place(whole, line, inner, nx, halves, half)
        for j in range(1, nx):
            other = lax.ppermute(line, "tensor", swap[j])
            whole = place(whole, other, inner ^ j, nx, halves, half)
    return (stream.astype(jnp.bfloat16), whole)


def solution(mesh):
    placed = (
        P(("groups", "dp"), "tensor"),
        P("tensor", None),
        P(("groups", "dp"), "tensor"),
        P("tensor"),
        P("tensor"),
    )
    return jax.shard_map(
        body,
        mesh=mesh,
        in_specs=placed,
        out_specs=(P(("groups", "dp"), "tensor"), P(("groups", "dp"), None)),
        check_vma=False,
    )
```

```python
import functools
import math

import jax
import jax.numpy as jnp
from jax import lax
from jax.experimental import pallas as pl
from jax.experimental.pallas import tpu as pltpu
from jax.sharding import PartitionSpec as P

BLOCK_LEN = 128
LANES = 128
VMEM_BYTES = 40 * 1024 * 1024


def factors(n):
    inner = 1 << ((n.bit_length() - 1) // 2)
    return n // inner, inner


def tile_width(width, most):
    while width % most:
        most //= 2
    return most


def signs(length):
    rows = lax.broadcasted_iota(jnp.int32, (length, length), 0)
    columns = lax.broadcasted_iota(jnp.int32, (length, length), 1)
    common = jnp.bitwise_and(rows, columns)
    parity = jnp.zeros((length, length), jnp.int32)
    for bit_index in range(length.bit_length() - 1):
        parity = parity + jnp.bitwise_and(jnp.right_shift(common, bit_index), 1)
    return (1 - 2 * jnp.bitwise_and(parity, 1)).astype(jnp.bfloat16)


def product_kernel(which, rows_ref, weight_ref, out_ref):
    del which
    out_ref[...] = jnp.dot(
        rows_ref[...], weight_ref[...], preferred_element_type=jnp.float32
    ).astype(out_ref.dtype)


def product(attended, weight, target, local, dtype):
    rows, depth = attended.shape
    tile = tile_width(local, 512)
    per = local // tile
    return pl.pallas_call(
        product_kernel,
        out_shape=jax.ShapeDtypeStruct((rows, local), dtype),
        grid_spec=pltpu.PrefetchScalarGridSpec(
            num_scalar_prefetch=1,
            grid=(per,),
            in_specs=[
                pl.BlockSpec((rows, depth), lambda j, which: (0, 0)),
                pl.BlockSpec((depth, tile), lambda j, which: (0, which[0] * per + j)),
            ],
            out_specs=pl.BlockSpec((rows, tile), lambda j, which: (0, j)),
        ),
        compiler_params=pltpu.CompilerParams(vmem_limit_bytes=VMEM_BYTES),
        cost_estimate=pl.CostEstimate(
            flops=2 * rows * depth * local,
            bytes_accessed=2 * depth * local,
            transcendentals=0,
        ),
        name="product",
    )(target.reshape(1), attended, weight)


def stream_kernel(count, residual_ref, *refs):
    terms, (half_ref, stats_ref) = refs[:count], refs[count:]
    stream = residual_ref[...].astype(jnp.float32)
    for term in terms:
        stream = stream + term[...].astype(jnp.float32)
    rows, width = stream.shape
    half_ref[...] = stream.astype(half_ref.dtype)
    mean = jnp.sum(stream, axis=1, keepdims=True) / width
    square = jnp.sum((stream - mean) ** 2, axis=1, keepdims=True)
    lane = lax.broadcasted_iota(jnp.int32, (rows, LANES), 1)
    table = jnp.where(lane == 0, mean, jnp.where(lane == 1, square, 0.0))
    if rows < LANES:
        table = jnp.concatenate(
            [table, jnp.zeros((LANES - rows, LANES), jnp.float32)], axis=0
        )
    stats = jnp.transpose(table)[:8]
    for d in range(stats_ref.shape[0]):
        stats_ref[d] = stats


def own_stream(residual, terms, n):
    rows, local = residual.shape
    return pl.pallas_call(
        functools.partial(stream_kernel, len(terms)),
        out_shape=(
            jax.ShapeDtypeStruct((rows, local), jnp.bfloat16),
            jax.ShapeDtypeStruct((n, 8, LANES), jnp.float32),
        ),
        compiler_params=pltpu.CompilerParams(vmem_limit_bytes=VMEM_BYTES),
        cost_estimate=pl.CostEstimate(
            flops=20 * rows * local, bytes_accessed=16 * rows * local, transcendentals=0
        ),
        name="own_stream",
    )(residual, *terms)


def moments_kernel(local, stats_ref, out_ref):
    n = stats_ref.shape[0]
    rows = out_ref.shape[0]
    centre = jnp.zeros((1, LANES), jnp.float32)
    for d in range(n):
        centre = centre + stats_ref[d, 0:1]
    centre = centre / n
    spread = jnp.zeros((1, LANES), jnp.float32)
    for d in range(n):
        away = stats_ref[d, 0:1] - centre
        spread = spread + stats_ref[d, 1:2] + local * (away * away)
    inverse = lax.rsqrt(spread / (n * local) + 1e-05)
    row = lax.broadcasted_iota(jnp.int32, (LANES, LANES), 0)
    table = jnp.where(row == 0, centre, jnp.where(row == 1, inverse, 0.0))
    out_ref[...] = jnp.transpose(table)[:rows]


def moments(stats, rows, local):
    return pl.pallas_call(
        functools.partial(moments_kernel, local),
        out_shape=jax.ShapeDtypeStruct((rows, LANES), jnp.float32),
        name="moments",
    )(stats)


def rows_kernel(source, piece_ref, moments_ref, scaling_ref, *refs):
    out_ref, done_ref, semaphore = refs[-3:]
    rows, width = piece_ref.shape
    blocks = width // BLOCK_LEN
    table = signs(BLOCK_LEN)
    unit = 1.0 / math.sqrt(BLOCK_LEN)
    owner = source[0]
    scaling = scaling_ref[owner].astype(jnp.float32)
    gain, bias = scaling[0:1], scaling[1:2]
    centre = moments_ref[:, 0:1]
    inverse = moments_ref[:, 1:2]
    normal = (piece_ref[...].astype(jnp.float32) - centre) * inverse * gain + bias
    normal = jnp.concatenate(
        [normal[:, b * BLOCK_LEN : (b + 1) * BLOCK_LEN] for b in range(blocks)], axis=0
    )
    coded = jnp.zeros(normal.shape, jnp.float32)
    rest = normal
    for _ in range(3):
        part = rest.astype(jnp.bfloat16)
        coded = coded + jnp.dot(part, table, preferred_element_type=jnp.float32)
        rest = rest - part.astype(jnp.float32)
    coded = coded * unit
    largest = jnp.max(jnp.abs(coded), axis=1, keepdims=True)
    scales = (largest / 448.0 + 1e-06).astype(jnp.bfloat16).astype(jnp.float32)
    quanta = (coded / scales).astype(jnp.bfloat16)
    back = jnp.dot(quanta, table, preferred_element_type=jnp.float32) * (scales * unit)
    back = back.astype(out_ref.dtype)
    for b in range(blocks):
        done_ref[:, b * BLOCK_LEN : (b + 1) * BLOCK_LEN] = back[b * rows : (b + 1) * rows]
    columns = pl.ds(pl.multiple_of(owner * width, LANES), width)
    copy = pltpu.make_async_copy(done_ref, out_ref.at[:, columns], semaphore)
    copy.start()
    copy.wait()


def finish(whole, source, piece, columns, scaling):
    rows, local = piece.shape
    n = scaling.shape[0]
    earlier = [] if whole is None else [whole]
    vmem = pl.BlockSpec(memory_space=pltpu.VMEM)
    return pl.pallas_call(
        rows_kernel,
        out_shape=jax.ShapeDtypeStruct((rows, n * local), jnp.bfloat16),
        grid_spec=pltpu.PrefetchScalarGridSpec(
            num_scalar_prefetch=1,
            grid=(1,),
            in_specs=[
                pl.BlockSpec((rows, local), lambda i, source: (0, 0)),
                pl.BlockSpec((rows, LANES), lambda i, source: (0, 0)),
                pl.BlockSpec((n, 2, local), lambda i, source: (0, 0, 0)),
            ]
            + [pl.BlockSpec(memory_space=pl.ANY)] * len(earlier),
            out_specs=pl.BlockSpec(memory_space=pl.ANY),
            scratch_shapes=[
                pltpu.VMEM((rows, local), jnp.bfloat16),
                pltpu.SemaphoreType.DMA,
            ],
        ),
        input_output_aliases={4: 0} if earlier else {},
        compiler_params=pltpu.CompilerParams(vmem_limit_bytes=VMEM_BYTES),
        cost_estimate=pl.CostEstimate(
            flops=8 * BLOCK_LEN * rows * local,
            bytes_accessed=4 * rows * local,
            transcendentals=0,
        ),
        name="finish",
    )(source.reshape(1), piece, columns, scaling, *earlier)


def body(attended, out_weight, residual, norm_gain, norm_bias):
    n = lax.axis_size("tensor")
    nz, nx = factors(n)
    rows = attended.shape[0]
    local = out_weight.shape[1] // n
    me = lax.axis_index("tensor")
    outer, inner = me // nx, me % nx
    every = [(z, x) for z in range(nz) for x in range(nx)]
    swap = [[(z * nx + x, z * nx + (x ^ j)) for z, x in every] for j in range(nx)]
    jump = [[(z * nx + x, (z ^ k) * nx + x) for z, x in every] for k in range(nz)]
    order = list(range(nz - 1, -1, -1))

    arrived = []
    kept = None
    for k in order:
        sent = []
        for j in range(1, nx):
            target = (outer ^ k) * nx + (inner ^ j)
            sent.append(
                lax.ppermute(
                    product(attended, out_weight, target, local, jnp.bfloat16),
                    "tensor",
                    swap[j],
                )
            )
        kept = product(attended, out_weight, (outer ^ k) * nx + inner, local, jnp.float32)
        if k:
            for piece in sent:
                kept = kept + piece.astype(jnp.float32)
            last = kept.astype(jnp.bfloat16)
            arrived.append(lax.ppermute(last, "tensor", jump[k]))
        else:
            arrived += [kept] + sent

    scaling = jnp.stack([norm_gain, norm_bias])
    scaling, _ = lax.optimization_barrier((scaling, last))
    scaling = lax.all_to_all(
        jnp.broadcast_to(scaling[None], (n,) + scaling.shape), "tensor", 0, 0, tiled=True
    )

    stream_out, stats = own_stream(residual, arrived, n)
    near = [(k, lax.ppermute(stream_out, "tensor", jump[k])) for k in order[:-1]]
    pieces = [(0, stream_out)] + near[::-1]
    stats = lax.all_to_all(stats, "tensor", 0, 0, tiled=True)
    columns = moments(stats, rows, local)

    whole = None
    for k, piece in pieces:
        whole = finish(whole, (outer ^ k) * nx + inner, piece, columns, scaling)
        for j in range(1, nx):
            other = lax.ppermute(piece, "tensor", swap[j])
            whole = finish(whole, (outer ^ k) * nx + (inner ^ j), other, columns, scaling)
    return (stream_out, whole)


def solution(mesh):
    placed = (
        P(("groups", "dp"), "tensor"),
        P("tensor", None),
        P(("groups", "dp"), "tensor"),
        P("tensor"),
        P("tensor"),
    )
    return jax.shard_map(
        body,
        mesh=mesh,
        in_specs=placed,
        out_specs=(P(("groups", "dp"), "tensor"), P(("groups", "dp"), None)),
        check_vma=False,
    )
```

```python
import functools
import math

import jax
import jax.numpy as jnp
from jax import lax
from jax.experimental import pallas as pl
from jax.experimental.pallas import tpu as pltpu
from jax.sharding import PartitionSpec as P

BLOCK_LEN = 128
LANES = 128
VMEM_BYTES = 40 * 1024 * 1024


def factors(n):
    inner = 1 << ((n.bit_length() - 1) // 2)
    return n // inner, inner


def tile_width(width, most):
    while width % most:
        most //= 2
    return most


def signs(length):
    rows = lax.broadcasted_iota(jnp.int32, (length, length), 0)
    columns = lax.broadcasted_iota(jnp.int32, (length, length), 1)
    common = jnp.bitwise_and(rows, columns)
    parity = jnp.zeros((length, length), jnp.int32)
    for bit_index in range(length.bit_length() - 1):
        parity = parity + jnp.bitwise_and(jnp.right_shift(common, bit_index), 1)
    return (1 - 2 * jnp.bitwise_and(parity, 1)).astype(jnp.bfloat16)


def product_kernel(targets, splits, local, tile, rows_ref, weight_ref, *refs):
    count = len(targets)
    scratch, semaphores = refs[-2:]
    outs = refs[-2 - count : -2]
    nx, per = splits[1], local // tile
    me = lax.axis_index("tensor")
    outer, inner = me // nx, lax.rem(me, nx)
    copies = []
    for t, (k, j) in enumerate(targets):
        owner = jnp.bitwise_xor(outer, k) * nx + jnp.bitwise_xor(inner, j)
        for i in range(per):
            start = pl.multiple_of(owner * local + i * tile, LANES)
            copy = pltpu.make_async_copy(
                weight_ref.at[:, pl.ds(start, tile)],
                scratch.at[t * per + i],
                semaphores.at[t * per + i],
            )
            copy.start()
            copies.append(copy)
    for t in range(count):
        for i in range(per):
            copies[t * per + i].wait()
            outs[t][:, i * tile : (i + 1) * tile] = jnp.dot(
                rows_ref[...], scratch[t * per + i], preferred_element_type=jnp.float32
            ).astype(outs[t].dtype)


def products(attended, weight, targets, splits, local, after):
    rows, depth = attended.shape
    tile = tile_width(local, 512)
    slots = len(targets) * (local // tile)
    vmem = pl.BlockSpec(memory_space=pltpu.VMEM)
    return pl.pallas_call(
        functools.partial(product_kernel, targets, splits, local, tile),
        out_shape=[
            jax.ShapeDtypeStruct((rows, local), jnp.bfloat16 if j else jnp.float32)
            for _, j in targets
        ],
        in_specs=[vmem] + [pl.BlockSpec(memory_space=pl.ANY)] * (1 + len(after)),
        out_specs=[vmem] * len(targets),
        scratch_shapes=[
            pltpu.VMEM((slots, depth, tile), jnp.bfloat16),
            pltpu.SemaphoreType.DMA((slots,)),
        ],
        compiler_params=pltpu.CompilerParams(vmem_limit_bytes=VMEM_BYTES),
        cost_estimate=pl.CostEstimate(
            flops=2 * rows * depth * local * len(targets),
            bytes_accessed=2 * depth * local * len(targets),
            transcendentals=0,
        ),
        name="products",
    )(attended, weight, *after)


def in_three(values):
    parts = []
    for _ in range(3):
        part = values.astype(jnp.bfloat16)
        parts.append(part.astype(jnp.float32))
        values = values - parts[-1]
    return parts


def stream_kernel(count, residual_ref, gain_ref, bias_ref, *refs):
    terms, (half_ref, shared_ref) = refs[:count], refs[count:]
    stream = residual_ref[...].astype(jnp.float32)
    for term in terms:
        stream = stream + term[...].astype(jnp.float32)
    rows, width = stream.shape
    half_ref[...] = stream.astype(half_ref.dtype)
    mean = jnp.sum(stream, axis=1, keepdims=True) / width
    square = jnp.sum((stream - mean) ** 2, axis=1, keepdims=True)
    lane = lax.broadcasted_iota(jnp.int32, (rows, LANES), 1)
    table = jnp.zeros((rows, LANES), jnp.float32)
    for place, part in enumerate(in_three(mean) + in_three(square)):
        table = jnp.where(lane == place, part, table)
    if rows < LANES:
        table = jnp.concatenate(
            [table, jnp.zeros((LANES - rows, LANES), jnp.float32)], axis=0
        )
    stats = jnp.transpose(table)
    fill = shared_ref.shape[1] - 2 * gain_ref.shape[0]
    shared = jnp.concatenate(
        [stats[:fill], gain_ref[...].astype(jnp.float32), bias_ref[...].astype(jnp.float32)],
        axis=0,
    ).astype(jnp.bfloat16)
    for d in range(shared_ref.shape[0]):
        shared_ref[d] = shared


def own_stream(residual, gain, bias, terms, n):
    rows, local = residual.shape
    blocks = local // LANES
    height = (8 + 2 * blocks + 15) // 16 * 16
    return pl.pallas_call(
        functools.partial(stream_kernel, len(terms)),
        out_shape=(
            jax.ShapeDtypeStruct((rows, local), jnp.bfloat16),
            jax.ShapeDtypeStruct((n, height, LANES), jnp.bfloat16),
        ),
        compiler_params=pltpu.CompilerParams(vmem_limit_bytes=VMEM_BYTES),
        cost_estimate=pl.CostEstimate(
            flops=20 * rows * local, bytes_accessed=16 * rows * local, transcendentals=0
        ),
        name="own_stream",
    )(residual, gain.reshape(blocks, LANES), bias.reshape(blocks, LANES), *terms)


def moments_kernel(local, shared_ref, out_ref):
    n = shared_ref.shape[0]
    rows = out_ref.shape[0]
    means, spread = [], jnp.zeros((1, LANES), jnp.float32)
    for d in range(n):
        stats = shared_ref[d, 0:8].astype(jnp.float32)
        means.append(stats[0:1] + stats[1:2] + stats[2:3])
        spread = spread + (stats[3:4] + stats[4:5] + stats[5:6])
    centre = sum(means) / n
    for mean in means:
        spread = spread + local * ((mean - centre) * (mean - centre))
    inverse = lax.rsqrt(spread / (n * local) + 1e-05)
    row = lax.broadcasted_iota(jnp.int32, (LANES, LANES), 0)
    table = jnp.where(row == 0, centre, jnp.where(row == 1, inverse, 0.0))
    out_ref[...] = jnp.transpose(table)[:rows]


def moments(shared, rows, local):
    return pl.pallas_call(
        functools.partial(moments_kernel, local),
        out_shape=jax.ShapeDtypeStruct((rows, LANES), jnp.float32),
        name="moments",
    )(shared)


def rows_kernel(place, splits, piece_ref, moments_ref, shared_ref, *refs):
    out_ref, done_ref, semaphore = refs[-3:]
    rows, width = piece_ref.shape
    blocks = width // BLOCK_LEN
    table = signs(BLOCK_LEN)
    unit = 1.0 / math.sqrt(BLOCK_LEN)
    me = lax.axis_index("tensor")
    outer, inner = me // splits[1], lax.rem(me, splits[1])
    owner = jnp.bitwise_xor(outer, place[0]) * splits[1] + jnp.bitwise_xor(inner, place[1])
    shared = shared_ref[owner].astype(jnp.float32)
    scaling = shared[shared.shape[0] - 2 * blocks :]
    centre = moments_ref[:, 0:1]
    inverse = moments_ref[:, 1:2]
    normal = []
    for b in range(blocks):
        block = piece_ref[:, b * BLOCK_LEN : (b + 1) * BLOCK_LEN].astype(jnp.float32)
        block = (block - centre) * inverse
        normal.append(block * scaling[b : b + 1] + scaling[blocks + b : blocks + b + 1])
    normal = jnp.concatenate(normal, axis=0)
    first = normal.astype(jnp.bfloat16)
    second = (normal - first.astype(jnp.float32)).astype(jnp.bfloat16)
    coded = jnp.dot(first, table, preferred_element_type=jnp.float32)
    coded = coded + jnp.dot(second, table, preferred_element_type=jnp.float32)
    coded = coded * unit
    largest = jnp.max(jnp.abs(coded), axis=1, keepdims=True)
    scales = (largest / 448.0 + 1e-06).astype(jnp.bfloat16).astype(jnp.float32)
    quanta = (coded * (1.0 / scales)).astype(jnp.bfloat16)
    back = jnp.dot(quanta, table, preferred_element_type=jnp.float32) * (scales * unit)
    back = back.astype(out_ref.dtype)
    for b in range(blocks):
        done_ref[:, b * BLOCK_LEN : (b + 1) * BLOCK_LEN] = back[b * rows : (b + 1) * rows]
    columns = pl.ds(pl.multiple_of(owner * width, LANES), width)
    copy = pltpu.make_async_copy(done_ref, out_ref.at[:, columns], semaphore)
    copy.start()
    copy.wait()


def finish(whole, place, splits, piece, columns, shared):
    rows, local = piece.shape
    n = shared.shape[0]
    earlier = [] if whole is None else [whole]
    vmem = pl.BlockSpec(memory_space=pltpu.VMEM)
    return pl.pallas_call(
        functools.partial(rows_kernel, place, splits),
        out_shape=jax.ShapeDtypeStruct((rows, n * local), jnp.bfloat16),
        in_specs=[vmem] * 3 + [pl.BlockSpec(memory_space=pl.ANY)] * len(earlier),
        out_specs=pl.BlockSpec(memory_space=pl.ANY),
        scratch_shapes=[
            pltpu.VMEM((rows, local), jnp.bfloat16),
            pltpu.SemaphoreType.DMA,
        ],
        input_output_aliases={3: 0} if earlier else {},
        compiler_params=pltpu.CompilerParams(vmem_limit_bytes=VMEM_BYTES),
        cost_estimate=pl.CostEstimate(
            flops=8 * BLOCK_LEN * rows * local,
            bytes_accessed=4 * rows * local,
            transcendentals=0,
        ),
        name="finish",
    )(piece, columns, shared, *earlier)


def body(attended, out_weight, residual, norm_gain, norm_bias):
    n = lax.axis_size("tensor")
    nz, nx = splits = factors(n)
    rows = attended.shape[0]
    local = out_weight.shape[1] // n
    every = [(z, x) for z in range(nz) for x in range(nx)]
    swap = [[(z * nx + x, z * nx + (x ^ j)) for z, x in every] for j in range(nx)]
    jump = [[(z * nx + x, (z ^ k) * nx + x) for z, x in every] for k in range(nz)]
    order = list(range(nz - 1, -1, -1))

    arrived, after = [], []
    sent, before = None, None
    for k in order + [None]:
        targets = [] if k is None else [(k, j) for j in range(1, nx)]
        targets += [] if before is None else [(before, 0)]
        terms = products(attended, out_weight, targets, splits, local, after)
        after = [terms[-1]]
        leaving = [] if k is None else [lax.ppermute(t, "tensor", swap[j + 1]) for j, t in enumerate(terms[: nx - 1])]
        if before:
            kept = terms[-1]
            for piece in sent:
                kept = kept + piece.astype(jnp.float32)
            kept = kept.astype(jnp.bfloat16)
            after = [kept]
            arrived.append(lax.ppermute(kept, "tensor", jump[before]))
        elif before == 0:
            arrived += [terms[-1]] + sent
        sent, before = leaving, k

    stream_out, shared = own_stream(residual, norm_gain, norm_bias, arrived, n)
    near = {k: lax.ppermute(stream_out, "tensor", jump[k]) for k in order[:-1]}
    near[0] = stream_out
    shared = lax.all_to_all(shared, "tensor", 0, 0, tiled=True)
    columns = moments(shared, rows, local)

    whole = None
    for k in [0, 1] + order[:-2]:
        whole = finish(whole, (k, 0), splits, near[k], columns, shared)
        for j in range(1, nx):
            other = lax.ppermute(near[k], "tensor", swap[j])
            whole = finish(whole, (k, j), splits, other, columns, shared)
    return (stream_out, whole)


def solution(mesh):
    placed = (
        P(("groups", "dp"), "tensor"),
        P("tensor", None),
        P(("groups", "dp"), "tensor"),
        P("tensor"),
        P("tensor"),
    )
    return jax.shard_map(
        body,
        mesh=mesh,
        in_specs=placed,
        out_specs=(P(("groups", "dp"), "tensor"), P(("groups", "dp"), None)),
        check_vma=False,
    )
```

```python
import functools
import math

import jax
import jax.numpy as jnp
from jax import lax
from jax.experimental import pallas as pl
from jax.experimental.pallas import tpu as pltpu
from jax.sharding import PartitionSpec as P

BLOCK_LEN = 128
LANES = 128
VMEM_BYTES = 40 * 1024 * 1024


def factors(n):
    inner = 1 << ((n.bit_length() - 1) // 2)
    return n // inner, inner


def tile_width(width, most):
    while width % most:
        most //= 2
    return most


def signs(length):
    rows = lax.broadcasted_iota(jnp.int32, (length, length), 0)
    columns = lax.broadcasted_iota(jnp.int32, (length, length), 1)
    common = jnp.bitwise_and(rows, columns)
    parity = jnp.zeros((length, length), jnp.int32)
    for bit_index in range(length.bit_length() - 1):
        parity = parity + jnp.bitwise_and(jnp.right_shift(common, bit_index), 1)
    return (1 - 2 * jnp.bitwise_and(parity, 1)).astype(jnp.bfloat16)


def product_kernel(targets, splits, local, tile, rows_ref, weight_ref, *refs):
    count = len(targets)
    held, scratch, semaphores = refs[-3:]
    outs = refs[-3 - count : -3]
    nx, per = splits[1], local // tile
    me = lax.axis_index("tensor")
    outer, inner = me // nx, lax.rem(me, nx)
    first = pltpu.make_async_copy(rows_ref, held, semaphores.at[count * per])
    first.start()
    copies = []
    for t, (k, j) in enumerate(targets):
        owner = jnp.bitwise_xor(outer, k) * nx + jnp.bitwise_xor(inner, j)
        for i in range(per):
            start = pl.multiple_of(owner * local + i * tile, LANES)
            copy = pltpu.make_async_copy(
                weight_ref.at[:, pl.ds(start, tile)],
                scratch.at[t * per + i],
                semaphores.at[t * per + i],
            )
            copy.start()
            copies.append(copy)
    first.wait()
    for t in range(count):
        for i in range(per):
            copies[t * per + i].wait()
            outs[t][:, i * tile : (i + 1) * tile] = jnp.dot(
                held[...], scratch[t * per + i], preferred_element_type=jnp.float32
            ).astype(outs[t].dtype)


def products(attended, weight, targets, splits, local, after):
    rows, depth = attended.shape
    tile = tile_width(local, 512)
    slots = len(targets) * (local // tile)
    vmem = pl.BlockSpec(memory_space=pltpu.VMEM)
    return pl.pallas_call(
        functools.partial(product_kernel, targets, splits, local, tile),
        out_shape=[
            jax.ShapeDtypeStruct((rows, local), jnp.bfloat16 if j else jnp.float32)
            for _, j in targets
        ],
        in_specs=[pl.BlockSpec(memory_space=pltpu.HBM)] * 2
        + [pl.BlockSpec(memory_space=pl.ANY)] * len(after),
        out_specs=[vmem] * len(targets),
        scratch_shapes=[
            pltpu.VMEM((rows, depth), jnp.bfloat16),
            pltpu.VMEM((slots, depth, tile), jnp.bfloat16),
            pltpu.SemaphoreType.DMA((slots + 1,)),
        ],
        compiler_params=pltpu.CompilerParams(vmem_limit_bytes=VMEM_BYTES),
        cost_estimate=pl.CostEstimate(
            flops=2 * rows * depth * local * len(targets),
            bytes_accessed=2 * depth * local * len(targets),
            transcendentals=0,
        ),
        name="products",
    )(attended, weight, *after)


def in_three(values):
    parts = []
    for _ in range(3):
        part = values.astype(jnp.bfloat16)
        parts.append(part.astype(jnp.float32))
        values = values - parts[-1]
    return parts


def stream_kernel(count, residual_ref, gain_ref, bias_ref, *refs):
    terms, (half_ref, shared_ref) = refs[:count], refs[count:]
    stream = residual_ref[...].astype(jnp.float32)
    for term in terms:
        stream = stream + term[...].astype(jnp.float32)
    rows, width = stream.shape
    half_ref[...] = stream.astype(half_ref.dtype)
    mean = jnp.sum(stream, axis=1, keepdims=True) / width
    square = jnp.sum((stream - mean) ** 2, axis=1, keepdims=True)
    lane = lax.broadcasted_iota(jnp.int32, (rows, LANES), 1)
    table = jnp.zeros((rows, LANES), jnp.float32)
    for place, part in enumerate(in_three(mean) + in_three(square)):
        table = jnp.where(lane == place, part, table)
    if rows < LANES:
        table = jnp.concatenate(
            [table, jnp.zeros((LANES - rows, LANES), jnp.float32)], axis=0
        )
    stats = jnp.transpose(table)
    fill = shared_ref.shape[1] - 2 * gain_ref.shape[0]
    shared = jnp.concatenate(
        [stats[:fill], gain_ref[...].astype(jnp.float32), bias_ref[...].astype(jnp.float32)],
        axis=0,
    ).astype(jnp.bfloat16)
    for d in range(shared_ref.shape[0]):
        shared_ref[d] = shared


def own_stream(residual, gain, bias, terms, n):
    rows, local = residual.shape
    blocks = local // LANES
    height = (8 + 2 * blocks + 15) // 16 * 16
    return pl.pallas_call(
        functools.partial(stream_kernel, len(terms)),
        out_shape=(
            jax.ShapeDtypeStruct((rows, local), jnp.bfloat16),
            jax.ShapeDtypeStruct((n, height, LANES), jnp.bfloat16),
        ),
        compiler_params=pltpu.CompilerParams(vmem_limit_bytes=VMEM_BYTES),
        cost_estimate=pl.CostEstimate(
            flops=20 * rows * local, bytes_accessed=16 * rows * local, transcendentals=0
        ),
        name="own_stream",
    )(residual, gain.reshape(blocks, LANES), bias.reshape(blocks, LANES), *terms)


def moments_kernel(local, passed, shared_ref, *refs):
    out_ref = refs[passed]
    n = shared_ref.shape[0]
    rows = out_ref.shape[0]
    means, spread = [], jnp.zeros((1, LANES), jnp.float32)
    for d in range(n):
        stats = shared_ref[d, 0:8].astype(jnp.float32)
        means.append(stats[0:1] + stats[1:2] + stats[2:3])
        spread = spread + (stats[3:4] + stats[4:5] + stats[5:6])
    centre = sum(means) / n
    for mean in means:
        spread = spread + local * ((mean - centre) * (mean - centre))
    inverse = lax.rsqrt(spread / (n * local) + 1e-05)
    row = lax.broadcasted_iota(jnp.int32, (LANES, LANES), 0)
    table = jnp.where(row == 0, centre, jnp.where(row == 1, inverse, 0.0))
    out_ref[...] = jnp.transpose(table)[:rows]


def moments(shared, passed, rows, local):
    vmem = pl.BlockSpec(memory_space=pltpu.VMEM)
    anywhere = [pl.BlockSpec(memory_space=pl.ANY)] * len(passed)
    columns, *passed = pl.pallas_call(
        functools.partial(moments_kernel, local, len(passed)),
        out_shape=[jax.ShapeDtypeStruct((rows, LANES), jnp.float32)]
        + [jax.ShapeDtypeStruct(p.shape, p.dtype) for p in passed],
        in_specs=[vmem] + anywhere,
        out_specs=[vmem] + anywhere,
        input_output_aliases={1 + i: 1 + i for i in range(len(passed))},
        name="moments",
    )(shared, *passed)
    return columns, passed


def coded_rows(piece_ref, moments_ref, scaling, table):
    blocks = piece_ref.shape[1] // BLOCK_LEN
    unit = 1.0 / math.sqrt(BLOCK_LEN)
    centre = moments_ref[:, 0:1]
    inverse = moments_ref[:, 1:2]
    normal = []
    for b in range(blocks):
        block = piece_ref[:, b * BLOCK_LEN : (b + 1) * BLOCK_LEN].astype(jnp.float32)
        block = (block - centre) * inverse
        normal.append(block * scaling[b : b + 1] + scaling[blocks + b : blocks + b + 1])
    normal = jnp.concatenate(normal, axis=0)
    first = normal.astype(jnp.bfloat16)
    second = (normal - first.astype(jnp.float32)).astype(jnp.bfloat16)
    coded = jnp.dot(first, table, preferred_element_type=jnp.float32)
    coded = coded + jnp.dot(second, table, preferred_element_type=jnp.float32)
    coded = coded * unit
    largest = jnp.max(jnp.abs(coded), axis=1, keepdims=True)
    scales = (largest / 448.0 + 1e-06).astype(jnp.bfloat16).astype(jnp.float32)
    quanta = (coded * (1.0 / scales)).astype(jnp.bfloat16)
    back = jnp.dot(quanta, table, preferred_element_type=jnp.float32) * (scales * unit)
    return back.astype(jnp.bfloat16)


def finish_kernel(places, splits, moments_ref, shared_ref, *refs):
    count = len(places)
    pieces = refs[:count]
    out_ref, done_ref, semaphores = refs[-3:]
    rows, width = pieces[0].shape
    blocks = width // BLOCK_LEN
    table = signs(BLOCK_LEN)
    me = lax.axis_index("tensor")
    outer, inner = me // splits[1], lax.rem(me, splits[1])
    copies = []
    for p, (k, j) in enumerate(places):
        owner = jnp.bitwise_xor(outer, k) * splits[1] + jnp.bitwise_xor(inner, j)
        shared = shared_ref[owner].astype(jnp.float32)
        back = coded_rows(
            pieces[p], moments_ref, shared[shared.shape[0] - 2 * blocks :], table
        )
        for b in range(blocks):
            done_ref[p, :, b * BLOCK_LEN : (b + 1) * BLOCK_LEN] = back[
                b * rows : (b + 1) * rows
            ]
        columns = pl.ds(pl.multiple_of(owner * width, LANES), width)
        copy = pltpu.make_async_copy(
            done_ref.at[p], out_ref.at[:, columns], semaphores.at[p]
        )
        copy.start()
        copies.append(copy)
    for copy in copies:
        copy.wait()


def finish(whole, places, splits, pieces, columns, shared):
    rows, local = pieces[0].shape
    count = len(pieces)
    n = shared.shape[0]
    earlier = [] if whole is None else [whole]
    vmem = pl.BlockSpec(memory_space=pltpu.VMEM)
    return pl.pallas_call(
        functools.partial(finish_kernel, places, splits),
        out_shape=jax.ShapeDtypeStruct((rows, n * local), jnp.bfloat16),
        in_specs=[vmem] * (2 + count)
        + [pl.BlockSpec(memory_space=pl.ANY)] * len(earlier),
        out_specs=pl.BlockSpec(memory_space=pl.ANY),
        scratch_shapes=[
            pltpu.VMEM((count, rows, local), jnp.bfloat16),
            pltpu.SemaphoreType.DMA((count,)),
        ],
        input_output_aliases={2 + count: 0} if earlier else {},
        compiler_params=pltpu.CompilerParams(vmem_limit_bytes=VMEM_BYTES),
        cost_estimate=pl.CostEstimate(
            flops=8 * BLOCK_LEN * rows * local * count,
            bytes_accessed=4 * rows * local * count,
            transcendentals=0,
        ),
        name="finish",
    )(columns, shared, *pieces, *earlier)


def body(attended, out_weight, residual, norm_gain, norm_bias):
    n = lax.axis_size("tensor")
    nz, nx = splits = factors(n)
    rows = attended.shape[0]
    local = out_weight.shape[1] // n
    every = [(z, x) for z in range(nz) for x in range(nx)]
    swap = [[(z * nx + x, z * nx + (x ^ j)) for z, x in every] for j in range(nx)]
    jump = [[(z * nx + x, (z ^ k) * nx + x) for z, x in every] for k in range(nz)]

    away = [[(k, j) for j in range(1, nx)] for k in range(nz)]
    here = [[(k, 0)] for k in range(nz)]
    order = list(range(nz - 1, -1, -1))
    calls = [away[order[0]], away[order[1]] + away[order[2]] + here[order[0]]]
    for i in range(2, nz - 1):
        calls.append(away[order[i + 1]] + here[order[i - 1]])
    calls[-1] = calls[-1] + here[1]
    calls.append(here[0])
    joins = [[]] + [[k] for k in order[:-1]] + [[]]
    joins[-3:] = [joins[-3] + joins[-2], []]
    terms = {k: [] for k in range(nz)}
    after = []
    for targets, joined in zip(calls, joins):
        results = products(attended, out_weight, targets, splits, local, after)
        after = [results[-1]]
        for (k, j), result in zip(targets, results):
            terms[k].append(lax.ppermute(result, "tensor", swap[j]) if j else result)
        for k in joined:
            bit = k & -k
            total = terms[k][0].astype(jnp.float32)
            for term in terms[k][1:]:
                total = total + term.astype(jnp.float32)
            total = total.astype(jnp.bfloat16)
            after = [total]
            terms[k ^ bit].append(lax.ppermute(total, "tensor", jump[bit]))

    stream_out, shared = own_stream(residual, norm_gain, norm_bias, terms[0], n)
    shared = lax.all_to_all(shared, "tensor", 0, 0, tiled=True)
    have = {0: stream_out}
    top = nz // 2
    have[top] = lax.ppermute(stream_out, "tensor", jump[top])
    have[1] = lax.ppermute(stream_out, "tensor", jump[1])
    early = away[0] + away[1]
    crossed = {(k, j): lax.ppermute(have[k], "tensor", swap[j]) for k, j in early}
    columns, passed = moments(
        shared, [have[top]] + [crossed[p] for p in early], rows, local
    )
    have[top] = passed[0]
    crossed.update(zip(early, passed[1:]))
    for k in sorted(range(2, nz), key=lambda k: (-(k & -k), k)):
        if k != top:
            have[k] = lax.ppermute(have[k ^ (k & -k)], "tensor", jump[k & -k])

    whole = None
    for k in range(nz):
        places = here[k] + away[k]
        pieces = [have[k]] + [
            crossed.get(p) if p in crossed else lax.ppermute(have[k], "tensor", swap[p[1]])
            for p in away[k]
        ]
        if k < nz - 1:
            whole = finish(whole, places, splits, pieces, columns, shared)
        else:
            for place, piece in zip(places, pieces):
                whole = finish(whole, [place], splits, [piece], columns, shared)
    return (stream_out, whole)


def solution(mesh):
    placed = (
        P(("groups", "dp"), "tensor"),
        P("tensor", None),
        P(("groups", "dp"), "tensor"),
        P("tensor"),
        P("tensor"),
    )
    return jax.shard_map(
        body,
        mesh=mesh,
        in_specs=placed,
        out_specs=(P(("groups", "dp"), "tensor"), P(("groups", "dp"), None)),
        check_vma=False,
    )
```

```python
import functools
import math

import jax
import jax.numpy as jnp
from jax import lax
from jax.experimental import pallas as pl
from jax.experimental.pallas import tpu as pltpu
from jax.sharding import PartitionSpec as P

BLOCK_LEN = 128
LANES = 128
MIB = 1024 * 1024


def factors(n):
    inner = 1 << ((n.bit_length() - 1) // 2)
    return n // inner, inner


def tile_width(width, most):
    while width % most:
        most //= 2
    return most


def signs(length):
    rows = lax.broadcasted_iota(jnp.int32, (length, length), 0)
    columns = lax.broadcasted_iota(jnp.int32, (length, length), 1)
    common = jnp.bitwise_and(rows, columns)
    parity = jnp.zeros((length, length), jnp.int32)
    for bit_index in range(length.bit_length() - 1):
        parity = parity + jnp.bitwise_and(jnp.right_shift(common, bit_index), 1)
    return (1 - 2 * jnp.bitwise_and(parity, 1)).astype(jnp.bfloat16)


def product_kernel(targets, splits, local, tile, rows_ref, weight_ref, *refs):
    count = len(targets)
    held, scratch, semaphores = refs[-3:]
    outs = refs[-3 - count : -3]
    nx, per = splits[1], local // tile
    me = lax.axis_index("tensor")
    outer, inner = me // nx, lax.rem(me, nx)
    first = pltpu.make_async_copy(rows_ref, held, semaphores.at[count * per])
    first.start()
    copies = []
    for t, (k, j) in enumerate(targets):
        owner = jnp.bitwise_xor(outer, k) * nx + jnp.bitwise_xor(inner, j)
        for i in range(per):
            start = pl.multiple_of(owner * local + i * tile, LANES)
            copy = pltpu.make_async_copy(
                weight_ref.at[:, pl.ds(start, tile)],
                scratch.at[t * per + i],
                semaphores.at[t * per + i],
            )
            copy.start()
            copies.append(copy)
    first.wait()
    for t in range(count):
        for i in range(per):
            copies[t * per + i].wait()
            outs[t][:, i * tile : (i + 1) * tile] = jnp.dot(
                held[...], scratch[t * per + i], preferred_element_type=jnp.float32
            ).astype(outs[t].dtype)


def products(attended, weight, targets, splits, local, after):
    rows, depth = attended.shape
    tile = tile_width(local, 512)
    slots = len(targets) * (local // tile)
    vmem = pl.BlockSpec(memory_space=pltpu.VMEM)
    return pl.pallas_call(
        functools.partial(product_kernel, targets, splits, local, tile),
        out_shape=[
            jax.ShapeDtypeStruct((rows, local), jnp.bfloat16 if j else jnp.float32)
            for _, j in targets
        ],
        in_specs=[pl.BlockSpec(memory_space=pltpu.HBM)] * 2
        + [pl.BlockSpec(memory_space=pl.ANY)] * len(after),
        out_specs=[vmem] * len(targets),
        scratch_shapes=[
            pltpu.VMEM((rows, depth), jnp.bfloat16),
            pltpu.VMEM((slots, depth, tile), jnp.bfloat16),
            pltpu.SemaphoreType.DMA((slots + 1,)),
        ],
        compiler_params=pltpu.CompilerParams(
            vmem_limit_bytes=40 * MIB
        ),
        cost_estimate=pl.CostEstimate(
            flops=2 * rows * depth * local * len(targets),
            bytes_accessed=2 * depth * local * len(targets),
            transcendentals=0,
        ),
        name="products",
    )(attended, weight, *after)


def in_three(values):
    parts = []
    for _ in range(3):
        part = values.astype(jnp.bfloat16)
        parts.append(part.astype(jnp.float32))
        values = values - parts[-1]
    return parts


def stream_kernel(count, residual_ref, gain_ref, bias_ref, *refs):
    terms, (half_ref, sent_ref) = refs[:count], refs[count:]
    stream = residual_ref[...].astype(jnp.float32)
    for term in terms:
        stream = stream + term[...].astype(jnp.float32)
    rows, width = stream.shape
    half = stream.astype(half_ref.dtype)
    half_ref[...] = half
    sent_ref[:, :width] = half
    mean = jnp.sum(stream, axis=1, keepdims=True) / width
    square = jnp.sum((stream - mean) ** 2, axis=1, keepdims=True)
    lane = lax.broadcasted_iota(jnp.int32, (rows, LANES), 1)
    table = jnp.zeros((rows, LANES), jnp.float32)
    for place, part in enumerate(in_three(mean) + in_three(square)):
        table = jnp.where(lane == place, part, table)
    if rows < LANES:
        table = jnp.concatenate(
            [table, jnp.zeros((LANES - rows, LANES), jnp.float32)], axis=0
        )
    stats = jnp.transpose(table)[: rows - 2 * gain_ref.shape[0]]
    sent_ref[:, width:] = jnp.concatenate(
        [stats, gain_ref[...].astype(jnp.float32), bias_ref[...].astype(jnp.float32)],
        axis=0,
    ).astype(sent_ref.dtype)


def own_stream(residual, gain, bias, terms):
    rows, local = residual.shape
    blocks = local // LANES
    return pl.pallas_call(
        functools.partial(stream_kernel, len(terms)),
        out_shape=(
            jax.ShapeDtypeStruct((rows, local), jnp.bfloat16),
            jax.ShapeDtypeStruct((rows, local + LANES), jnp.bfloat16),
        ),
        compiler_params=pltpu.CompilerParams(vmem_limit_bytes=8 * MIB),
        cost_estimate=pl.CostEstimate(
            flops=20 * rows * local, bytes_accessed=16 * rows * local, transcendentals=0
        ),
        name="own_stream",
    )(residual, gain.reshape(blocks, LANES), bias.reshape(blocks, LANES), *terms)


def nothing_kernel(*refs):
    del refs


def first_of_all(piece, *after):
    anywhere = pl.BlockSpec(memory_space=pl.ANY)
    return pl.pallas_call(
        nothing_kernel,
        out_shape=jax.ShapeDtypeStruct(piece.shape, piece.dtype),
        in_specs=[anywhere] * (1 + len(after)),
        out_specs=anywhere,
        input_output_aliases={0: 0},
        compiler_params=pltpu.CompilerParams(vmem_limit_bytes=MIB),
        cost_estimate=pl.CostEstimate(
            flops=10**10, bytes_accessed=10**8, transcendentals=0
        ),
        name="first_of_all",
    )(piece, *after)


def moments(pieces, local):
    rows = pieces[0].shape[0]
    means, spread = [], jnp.zeros((1, LANES), jnp.float32)
    for piece in pieces:
        stats = piece[0:8, local:].astype(jnp.float32)
        means.append(stats[0:1] + stats[1:2] + stats[2:3])
        spread = spread + (stats[3:4] + stats[4:5] + stats[5:6])
    centre = sum(means) / len(means)
    for mean in means:
        spread = spread + local * ((mean - centre) * (mean - centre))
    inverse = lax.rsqrt(spread / (len(means) * local) + 1e-05)
    row = lax.broadcasted_iota(jnp.int32, (LANES, LANES), 0)
    table = jnp.where(row == 0, centre, jnp.where(row == 1, inverse, 0.0))
    table = jnp.transpose(table)[:rows]
    return table[:, 0:1], table[:, 1:2]


def coded_rows(piece, local, centre, inverse, table):
    rows, blocks = piece.shape[0], local // BLOCK_LEN
    unit = 1.0 / math.sqrt(BLOCK_LEN)
    scaling = piece[rows - 2 * blocks :, local:].astype(jnp.float32)
    normal = []
    for b in range(blocks):
        block = piece[:, b * BLOCK_LEN : (b + 1) * BLOCK_LEN].astype(jnp.float32)
        block = (block - centre) * inverse
        normal.append(block * scaling[b : b + 1] + scaling[blocks + b : blocks + b + 1])
    normal = jnp.concatenate(normal, axis=0)
    first = normal.astype(jnp.bfloat16)
    second = (normal - first.astype(jnp.float32)).astype(jnp.bfloat16)
    coded = jnp.dot(first, table, preferred_element_type=jnp.float32)
    coded = coded + jnp.dot(second, table, preferred_element_type=jnp.float32)
    coded = coded * unit
    largest = jnp.max(jnp.abs(coded), axis=1, keepdims=True)
    scales = (largest / 448.0 + 1e-06).astype(jnp.bfloat16).astype(jnp.float32)
    quanta = (coded * (1.0 / scales)).astype(jnp.bfloat16)
    back = jnp.dot(quanta, table, preferred_element_type=jnp.float32) * (scales * unit)
    return back.astype(jnp.bfloat16)


def finish_kernel(places, splits, *refs):
    count = len(places)
    pieces, (out_ref, done_ref, semaphores) = refs[:count], refs[count:]
    rows = pieces[0].shape[0]
    width = done_ref.shape[2]
    table = signs(BLOCK_LEN)
    centre, inverse = moments(pieces, width)
    me = lax.axis_index("tensor")
    outer, inner = me // splits[1], lax.rem(me, splits[1])
    copies = []
    for p, (k, j) in enumerate(places):
        back = coded_rows(pieces[p], width, centre, inverse, table)
        for b in range(width // BLOCK_LEN):
            done_ref[p, :, b * BLOCK_LEN : (b + 1) * BLOCK_LEN] = back[
                b * rows : (b + 1) * rows
            ]
        owner = jnp.bitwise_xor(outer, k) * splits[1] + jnp.bitwise_xor(inner, j)
        columns = pl.ds(pl.multiple_of(owner * width, LANES), width)
        copy = pltpu.make_async_copy(
            done_ref.at[p], out_ref.at[:, columns], semaphores.at[p]
        )
        copy.start()
        copies.append(copy)
    for copy in copies:
        copy.wait()


def finish(places, splits, pieces, local):
    rows = pieces[0].shape[0]
    count = len(pieces)
    vmem = pl.BlockSpec(memory_space=pltpu.VMEM)
    return pl.pallas_call(
        functools.partial(finish_kernel, places, splits),
        out_shape=jax.ShapeDtypeStruct((rows, count * local), jnp.bfloat16),
        in_specs=[vmem] * count,
        out_specs=pl.BlockSpec(memory_space=pl.ANY),
        scratch_shapes=[
            pltpu.VMEM((count, rows, local), jnp.bfloat16),
            pltpu.SemaphoreType.DMA((count,)),
        ],
        compiler_params=pltpu.CompilerParams(vmem_limit_bytes=16 * MIB),
        cost_estimate=pl.CostEstimate(
            flops=8 * BLOCK_LEN * rows * local * count,
            bytes_accessed=4 * rows * local * count,
            transcendentals=0,
        ),
        name="finish",
    )(*pieces)


def body(attended, out_weight, residual, norm_gain, norm_bias):
    n = lax.axis_size("tensor")
    nz, nx = splits = factors(n)
    rows = attended.shape[0]
    local = out_weight.shape[1] // n
    every = [(z, x) for z in range(nz) for x in range(nx)]
    swap = [[(z * nx + x, z * nx + (x ^ j)) for z, x in every] for j in range(nx)]
    jump = [[(z * nx + x, (z ^ k) * nx + x) for z, x in every] for k in range(nz)]

    away = [[(k, j) for j in range(1, nx)] for k in range(nz)]
    here = [[(k, 0)] for k in range(nz)]
    order = list(range(nz - 1, -1, -1))
    calls = [away[order[0]], away[order[1]] + away[order[2]] + here[order[0]]]
    for i in range(2, nz - 1):
        calls.append(away[order[i + 1]] + here[order[i - 1]])
    calls[-1] = calls[-1] + here[1]
    calls.append(here[0])
    joins = [[]] + [[k] for k in order[:-1]] + [[]]
    joins[-3:] = [joins[-3] + joins[-2], []]
    terms = {k: [] for k in range(nz)}
    after = []
    for targets, joined in zip(calls, joins):
        results = products(attended, out_weight, targets, splits, local, after)
        after = [results[-1]]
        for (k, j), result in zip(targets, results):
            terms[k].append(lax.ppermute(result, "tensor", swap[j]) if j else result)
        for k in joined:
            bit = k & -k
            total = terms[k][0].astype(jnp.float32)
            for term in terms[k][1:]:
                total = total + term.astype(jnp.float32)
            total = total.astype(jnp.bfloat16)
            after = [total]
            joined_to = lax.ppermute(total, "tensor", jump[bit])
            if k == nz // 2:
                joined_to = first_of_all(joined_to)
            terms[k ^ bit].append(joined_to)

    stream_out, sent = own_stream(residual, norm_gain, norm_bias, terms[0])
    have = {0: sent}
    crossed = {}
    top = nz // 2
    have[top] = lax.ppermute(sent, "tensor", jump[top])
    have[1] = lax.ppermute(sent, "tensor", jump[1])
    for p in away[0] + away[1]:
        crossed[p] = lax.ppermute(have[p[0]], "tensor", swap[p[1]])
    have[top] = first_of_all(have[top], *crossed.values())
    for k in sorted(range(2, nz), key=lambda k: (k & (k - 1), k)):
        if k != top:
            have[k] = lax.ppermute(have[k ^ (k & -k)], "tensor", jump[k & -k])
    places = [place for k in range(nz) for place in here[k] + away[k]]
    for p in places:
        if p[1] and p not in crossed:
            crossed[p] = lax.ppermute(have[p[0]], "tensor", swap[p[1]])
    pieces = [crossed[p] if p[1] else have[p[0]] for p in places]
    return (stream_out, finish(places, splits, pieces, local))


def solution(mesh):
    placed = (
        P(("groups", "dp"), "tensor"),
        P("tensor", None),
        P(("groups", "dp"), "tensor"),
        P("tensor"),
        P("tensor"),
    )
    return jax.shard_map(
        body,
        mesh=mesh,
        in_specs=placed,
        out_specs=(P(("groups", "dp"), "tensor"), P(("groups", "dp"), None)),
        check_vma=False,
    )
```

```python
import functools
import math

import jax
import jax.numpy as jnp
from jax import lax
from jax.experimental import pallas as pl
from jax.experimental.pallas import tpu as pltpu
from jax.sharding import PartitionSpec as P

BLOCK_LEN = 128
LANES = 128
MIB = 1024 * 1024


def factors(n):
    inner = 1 << ((n.bit_length() - 1) // 2)
    return n // inner, inner


def tile_width(width, most):
    while width % most:
        most //= 2
    return most


def signs(length):
    rows = lax.broadcasted_iota(jnp.int32, (length, length), 0)
    columns = lax.broadcasted_iota(jnp.int32, (length, length), 1)
    common = jnp.bitwise_and(rows, columns)
    parity = jnp.zeros((length, length), jnp.int32)
    for bit_index in range(length.bit_length() - 1):
        parity = parity + jnp.bitwise_and(jnp.right_shift(common, bit_index), 1)
    return (1 - 2 * jnp.bitwise_and(parity, 1)).astype(jnp.bfloat16)


def product_kernel(targets, splits, local, tile, rows_ref, weight_ref, *refs):
    count = len(targets)
    held, scratch, semaphores = refs[-3:]
    outs = refs[-3 - count : -3]
    nx, per = splits[1], local // tile
    me = lax.axis_index("tensor")
    outer, inner = me // nx, lax.rem(me, nx)
    first = pltpu.make_async_copy(rows_ref, held, semaphores.at[count * per])
    first.start()
    copies = []
    for t, (k, j) in enumerate(targets):
        owner = jnp.bitwise_xor(outer, k) * nx + jnp.bitwise_xor(inner, j)
        for i in range(per):
            start = pl.multiple_of(owner * local + i * tile, LANES)
            copy = pltpu.make_async_copy(
                weight_ref.at[:, pl.ds(start, tile)],
                scratch.at[t * per + i],
                semaphores.at[t * per + i],
            )
            copy.start()
            copies.append(copy)
    first.wait()
    for t in range(count):
        for i in range(per):
            copies[t * per + i].wait()
            outs[t][:, i * tile : (i + 1) * tile] = jnp.dot(
                held[...], scratch[t * per + i], preferred_element_type=jnp.float32
            ).astype(outs[t].dtype)


def products(attended, weight, targets, splits, local, after):
    rows, depth = attended.shape
    tile = tile_width(local, 512)
    slots = len(targets) * (local // tile)
    vmem = pl.BlockSpec(memory_space=pltpu.VMEM)
    return pl.pallas_call(
        functools.partial(product_kernel, targets, splits, local, tile),
        out_shape=[
            jax.ShapeDtypeStruct((rows, local), jnp.bfloat16 if j else jnp.float32)
            for _, j in targets
        ],
        in_specs=[pl.BlockSpec(memory_space=pltpu.HBM)] * 2
        + [pl.BlockSpec(memory_space=pl.ANY)] * len(after),
        out_specs=[vmem] * len(targets),
        scratch_shapes=[
            pltpu.VMEM((rows, depth), jnp.bfloat16),
            pltpu.VMEM((slots, depth, tile), jnp.bfloat16),
            pltpu.SemaphoreType.DMA((slots + 1,)),
        ],
        compiler_params=pltpu.CompilerParams(
            vmem_limit_bytes=40 * MIB
        ),
        cost_estimate=pl.CostEstimate(
            flops=2 * rows * depth * local * len(targets),
            bytes_accessed=2 * depth * local * len(targets),
            transcendentals=0,
        ),
        name="products",
    )(attended, weight, *after)


def in_three(values):
    parts = []
    for _ in range(3):
        part = values.astype(jnp.bfloat16)
        parts.append(part.astype(jnp.float32))
        values = values - parts[-1]
    return parts


def stream_kernel(count, residual_ref, gain_ref, bias_ref, *refs):
    terms, (half_ref, sent_ref, stats_ref) = refs[:count], refs[count:]
    stream = residual_ref[...].astype(jnp.float32)
    for term in terms:
        stream = stream + term[...].astype(jnp.float32)
    rows, width = stream.shape
    half = stream.astype(half_ref.dtype)
    half_ref[...] = half
    sent_ref[:, :width] = half
    mean = jnp.sum(stream, axis=1, keepdims=True) / width
    square = jnp.sum((stream - mean) ** 2, axis=1, keepdims=True)
    lane = lax.broadcasted_iota(jnp.int32, (rows, LANES), 1)
    table = jnp.zeros((rows, LANES), jnp.float32)
    for place, part in enumerate(in_three(mean) + in_three(square)):
        table = jnp.where(lane == place, part, table)
    if rows < LANES:
        table = jnp.concatenate(
            [table, jnp.zeros((LANES - rows, LANES), jnp.float32)], axis=0
        )
    stats = jnp.transpose(table)
    stats_ref[...] = stats[: stats_ref.shape[0]].astype(stats_ref.dtype)
    stats = stats[: rows - 2 * gain_ref.shape[0]]
    sent_ref[:, width:] = jnp.concatenate(
        [stats, gain_ref[...].astype(jnp.float32), bias_ref[...].astype(jnp.float32)],
        axis=0,
    ).astype(sent_ref.dtype)


def own_stream(residual, gain, bias, terms):
    rows, local = residual.shape
    blocks = local // LANES
    return pl.pallas_call(
        functools.partial(stream_kernel, len(terms)),
        out_shape=(
            jax.ShapeDtypeStruct((rows, local), jnp.bfloat16),
            jax.ShapeDtypeStruct((rows, local + LANES), jnp.bfloat16),
            jax.ShapeDtypeStruct((16, LANES), jnp.bfloat16),
        ),
        compiler_params=pltpu.CompilerParams(vmem_limit_bytes=8 * MIB),
        cost_estimate=pl.CostEstimate(
            flops=20 * rows * local, bytes_accessed=16 * rows * local, transcendentals=0
        ),
        name="own_stream",
    )(residual, gain.reshape(blocks, LANES), bias.reshape(blocks, LANES), *terms)


def nothing_kernel(*refs):
    del refs


def unchanged(piece, *after, cost=10**10):
    anywhere = pl.BlockSpec(memory_space=pl.ANY)
    return pl.pallas_call(
        nothing_kernel,
        out_shape=jax.ShapeDtypeStruct(piece.shape, piece.dtype),
        in_specs=[anywhere] * (1 + len(after)),
        out_specs=anywhere,
        input_output_aliases={0: 0},
        compiler_params=pltpu.CompilerParams(vmem_limit_bytes=MIB),
        cost_estimate=pl.CostEstimate(
            flops=cost, bytes_accessed=cost // 100, transcendentals=0
        ),
        name="unchanged",
    )(piece, *after)


def moments(tables, counts):
    whole = sum(counts)
    means, squares = [], jnp.zeros((1, LANES), jnp.float32)
    for table in tables:
        stats = table.astype(jnp.float32)
        means.append(stats[0:1] + stats[1:2] + stats[2:3])
        squares = squares + (stats[3:4] + stats[4:5] + stats[5:6])
    centre = sum(mean * (count / whole) for mean, count in zip(means, counts))
    for mean, count in zip(means, counts):
        squares = squares + count * ((mean - centre) * (mean - centre))
    return centre, squares


def merge_kernel(sent_ref, *refs):
    out_ref = refs[-1]
    rows = out_ref.shape[0]
    local = out_ref.shape[1] - LANES
    tables = [sent_ref[0:8, local:]] + [ref[0:8] for ref in refs[:-1]]
    centre, squares = moments(tables, [local] * len(tables))
    row = lax.broadcasted_iota(jnp.int32, (rows, LANES), 0)
    table = sent_ref[:, local:].astype(jnp.float32)
    for place, part in enumerate(in_three(centre) + in_three(squares)):
        table = jnp.where(row == place, part, table)
    out_ref[:, :local] = sent_ref[:, :local]
    out_ref[:, local:] = table.astype(out_ref.dtype)


def merge(sent, others):
    return pl.pallas_call(
        merge_kernel,
        out_shape=jax.ShapeDtypeStruct(sent.shape, sent.dtype),
        compiler_params=pltpu.CompilerParams(vmem_limit_bytes=4 * MIB),
        name="merge",
    )(sent, *others)


def coded_rows(piece, local, centre, inverse, table):
    rows, blocks = piece.shape[0], local // BLOCK_LEN
    unit = 1.0 / math.sqrt(BLOCK_LEN)
    scaling = piece[rows - 2 * blocks :, local:].astype(jnp.float32)
    normal = []
    for b in range(blocks):
        block = piece[:, b * BLOCK_LEN : (b + 1) * BLOCK_LEN].astype(jnp.float32)
        block = (block - centre) * inverse
        normal.append(block * scaling[b : b + 1] + scaling[blocks + b : blocks + b + 1])
    normal = jnp.concatenate(normal, axis=0)
    first = normal.astype(jnp.bfloat16)
    second = (normal - first.astype(jnp.float32)).astype(jnp.bfloat16)
    coded = jnp.dot(first, table, preferred_element_type=jnp.float32)
    coded = coded + jnp.dot(second, table, preferred_element_type=jnp.float32)
    coded = coded * unit
    largest = jnp.max(jnp.abs(coded), axis=1, keepdims=True)
    scales = (largest / 448.0 + 1e-06).astype(jnp.bfloat16).astype(jnp.float32)
    quanta = (coded * (1.0 / scales)).astype(jnp.bfloat16)
    back = jnp.dot(quanta, table, preferred_element_type=jnp.float32) * (scales * unit)
    return back.astype(jnp.bfloat16)


def finish_kernel(places, splits, counts, total, *refs):
    pieces, refs = refs[: len(places)], refs[len(places) :]
    rows = pieces[0].shape[0]
    width = pieces[0].shape[1] - LANES
    if counts:
        tables, (out_ref, columns_ref) = refs[: len(counts)], refs[-4:-2]
        centre, squares = moments([t[0:8, width:] for t in tables], counts)
        inverse = lax.rsqrt(squares / total + 1e-05)
        row = lax.broadcasted_iota(jnp.int32, (LANES, LANES), 0)
        table = jnp.where(row == 0, centre, jnp.where(row == 1, inverse, 0.0))
        columns = jnp.transpose(table)[:rows]
        columns_ref[...] = columns
    else:
        columns, out_ref = refs[0][...], refs[-3]
    done_ref, semaphores = refs[-2:]
    table = signs(BLOCK_LEN)
    me = lax.axis_index("tensor")
    outer, inner = me // splits[1], lax.rem(me, splits[1])
    copies = []
    for p, (k, j) in enumerate(places):
        back = coded_rows(pieces[p], width, columns[:, 0:1], columns[:, 1:2], table)
        for b in range(width // BLOCK_LEN):
            done_ref[p, :, b * BLOCK_LEN : (b + 1) * BLOCK_LEN] = back[
                b * rows : (b + 1) * rows
            ]
        owner = jnp.bitwise_xor(outer, k) * splits[1] + jnp.bitwise_xor(inner, j)
        place = pl.ds(pl.multiple_of(owner * width, LANES), width)
        copy = pltpu.make_async_copy(
            done_ref.at[p], out_ref.at[:, place], semaphores.at[p]
        )
        copy.start()
        copies.append(copy)
    for copy in copies:
        copy.wait()


def finish(places, splits, pieces, tables, counts, earlier, total):
    rows, local = pieces[0].shape[0], pieces[0].shape[1] - LANES
    count = len(pieces)
    vmem = pl.BlockSpec(memory_space=pltpu.VMEM)
    anywhere = pl.BlockSpec(memory_space=pl.ANY)
    given = tables + earlier[::-1]
    out_shape = [jax.ShapeDtypeStruct((rows, total), jnp.bfloat16)]
    if not earlier:
        out_shape.append(jax.ShapeDtypeStruct((rows, LANES), jnp.float32))
    return pl.pallas_call(
        functools.partial(finish_kernel, places, splits, counts, total),
        out_shape=out_shape,
        in_specs=[vmem] * (count + len(given) - len(earlier) // 2)
        + [anywhere] * (len(earlier) // 2),
        out_specs=[anywhere, vmem][: len(out_shape)],
        scratch_shapes=[
            pltpu.VMEM((count, rows, local), jnp.bfloat16),
            pltpu.SemaphoreType.DMA((count,)),
        ],
        input_output_aliases={count + len(given) - 1: 0} if earlier else {},
        compiler_params=pltpu.CompilerParams(vmem_limit_bytes=16 * MIB),
        cost_estimate=pl.CostEstimate(
            flops=8 * BLOCK_LEN * rows * local * count,
            bytes_accessed=4 * rows * local * count,
            transcendentals=0,
        ),
        name="finish",
    )(*pieces, *given)


def body(attended, out_weight, residual, norm_gain, norm_bias):
    n = lax.axis_size("tensor")
    nz, nx = splits = factors(n)
    rows = attended.shape[0]
    local = out_weight.shape[1] // n
    every = [(z, x) for z in range(nz) for x in range(nx)]
    swap = [[(z * nx + x, z * nx + (x ^ j)) for z, x in every] for j in range(nx)]
    jump = [[(z * nx + x, (z ^ k) * nx + x) for z, x in every] for k in range(nz)]

    away = [[(k, j) for j in range(1, nx)] for k in range(nz)]
    here = [[(k, 0)] for k in range(nz)]
    order = list(range(nz - 1, -1, -1))
    calls = [away[order[0]], away[order[1]] + away[order[2]] + here[order[0]]]
    for i in range(2, nz - 1):
        calls.append(away[order[i + 1]] + here[order[i - 1]])
    calls[-1] = calls[-1] + here[1]
    calls.append(here[0])
    joins = [[]] + [[k] for k in order[:-1]] + [[]]
    joins[-3:] = [joins[-3] + joins[-2], []]
    terms = {k: [] for k in range(nz)}
    after, held, released = [], [], []
    for targets, joined in zip(calls, joins):
        results = products(
            attended, out_weight, targets, splits, local, after + released
        )
        after = [results[-1]]
        for (k, j), result in zip(targets, results):
            if j and k:
                result = lax.ppermute(result, "tensor", swap[j])
            if j and not k:
                held.append((result, swap[j]))
            else:
                terms[k].append(result)
        for k in joined:
            bit = k & -k
            total = terms[k][0].astype(jnp.float32)
            for term in terms[k][1:]:
                total = total + term.astype(jnp.float32)
            total = total.astype(jnp.bfloat16)
            after = [total]
            if k == 2:
                for piece, pairs in held:
                    piece = unchanged(piece, total, cost=0)
                    released.append(piece)
                    piece = lax.ppermute(piece, "tensor", pairs)
                    terms[0].append(piece)
            joined_to = lax.ppermute(total, "tensor", jump[bit])
            if k == nz // 2:
                joined_to = unchanged(joined_to)
            terms[k ^ bit].append(joined_to)

    stream_out, sent, stats = own_stream(residual, norm_gain, norm_bias, terms[0])
    others = [lax.ppermute(stats, "tensor", swap[j]) for j in range(1, nx)]
    merged = merge(sent, others)
    have = {0: merged, 1: lax.ppermute(sent, "tensor", jump[1])}
    crossed = {}
    top = nz // 2
    have[top] = lax.ppermute(merged, "tensor", jump[top])
    for k, j in away[0] + away[1]:
        crossed[k, j] = lax.ppermute(have[k] if k else sent, "tensor", swap[j])
    have[top] = unchanged(have[top], *crossed.values())
    for k in sorted(range(2, nz), key=lambda k: (k & (k - 1), k)):
        if k != top:
            have[k] = lax.ppermute(have[k ^ (k & -k)], "tensor", jump[k & -k])
    places = [place for k in range(nz) for place in here[k] + away[k]]
    for k, j in places:
        if j and k > 1:
            crossed[k, j] = lax.ppermute(have[k], "tensor", swap[j])
    pieces = {(k, j): crossed[k, j] if j else have[k] for k, j in places}
    alone = here[1] + away[1]
    tables = [have[k] for k in range(nz) if k != 1] + [pieces[p] for p in alone]
    counts = [nx * local] * (nz - 1) + [local] * len(alone)
    first, last = places[: 1 - nx], places[1 - nx :]
    result = finish(first, splits, [pieces[p] for p in first], tables, counts, [], n * local)
    result = finish(last, splits, [pieces[p] for p in last], [], [], list(result), n * local)
    return (stream_out, result[0])


def solution(mesh):
    placed = (
        P(("groups", "dp"), "tensor"),
        P("tensor", None),
        P(("groups", "dp"), "tensor"),
        P("tensor"),
        P("tensor"),
    )
    return jax.shard_map(
        body,
        mesh=mesh,
        in_specs=placed,
        out_specs=(P(("groups", "dp"), "tensor"), P(("groups", "dp"), None)),
        check_vma=False,
    )
```

```python
import functools
import math

import jax
import jax.numpy as jnp
from jax import lax
from jax.experimental import pallas as pl
from jax.experimental.pallas import tpu as pltpu
from jax.sharding import PartitionSpec as P

BLOCK_LEN = 128
LANES = 128
MIB = 1024 * 1024


def factors(n):
    inner = 1 << ((n.bit_length() - 1) // 2)
    return n // inner, inner


def tile_width(width, most):
    while width % most:
        most //= 2
    return most


def signs(length):
    rows = lax.broadcasted_iota(jnp.int32, (length, length), 0)
    columns = lax.broadcasted_iota(jnp.int32, (length, length), 1)
    common = jnp.bitwise_and(rows, columns)
    parity = jnp.zeros((length, length), jnp.int32)
    for bit_index in range(length.bit_length() - 1):
        parity = parity + jnp.bitwise_and(jnp.right_shift(common, bit_index), 1)
    return (1 - 2 * jnp.bitwise_and(parity, 1)).astype(jnp.bfloat16)


def product_kernel(targets, splits, local, tile, rows_ref, weight_ref, *refs):
    count = len(targets)
    held, scratch, semaphores = refs[-3:]
    outs = refs[-3 - count : -3]
    nx, per = splits[1], local // tile
    me = lax.axis_index("tensor")
    outer, inner = me // nx, lax.rem(me, nx)
    first = pltpu.make_async_copy(rows_ref, held, semaphores.at[count * per])
    first.start()
    copies = []
    for t, (k, j) in enumerate(targets):
        owner = jnp.bitwise_xor(outer, k) * nx + jnp.bitwise_xor(inner, j)
        for i in range(per):
            start = pl.multiple_of(owner * local + i * tile, LANES)
            copy = pltpu.make_async_copy(
                weight_ref.at[:, pl.ds(start, tile)],
                scratch.at[t * per + i],
                semaphores.at[t * per + i],
            )
            copy.start()
            copies.append(copy)
    first.wait()
    for t in range(count):
        for i in range(per):
            copies[t * per + i].wait()
            outs[t][:, i * tile : (i + 1) * tile] = jnp.dot(
                held[...], scratch[t * per + i], preferred_element_type=jnp.float32
            ).astype(outs[t].dtype)


def products(attended, weight, targets, splits, local, after):
    rows, depth = attended.shape
    tile = tile_width(local, 512)
    slots = len(targets) * (local // tile)
    vmem = pl.BlockSpec(memory_space=pltpu.VMEM)
    return pl.pallas_call(
        functools.partial(product_kernel, targets, splits, local, tile),
        out_shape=[
            jax.ShapeDtypeStruct((rows, local), jnp.bfloat16 if j else jnp.float32)
            for _, j in targets
        ],
        in_specs=[pl.BlockSpec(memory_space=pltpu.HBM)] * 2
        + [pl.BlockSpec(memory_space=pl.ANY)] * len(after),
        out_specs=[vmem] * len(targets),
        scratch_shapes=[
            pltpu.VMEM((rows, depth), jnp.bfloat16),
            pltpu.VMEM((slots, depth, tile), jnp.bfloat16),
            pltpu.SemaphoreType.DMA((slots + 1,)),
        ],
        compiler_params=pltpu.CompilerParams(
            vmem_limit_bytes=40 * MIB
        ),
        cost_estimate=pl.CostEstimate(
            flops=2 * rows * depth * local * len(targets),
            bytes_accessed=2 * depth * local * len(targets),
            transcendentals=0,
        ),
        name="products",
    )(attended, weight, *after)


def in_three(values):
    parts = []
    for _ in range(3):
        part = values.astype(jnp.bfloat16)
        parts.append(part.astype(jnp.float32))
        values = values - parts[-1]
    return parts


def stream_kernel(count, residual_ref, gain_ref, bias_ref, *refs):
    terms, (half_ref, sent_ref, stats_ref) = refs[:count], refs[count:]
    stream = residual_ref[...].astype(jnp.float32)
    for term in terms:
        stream = stream + term[...].astype(jnp.float32)
    rows, width = stream.shape
    half = stream.astype(half_ref.dtype)
    half_ref[...] = half
    sent_ref[:, :width] = half
    mean = jnp.sum(stream, axis=1, keepdims=True) / width
    square = jnp.sum((stream - mean) ** 2, axis=1, keepdims=True)
    lane = lax.broadcasted_iota(jnp.int32, (rows, LANES), 1)
    table = jnp.zeros((rows, LANES), jnp.float32)
    for place, part in enumerate(in_three(mean) + in_three(square)):
        table = jnp.where(lane == place, part, table)
    if rows < LANES:
        table = jnp.concatenate(
            [table, jnp.zeros((LANES - rows, LANES), jnp.float32)], axis=0
        )
    stats = jnp.transpose(table)
    stats_ref[...] = stats[: stats_ref.shape[0]].astype(stats_ref.dtype)
    stats = stats[: rows - 2 * gain_ref.shape[0]]
    sent_ref[:, width:] = jnp.concatenate(
        [stats, gain_ref[...].astype(jnp.float32), bias_ref[...].astype(jnp.float32)],
        axis=0,
    ).astype(sent_ref.dtype)


def own_stream(residual, gain, bias, terms):
    rows, local = residual.shape
    blocks = local // LANES
    return pl.pallas_call(
        functools.partial(stream_kernel, len(terms)),
        out_shape=(
            jax.ShapeDtypeStruct((rows, local), jnp.bfloat16),
            jax.ShapeDtypeStruct((rows, local + LANES), jnp.bfloat16),
            jax.ShapeDtypeStruct((16, LANES), jnp.bfloat16),
        ),
        compiler_params=pltpu.CompilerParams(vmem_limit_bytes=8 * MIB),
        cost_estimate=pl.CostEstimate(
            flops=20 * rows * local, bytes_accessed=16 * rows * local, transcendentals=0
        ),
        name="own_stream",
    )(residual, gain.reshape(blocks, LANES), bias.reshape(blocks, LANES), *terms)


def nothing_kernel(*refs):
    del refs


def unchanged(piece, *after, cost=10**10):
    anywhere = pl.BlockSpec(memory_space=pl.ANY)
    return pl.pallas_call(
        nothing_kernel,
        out_shape=jax.ShapeDtypeStruct(piece.shape, piece.dtype),
        in_specs=[anywhere] * (1 + len(after)),
        out_specs=anywhere,
        input_output_aliases={0: 0},
        compiler_params=pltpu.CompilerParams(vmem_limit_bytes=MIB),
        cost_estimate=pl.CostEstimate(
            flops=cost, bytes_accessed=cost // 100, transcendentals=0
        ),
        name="unchanged",
    )(piece, *after)


def moments(tables, counts):
    whole = sum(counts)
    means, squares = [], jnp.zeros((1, LANES), jnp.float32)
    for table in tables:
        stats = table.astype(jnp.float32)
        means.append(stats[0:1] + stats[1:2] + stats[2:3])
        squares = squares + (stats[3:4] + stats[4:5] + stats[5:6])
    centre = sum(mean * (count / whole) for mean, count in zip(means, counts))
    for mean, count in zip(means, counts):
        squares = squares + count * ((mean - centre) * (mean - centre))
    return centre, squares


def merge_kernel(local, *refs):
    out_ref = refs[-1]
    centre, squares = moments([ref[0:8] for ref in refs[:-1]], [local] * len(refs[:-1]))
    row = lax.broadcasted_iota(jnp.int32, out_ref.shape, 0)
    table = jnp.zeros(out_ref.shape, jnp.float32)
    for place, part in enumerate(in_three(centre) + in_three(squares)):
        table = jnp.where(row == place, part, table)
    out_ref[...] = table.astype(out_ref.dtype)


def merge(tables, local):
    return pl.pallas_call(
        functools.partial(merge_kernel, local),
        out_shape=jax.ShapeDtypeStruct(tables[0].shape, tables[0].dtype),
        compiler_params=pltpu.CompilerParams(vmem_limit_bytes=2 * MIB),
        cost_estimate=pl.CostEstimate(
            flops=10**9, bytes_accessed=10**7, transcendentals=0
        ),
        name="merge",
    )(*tables)


def replace_kernel(piece_ref, table_ref, *refs):
    out_ref = refs[-1]
    local, height = piece_ref.shape[1] - LANES, table_ref.shape[0]
    out_ref[:, :local] = piece_ref[:, :local]
    out_ref[:, local:] = piece_ref[:, local:]
    row = lax.broadcasted_iota(jnp.int32, table_ref.shape, 0)
    table = jnp.where(
        row < 6,
        table_ref[...].astype(jnp.float32),
        piece_ref[:height, local:].astype(jnp.float32),
    )
    out_ref[:height, local:] = table.astype(out_ref.dtype)


def replace(piece, table, after):
    vmem = pl.BlockSpec(memory_space=pltpu.VMEM)
    return pl.pallas_call(
        replace_kernel,
        out_shape=jax.ShapeDtypeStruct(piece.shape, piece.dtype),
        in_specs=[vmem, vmem] + [pl.BlockSpec(memory_space=pl.ANY)] * len(after),
        out_specs=vmem,
        compiler_params=pltpu.CompilerParams(vmem_limit_bytes=4 * MIB),
        name="replace",
    )(piece, table, *after)


def coded_rows(piece, local, centre, inverse, table):
    rows, blocks = piece.shape[0], local // BLOCK_LEN
    unit = 1.0 / math.sqrt(BLOCK_LEN)
    scaling = piece[rows - 2 * blocks :, local:].astype(jnp.float32)
    normal = []
    for b in range(blocks):
        block = piece[:, b * BLOCK_LEN : (b + 1) * BLOCK_LEN].astype(jnp.float32)
        block = (block - centre) * inverse
        normal.append(block * scaling[b : b + 1] + scaling[blocks + b : blocks + b + 1])
    normal = jnp.concatenate(normal, axis=0)
    first = normal.astype(jnp.bfloat16)
    second = (normal - first.astype(jnp.float32)).astype(jnp.bfloat16)
    coded = jnp.dot(first, table, preferred_element_type=jnp.float32)
    coded = coded + jnp.dot(second, table, preferred_element_type=jnp.float32)
    coded = coded * unit
    largest = jnp.max(jnp.abs(coded), axis=1, keepdims=True)
    scales = (largest / 448.0 + 1e-06).astype(jnp.bfloat16).astype(jnp.float32)
    quanta = (coded * (1.0 / scales)).astype(jnp.bfloat16)
    back = jnp.dot(quanta, table, preferred_element_type=jnp.float32) * (scales * unit)
    return back.astype(jnp.bfloat16)


def finish_kernel(places, splits, counts, total, *refs):
    pieces, refs = refs[: len(places)], refs[len(places) :]
    rows = pieces[0].shape[0]
    width = pieces[0].shape[1] - LANES
    if counts:
        tables, (out_ref, columns_ref) = refs[: len(counts)], refs[-4:-2]
        centre, squares = moments(
            [t[0:8, t.shape[1] - LANES :] for t in tables], counts
        )
        inverse = lax.rsqrt(squares / total + 1e-05)
        row = lax.broadcasted_iota(jnp.int32, (LANES, LANES), 0)
        table = jnp.where(row == 0, centre, jnp.where(row == 1, inverse, 0.0))
        columns = jnp.transpose(table)[:rows]
        columns_ref[...] = columns
    else:
        columns, out_ref = refs[0][...], refs[-3]
    done_ref, semaphores = refs[-2:]
    table = signs(BLOCK_LEN)
    me = lax.axis_index("tensor")
    outer, inner = me // splits[1], lax.rem(me, splits[1])
    copies = []
    for p, (k, j) in enumerate(places):
        back = coded_rows(pieces[p], width, columns[:, 0:1], columns[:, 1:2], table)
        for b in range(width // BLOCK_LEN):
            done_ref[p, :, b * BLOCK_LEN : (b + 1) * BLOCK_LEN] = back[
                b * rows : (b + 1) * rows
            ]
        owner = jnp.bitwise_xor(outer, k) * splits[1] + jnp.bitwise_xor(inner, j)
        place = pl.ds(pl.multiple_of(owner * width, LANES), width)
        copy = pltpu.make_async_copy(
            done_ref.at[p], out_ref.at[:, place], semaphores.at[p]
        )
        copy.start()
        copies.append(copy)
    for copy in copies:
        copy.wait()


def finish(places, splits, pieces, tables, counts, earlier, total):
    rows, local = pieces[0].shape[0], pieces[0].shape[1] - LANES
    count = len(pieces)
    vmem = pl.BlockSpec(memory_space=pltpu.VMEM)
    anywhere = pl.BlockSpec(memory_space=pl.ANY)
    given = tables + earlier[::-1]
    out_shape = [jax.ShapeDtypeStruct((rows, total), jnp.bfloat16)]
    if not earlier:
        out_shape.append(jax.ShapeDtypeStruct((rows, LANES), jnp.float32))
    return pl.pallas_call(
        functools.partial(finish_kernel, places, splits, counts, total),
        out_shape=out_shape,
        in_specs=[vmem] * (count + len(given) - len(earlier) // 2)
        + [anywhere] * (len(earlier) // 2),
        out_specs=[anywhere, vmem][: len(out_shape)],
        scratch_shapes=[
            pltpu.VMEM((count, rows, local), jnp.bfloat16),
            pltpu.SemaphoreType.DMA((count,)),
        ],
        input_output_aliases={count + len(given) - 1: 0} if earlier else {},
        compiler_params=pltpu.CompilerParams(vmem_limit_bytes=16 * MIB),
        cost_estimate=pl.CostEstimate(
            flops=8 * BLOCK_LEN * rows * local * count,
            bytes_accessed=4 * rows * local * count,
            transcendentals=0,
        ),
        name="finish",
    )(*pieces, *given)


def body(attended, out_weight, residual, norm_gain, norm_bias):
    n = lax.axis_size("tensor")
    nz, nx = splits = factors(n)
    rows = attended.shape[0]
    local = out_weight.shape[1] // n
    every = [(z, x) for z in range(nz) for x in range(nx)]
    swap = [[(z * nx + x, z * nx + (x ^ j)) for z, x in every] for j in range(nx)]
    jump = [[(z * nx + x, (z ^ k) * nx + x) for z, x in every] for k in range(nz)]

    away = [[(k, j) for j in range(1, nx)] for k in range(nz)]
    here = [[(k, 0)] for k in range(nz)]
    order = list(range(nz - 1, -1, -1))
    calls = [away[order[0]], away[order[1]] + away[order[2]] + here[order[0]]]
    for i in range(2, nz - 1):
        calls.append(away[order[i + 1]] + here[order[i - 1]])
    calls[-1] = calls[-1] + here[1]
    calls.append(here[0])
    joins = [[]] + [[k] for k in order[:-1]] + [[]]
    joins[-3:] = [joins[-3] + joins[-2], []]
    terms = {k: [] for k in range(nz)}
    after, held, released = [], [], []
    for targets, joined in zip(calls, joins):
        results = products(
            attended, out_weight, targets, splits, local, after + released
        )
        after = [results[-1]]
        for (k, j), result in zip(targets, results):
            if j and k:
                result = lax.ppermute(result, "tensor", swap[j])
            if j and not k:
                held.append((result, swap[j]))
            else:
                terms[k].append(result)
        for k in joined:
            bit = k & -k
            total = terms[k][0].astype(jnp.float32)
            for term in terms[k][1:]:
                total = total + term.astype(jnp.float32)
            total = total.astype(jnp.bfloat16)
            after = [total]
            if k == 2:
                for piece, pairs in held:
                    piece = unchanged(piece, total, cost=0)
                    released.append(piece)
                    piece = lax.ppermute(piece, "tensor", pairs)
                    terms[0].append(piece)
            joined_to = lax.ppermute(total, "tensor", jump[bit])
            if k == nz // 2:
                joined_to = unchanged(joined_to)
            terms[k ^ bit].append(joined_to)

    stream_out, sent, stats = own_stream(residual, norm_gain, norm_bias, terms[0])
    have = {0: sent, 1: lax.ppermute(sent, "tensor", jump[1])}
    top = nz // 2
    far = lax.ppermute(sent, "tensor", jump[top])
    others = [lax.ppermute(stats, "tensor", swap[j]) for j in range(1, nx)]
    merged = merge([stats] + others, local)
    have[1] = unchanged(have[1], merged, cost=0)
    crossed = {}
    for k, j in away[0] + away[1]:
        crossed[k, j] = lax.ppermute(have[k], "tensor", swap[j])
    have[top] = replace(
        far,
        lax.ppermute(merged, "tensor", jump[top]),
        [have[1]] + [crossed[p] for p in away[0]],
    )
    whole = replace(sent, merged, []) if top > 2 else sent
    for k in sorted(range(2, nz), key=lambda k: (k & (k - 1), k)):
        if k != top:
            rest = k & (k - 1)
            have[k] = lax.ppermute(have[rest] if rest else whole, "tensor", jump[k & -k])
    for p in away[1]:
        crossed[p] = unchanged(unchanged(crossed[p]))
    places = [place for k in range(nz) for place in here[k] + away[k]]
    for k, j in places:
        if j and k > 1:
            crossed[k, j] = lax.ppermute(have[k], "tensor", swap[j])
    pieces = {(k, j): crossed[k, j] if j else have[k] for k, j in places}
    alone = here[1] + away[1]
    tables = [merged] + [have[k] for k in range(2, nz)] + [pieces[p] for p in alone]
    counts = [nx * local] * (nz - 1) + [local] * len(alone)
    first, last = places[: 1 - nx], places[1 - nx :]
    result = finish(first, splits, [pieces[p] for p in first], tables, counts, [], n * local)
    result = finish(last, splits, [pieces[p] for p in last], [], [], list(result), n * local)
    return (stream_out, result[0])


def solution(mesh):
    placed = (
        P(("groups", "dp"), "tensor"),
        P("tensor", None),
        P(("groups", "dp"), "tensor"),
        P("tensor"),
        P("tensor"),
    )
    return jax.shard_map(
        body,
        mesh=mesh,
        in_specs=placed,
        out_specs=(P(("groups", "dp"), "tensor"), P(("groups", "dp"), None)),
        check_vma=False,
    )
```

```python
import functools
import math

import jax
import jax.numpy as jnp
from jax import lax
from jax.experimental import pallas as pl
from jax.experimental.pallas import tpu as pltpu
from jax.sharding import PartitionSpec as P

BLOCK_LEN = 128
LANES = 128
MIB = 1024 * 1024


def factors(n):
    inner = 1 << ((n.bit_length() - 1) // 2)
    return n // inner, inner


def tile_width(width, most):
    while width % most:
        most //= 2
    return most


def signs(length):
    rows = lax.broadcasted_iota(jnp.int32, (length, length), 0)
    columns = lax.broadcasted_iota(jnp.int32, (length, length), 1)
    common = jnp.bitwise_and(rows, columns)
    parity = jnp.zeros((length, length), jnp.int32)
    for bit_index in range(length.bit_length() - 1):
        parity = parity + jnp.bitwise_and(jnp.right_shift(common, bit_index), 1)
    return (1 - 2 * jnp.bitwise_and(parity, 1)).astype(jnp.bfloat16)


def product_kernel(targets, splits, local, tile, rows_ref, weight_ref, *refs):
    count = len(targets)
    held, scratch, semaphores = refs[-3:]
    token = refs[-4]
    outs = refs[-4 - count : -4]
    token[...] = jnp.zeros_like(token)
    nx, per = splits[1], local // tile
    me = lax.axis_index("tensor")
    outer, inner = me // nx, lax.rem(me, nx)
    first = pltpu.make_async_copy(rows_ref, held, semaphores.at[count * per])
    first.start()
    copies = []
    for t, (k, j) in enumerate(targets):
        owner = jnp.bitwise_xor(outer, k) * nx + jnp.bitwise_xor(inner, j)
        for i in range(per):
            start = pl.multiple_of(owner * local + i * tile, LANES)
            copy = pltpu.make_async_copy(
                weight_ref.at[:, pl.ds(start, tile)],
                scratch.at[t * per + i],
                semaphores.at[t * per + i],
            )
            copy.start()
            copies.append(copy)
    first.wait()
    for t in range(count):
        for i in range(per):
            copies[t * per + i].wait()
            outs[t][:, i * tile : (i + 1) * tile] = jnp.dot(
                held[...], scratch[t * per + i], preferred_element_type=jnp.float32
            ).astype(outs[t].dtype)


def products(attended, weight, targets, splits, local, after):
    rows, depth = attended.shape
    tile = tile_width(local, 512)
    slots = len(targets) * (local // tile)
    vmem = pl.BlockSpec(memory_space=pltpu.VMEM)
    return pl.pallas_call(
        functools.partial(product_kernel, targets, splits, local, tile),
        out_shape=[
            jax.ShapeDtypeStruct((rows, local), jnp.bfloat16 if j else jnp.float32)
            for _, j in targets
        ]
        + [jax.ShapeDtypeStruct((8, LANES), jnp.float32)],
        in_specs=[pl.BlockSpec(memory_space=pltpu.HBM)] * 2
        + [pl.BlockSpec(memory_space=pl.ANY)] * len(after),
        out_specs=[vmem] * (len(targets) + 1),
        scratch_shapes=[
            pltpu.VMEM((rows, depth), jnp.bfloat16),
            pltpu.VMEM((slots, depth, tile), jnp.bfloat16),
            pltpu.SemaphoreType.DMA((slots + 1,)),
        ],
        compiler_params=pltpu.CompilerParams(
            vmem_limit_bytes=(40 if after else 60) * MIB
        ),
        cost_estimate=pl.CostEstimate(
            flops=2 * rows * depth * local * len(targets),
            bytes_accessed=2 * depth * local * len(targets),
            transcendentals=0,
        ),
        name="products",
    )(attended, weight, *after)


def in_three(values):
    parts = []
    for _ in range(3):
        part = values.astype(jnp.bfloat16)
        parts.append(part.astype(jnp.float32))
        values = values - parts[-1]
    return parts


def stream_kernel(count, residual_ref, gain_ref, bias_ref, *refs):
    terms, (half_ref, sent_ref, stats_ref, *head) = refs[:count], refs[count:]
    stream = residual_ref[...].astype(jnp.float32)
    for term in terms:
        stream = stream + term[...].astype(jnp.float32)
    rows, width = stream.shape
    half = stream.astype(half_ref.dtype)
    half_ref[...] = half
    sent_ref[:, :width] = half
    for ref in head:
        ref[...] = half[:, : ref.shape[1]]
    mean = jnp.sum(stream, axis=1, keepdims=True) / width
    square = jnp.sum((stream - mean) ** 2, axis=1, keepdims=True)
    lane = lax.broadcasted_iota(jnp.int32, (rows, LANES), 1)
    table = jnp.zeros((rows, LANES), jnp.float32)
    for place, part in enumerate(in_three(mean) + in_three(square)):
        table = jnp.where(lane == place, part, table)
    if rows < LANES:
        table = jnp.concatenate(
            [table, jnp.zeros((LANES - rows, LANES), jnp.float32)], axis=0
        )
    stats = jnp.transpose(table)
    stats_ref[...] = stats[: stats_ref.shape[0]].astype(stats_ref.dtype)
    stats = stats[: rows - 2 * gain_ref.shape[0]]
    sent_ref[:, width:] = jnp.concatenate(
        [stats, gain_ref[...].astype(jnp.float32), bias_ref[...].astype(jnp.float32)],
        axis=0,
    ).astype(sent_ref.dtype)


def own_stream(residual, gain, bias, terms, first):
    rows, local = residual.shape
    blocks = local // LANES
    return pl.pallas_call(
        functools.partial(stream_kernel, len(terms)),
        out_shape=(
            jax.ShapeDtypeStruct((rows, local), jnp.bfloat16),
            jax.ShapeDtypeStruct((rows, local + LANES), jnp.bfloat16),
            jax.ShapeDtypeStruct((16, LANES), jnp.bfloat16),
        )
        + (jax.ShapeDtypeStruct((rows, first), jnp.bfloat16),) * bool(first),
        compiler_params=pltpu.CompilerParams(vmem_limit_bytes=8 * MIB),
        cost_estimate=pl.CostEstimate(
            flops=20 * rows * local, bytes_accessed=16 * rows * local, transcendentals=0
        ),
        name="own_stream",
    )(residual, gain.reshape(blocks, LANES), bias.reshape(blocks, LANES), *terms)


def nothing_kernel(*refs):
    del refs


def unchanged(piece, *after, cost=10**10):
    anywhere = pl.BlockSpec(memory_space=pl.ANY)
    return pl.pallas_call(
        nothing_kernel,
        out_shape=jax.ShapeDtypeStruct(piece.shape, piece.dtype),
        in_specs=[anywhere] * (1 + len(after)),
        out_specs=anywhere,
        input_output_aliases={0: 0},
        compiler_params=pltpu.CompilerParams(vmem_limit_bytes=MIB),
        cost_estimate=pl.CostEstimate(
            flops=cost, bytes_accessed=cost // 100, transcendentals=0
        ),
        name="unchanged",
    )(piece, *after)


def moments(tables, counts):
    whole = sum(counts)
    means, squares = [], jnp.zeros((1, LANES), jnp.float32)
    for table in tables:
        stats = table.astype(jnp.float32)
        means.append(stats[0:1] + stats[1:2] + stats[2:3])
        squares = squares + (stats[3:4] + stats[4:5] + stats[5:6])
    centre = sum(mean * (count / whole) for mean, count in zip(means, counts))
    for mean, count in zip(means, counts):
        squares = squares + count * ((mean - centre) * (mean - centre))
    return centre, squares


def merge_kernel(first, sent_ref, *refs):
    out_ref = refs[-1]
    rows = out_ref.shape[0]
    local = sent_ref.shape[1] - LANES
    tables = [sent_ref[0:8, local:]] + [ref[0:8] for ref in refs[:-1]]
    centre, squares = moments(tables, [local] * len(tables))
    row = lax.broadcasted_iota(jnp.int32, (rows, LANES), 0)
    table = sent_ref[:, local:].astype(jnp.float32)
    for place, part in enumerate(in_three(centre) + in_three(squares)):
        table = jnp.where(row == place, part, table)
    out_ref[:, : local - first] = sent_ref[:, first:local]
    out_ref[:, local - first :] = table.astype(out_ref.dtype)


def merge(sent, others, first):
    return pl.pallas_call(
        functools.partial(merge_kernel, first),
        out_shape=jax.ShapeDtypeStruct((sent.shape[0], sent.shape[1] - first), sent.dtype),
        compiler_params=pltpu.CompilerParams(vmem_limit_bytes=4 * MIB),
        name="merge",
    )(sent, *others)


def coded_rows(parts, local, centre, inverse, table):
    rows, blocks = parts[0].shape[0], local // BLOCK_LEN
    unit = 1.0 / math.sqrt(BLOCK_LEN)
    columns = [part[:, c : c + LANES] for part in parts for c in range(0, part.shape[1], LANES)]
    scaling = columns[-1][rows - 2 * blocks :].astype(jnp.float32)
    normal = []
    for b in range(blocks):
        block = columns[b].astype(jnp.float32)
        block = (block - centre) * inverse
        normal.append(block * scaling[b : b + 1] + scaling[blocks + b : blocks + b + 1])
    normal = jnp.concatenate(normal, axis=0)
    first = normal.astype(jnp.bfloat16)
    second = (normal - first.astype(jnp.float32)).astype(jnp.bfloat16)
    coded = jnp.dot(first, table, preferred_element_type=jnp.float32)
    coded = coded + jnp.dot(second, table, preferred_element_type=jnp.float32)
    coded = coded * unit
    largest = jnp.max(jnp.abs(coded), axis=1, keepdims=True)
    scales = (largest / 448.0 + 1e-06).astype(jnp.bfloat16).astype(jnp.float32)
    quanta = (coded * (1.0 / scales)).astype(jnp.bfloat16)
    back = jnp.dot(quanta, table, preferred_element_type=jnp.float32) * (scales * unit)
    return back.astype(jnp.bfloat16)


def finish_kernel(places, splits, lengths, counts, total, *refs):
    pieces = []
    for length in lengths:
        pieces.append(refs[:length])
        refs = refs[length:]
    rows, width = refs[-2].shape[1:]
    if counts:
        tables, (out_ref, columns_ref) = refs[: len(counts)], refs[-4:-2]
        centre, squares = moments(
            [t[0:8, t.shape[1] - LANES :] for t in tables], counts
        )
        inverse = lax.rsqrt(squares / total + 1e-05)
        row = lax.broadcasted_iota(jnp.int32, (LANES, LANES), 0)
        table = jnp.where(row == 0, centre, jnp.where(row == 1, inverse, 0.0))
        columns = jnp.transpose(table)[:rows]
        columns_ref[...] = columns
    else:
        columns, out_ref = refs[0][...], refs[-3]
    done_ref, semaphores = refs[-2:]
    table = signs(BLOCK_LEN)
    me = lax.axis_index("tensor")
    outer, inner = me // splits[1], lax.rem(me, splits[1])
    copies = []
    for p, (k, j) in enumerate(places):
        back = coded_rows(pieces[p], width, columns[:, 0:1], columns[:, 1:2], table)
        for b in range(width // BLOCK_LEN):
            done_ref[p, :, b * BLOCK_LEN : (b + 1) * BLOCK_LEN] = back[
                b * rows : (b + 1) * rows
            ]
        owner = jnp.bitwise_xor(outer, k) * splits[1] + jnp.bitwise_xor(inner, j)
        place = pl.ds(pl.multiple_of(owner * width, LANES), width)
        copy = pltpu.make_async_copy(
            done_ref.at[p], out_ref.at[:, place], semaphores.at[p]
        )
        copy.start()
        copies.append(copy)
    for copy in copies:
        copy.wait()


def finish(places, splits, pieces, local, tables, counts, earlier, total):
    rows = pieces[0][0].shape[0]
    count = len(pieces)
    lengths = [len(parts) for parts in pieces]
    pieces = [part for parts in pieces for part in parts]
    vmem = pl.BlockSpec(memory_space=pltpu.VMEM)
    anywhere = pl.BlockSpec(memory_space=pl.ANY)
    given = pieces + tables + earlier[::-1]
    out_shape = [jax.ShapeDtypeStruct((rows, total), jnp.bfloat16)]
    if not earlier:
        out_shape.append(jax.ShapeDtypeStruct((rows, LANES), jnp.float32))
    return pl.pallas_call(
        functools.partial(finish_kernel, places, splits, lengths, counts, total),
        out_shape=out_shape,
        in_specs=[vmem] * (len(given) - len(earlier) // 2)
        + [anywhere] * (len(earlier) // 2),
        out_specs=[anywhere, vmem][: len(out_shape)],
        scratch_shapes=[
            pltpu.VMEM((count, rows, local), jnp.bfloat16),
            pltpu.SemaphoreType.DMA((count,)),
        ],
        input_output_aliases={len(given) - 1: 0} if earlier else {},
        compiler_params=pltpu.CompilerParams(vmem_limit_bytes=16 * MIB),
        cost_estimate=pl.CostEstimate(
            flops=8 * BLOCK_LEN * rows * local * count,
            bytes_accessed=4 * rows * local * count,
            transcendentals=0,
        ),
        name="finish",
    )(*given)


def body(attended, out_weight, residual, norm_gain, norm_bias):
    n = lax.axis_size("tensor")
    nz, nx = splits = factors(n)
    rows = attended.shape[0]
    local = out_weight.shape[1] // n
    every = [(z, x) for z in range(nz) for x in range(nx)]
    swap = [[(z * nx + x, z * nx + (x ^ j)) for z, x in every] for j in range(nx)]
    jump = [[(z * nx + x, (z ^ k) * nx + x) for z, x in every] for k in range(nz)]

    away = [[(k, j) for j in range(1, nx)] for k in range(nz)]
    here = [[(k, 0)] for k in range(nz)]
    order = list(range(nz - 1, -1, -1))
    calls = [away[order[0]], away[order[1]] + away[order[2]] + here[order[0]]]
    for i in range(2, nz - 1):
        calls.append(away[order[i + 1]] + here[order[i - 1]])
    calls[-1] = calls[-1] + here[1]
    calls.append(here[0])
    joins = [[]] + [[k] for k in order[:-1]] + [[]]
    joins[-3:] = [joins[-3] + joins[-2], []]
    terms = {k: [] for k in range(nz)}
    after, held, released = [], [], []
    for targets, joined in zip(calls, joins):
        *results, token = products(
            attended, out_weight, targets, splits, local, after + released
        )
        after = [token]
        for (k, j), result in zip(targets, results):
            if j and k:
                result = lax.ppermute(result, "tensor", swap[j])
            if j and not k:
                held.append((result, swap[j]))
            else:
                terms[k].append(result)
        for k in joined:
            bit = k & -k
            total = terms[k][0].astype(jnp.float32)
            for term in terms[k][1:]:
                total = total + term.astype(jnp.float32)
            total = total.astype(jnp.bfloat16)
            after = [total]
            if k == 2:
                for piece, pairs in held:
                    piece = unchanged(piece, total, cost=0)
                    released.append(piece)
                    piece = lax.ppermute(piece, "tensor", pairs)
                    terms[0].append(piece)
            joined_to = lax.ppermute(total, "tensor", jump[bit])
            if k == nz // 2:
                joined_to = unchanged(joined_to)
            terms[k ^ bit].append(joined_to)

    first = local // 2 if local % (2 * LANES) == 0 else 0
    stream_out, sent, stats, *head = own_stream(
        residual, norm_gain, norm_bias, terms[0], first
    )
    others = [lax.ppermute(stats, "tensor", swap[j]) for j in range(1, nx)]
    base = head + [merge(sent, others, first)]
    top = nz // 2
    near = unchanged(lax.ppermute(sent, "tensor", jump[1]), base[-1], cost=0)
    have = {0: [sent], 1: [near]}
    crossed = {}
    for k, j in away[0] + away[1]:
        crossed[k, j] = [lax.ppermute(have[k][0], "tensor", swap[j])]
    far = [lax.ppermute(part, "tensor", jump[top]) for part in base]
    far[:-1] = [unchanged(part, near) for part in far[:-1]]
    far[-1] = unchanged(far[-1], *far[:-1], *[crossed[p][0] for p in away[0] + away[1]])
    have[top] = far
    for k in sorted(range(2, nz), key=lambda k: (k & (k - 1), k)):
        if k != top:
            rest = k & (k - 1)
            have[k] = [
                lax.ppermute(part, "tensor", jump[k & -k])
                for part in (have[rest] if rest else base)
            ]
    places = [place for k in range(nz) for place in here[k] + away[k]]
    for k, j in places:
        if j and k > 1:
            parts = [lax.ppermute(part, "tensor", swap[j]) for part in have[k]]
            if k in (top, nz - 1):
                parts[:-1] = [unchanged(part) for part in parts[:-1]]
            crossed[k, j] = parts
    pieces = {(k, j): crossed[k, j] if j else have[k] for k, j in places}
    alone = here[1] + away[1]
    tables = [base[-1]] + [have[k][-1] for k in range(2, nz)] + [pieces[p][0] for p in alone]
    counts = [nx * local] * (nz - 1) + [local] * len(alone)
    early, last = places[: 1 - nx], places[1 - nx :]
    result = finish(
        early, splits, [pieces[p] for p in early], local, tables, counts, [], n * local
    )
    result = finish(
        last, splits, [pieces[p] for p in last], local, [], [], list(result), n * local
    )
    return (stream_out, result[0])


def solution(mesh):
    placed = (
        P(("groups", "dp"), "tensor"),
        P("tensor", None),
        P(("groups", "dp"), "tensor"),
        P("tensor"),
        P("tensor"),
    )
    return jax.shard_map(
        body,
        mesh=mesh,
        in_specs=placed,
        out_specs=(P(("groups", "dp"), "tensor"), P(("groups", "dp"), None)),
        check_vma=False,
    )
```

```python
import functools
import math

import jax
import jax.numpy as jnp
from jax import lax
from jax.experimental import pallas as pl
from jax.experimental.pallas import tpu as pltpu
from jax.sharding import PartitionSpec as P

BLOCK_LEN = 128
LANES = 128
MIB = 1024 * 1024


def factors(n):
    inner = 1 << ((n.bit_length() - 1) // 2)
    return n // inner, inner


def tile_width(width, most):
    while width % most:
        most //= 2
    return most


def signs(length):
    rows = lax.broadcasted_iota(jnp.int32, (length, length), 0)
    columns = lax.broadcasted_iota(jnp.int32, (length, length), 1)
    common = jnp.bitwise_and(rows, columns)
    parity = jnp.zeros((length, length), jnp.int32)
    for bit_index in range(length.bit_length() - 1):
        parity = parity + jnp.bitwise_and(jnp.right_shift(common, bit_index), 1)
    return (1 - 2 * jnp.bitwise_and(parity, 1)).astype(jnp.bfloat16)


def product_kernel(targets, splits, local, tile, rows_ref, weight_ref, *refs):
    count = len(targets)
    held, scratch, semaphores = refs[-3:]
    outs = refs[-3 - count : -3]
    nx, per = splits[1], local // tile
    me = lax.axis_index("tensor")
    outer, inner = me // nx, lax.rem(me, nx)
    first = pltpu.make_async_copy(rows_ref, held, semaphores.at[count * per])
    first.start()
    copies = []
    for t, (k, j) in enumerate(targets):
        owner = jnp.bitwise_xor(outer, k) * nx + jnp.bitwise_xor(inner, j)
        for i in range(per):
            start = pl.multiple_of(owner * local + i * tile, LANES)
            copy = pltpu.make_async_copy(
                weight_ref.at[:, pl.ds(start, tile)],
                scratch.at[t * per + i],
                semaphores.at[t * per + i],
            )
            copy.start()
            copies.append(copy)
    first.wait()
    for t in range(count):
        for i in range(per):
            copies[t * per + i].wait()
            outs[t][:, i * tile : (i + 1) * tile] = jnp.dot(
                held[...], scratch[t * per + i], preferred_element_type=jnp.float32
            ).astype(outs[t].dtype)


def products(attended, weight, targets, splits, local, after):
    rows, depth = attended.shape
    tile = tile_width(local, 512)
    slots = len(targets) * (local // tile)
    vmem = pl.BlockSpec(memory_space=pltpu.VMEM)
    return pl.pallas_call(
        functools.partial(product_kernel, targets, splits, local, tile),
        out_shape=[
            jax.ShapeDtypeStruct((rows, local), jnp.bfloat16 if j else jnp.float32)
            for _, j in targets
        ],
        in_specs=[pl.BlockSpec(memory_space=pltpu.HBM)] * 2
        + [pl.BlockSpec(memory_space=pl.ANY)] * len(after),
        out_specs=[vmem] * len(targets),
        scratch_shapes=[
            pltpu.VMEM((rows, depth), jnp.bfloat16),
            pltpu.VMEM((slots, depth, tile), jnp.bfloat16),
            pltpu.SemaphoreType.DMA((slots + 1,)),
        ],
        compiler_params=pltpu.CompilerParams(
            vmem_limit_bytes=40 * MIB
        ),
        cost_estimate=pl.CostEstimate(
            flops=2 * rows * depth * local * len(targets),
            bytes_accessed=2 * depth * local * len(targets),
            transcendentals=0,
        ),
        name="products",
    )(attended, weight, *after)


def in_three(values):
    parts = []
    for _ in range(3):
        part = values.astype(jnp.bfloat16)
        parts.append(part.astype(jnp.float32))
        values = values - parts[-1]
    return parts


def stream_kernel(count, residual_ref, gain_ref, bias_ref, *refs):
    terms, (half_ref, sent_ref, tail_ref, *head) = refs[:count], refs[count:]
    stream = residual_ref[...].astype(jnp.float32)
    for term in terms:
        stream = stream + term[...].astype(jnp.float32)
    rows, width = stream.shape
    half = stream.astype(half_ref.dtype)
    half_ref[...] = half
    sent_ref[:, :width] = half
    for ref in head:
        ref[...] = half[:, : ref.shape[1]]
    mean = jnp.sum(stream, axis=1, keepdims=True) / width
    square = jnp.sum((stream - mean) ** 2, axis=1, keepdims=True)
    lane = lax.broadcasted_iota(jnp.int32, (rows, LANES), 1)
    table = jnp.zeros((rows, LANES), jnp.float32)
    for place, part in enumerate(in_three(mean) + in_three(square)):
        table = jnp.where(lane == place, part, table)
    if rows < LANES:
        table = jnp.concatenate(
            [table, jnp.zeros((LANES - rows, LANES), jnp.float32)], axis=0
        )
    stats = jnp.transpose(table)
    stats = stats[: rows - 2 * gain_ref.shape[0]]
    shared = jnp.concatenate(
        [stats, gain_ref[...].astype(jnp.float32), bias_ref[...].astype(jnp.float32)],
        axis=0,
    ).astype(sent_ref.dtype)
    sent_ref[:, width:] = shared
    rest = tail_ref.shape[1] - LANES
    tail_ref[:, :rest] = half[:, width - rest :]
    tail_ref[:, rest:] = shared


def own_stream(residual, gain, bias, terms, first):
    rows, local = residual.shape
    blocks = local // LANES
    return pl.pallas_call(
        functools.partial(stream_kernel, len(terms)),
        out_shape=(
            jax.ShapeDtypeStruct((rows, local), jnp.bfloat16),
            jax.ShapeDtypeStruct((rows, local + LANES), jnp.bfloat16),
            jax.ShapeDtypeStruct((rows, local + LANES - first), jnp.bfloat16),
        )
        + (jax.ShapeDtypeStruct((rows, first), jnp.bfloat16),) * bool(first),
        compiler_params=pltpu.CompilerParams(vmem_limit_bytes=8 * MIB),
        cost_estimate=pl.CostEstimate(
            flops=20 * rows * local, bytes_accessed=16 * rows * local, transcendentals=0
        ),
        name="own_stream",
    )(residual, gain.reshape(blocks, LANES), bias.reshape(blocks, LANES), *terms)


def nothing_kernel(*refs):
    del refs


def unchanged(piece, *after, cost=10**10):
    anywhere = pl.BlockSpec(memory_space=pl.ANY)
    return pl.pallas_call(
        nothing_kernel,
        out_shape=jax.ShapeDtypeStruct(piece.shape, piece.dtype),
        in_specs=[anywhere] * (1 + len(after)),
        out_specs=anywhere,
        input_output_aliases={0: 0},
        compiler_params=pltpu.CompilerParams(vmem_limit_bytes=MIB),
        cost_estimate=pl.CostEstimate(
            flops=cost, bytes_accessed=cost // 100, transcendentals=0
        ),
        name="unchanged",
    )(piece, *after)


def moments(tables, counts):
    whole = sum(counts)
    means, squares = [], jnp.zeros((1, LANES), jnp.float32)
    for table in tables:
        stats = table.astype(jnp.float32)
        means.append(stats[0:1] + stats[1:2] + stats[2:3])
        squares = squares + (stats[3:4] + stats[4:5] + stats[5:6])
    centre = sum(mean * (count / whole) for mean, count in zip(means, counts))
    for mean, count in zip(means, counts):
        squares = squares + count * ((mean - centre) * (mean - centre))
    return centre, squares


def merge_kernel(local, *refs):
    tail_ref, out_ref = refs[0], refs[-1]
    rest = out_ref.shape[1] - LANES
    tables = [ref[0:8, rest:] for ref in refs[:-1]]
    centre, squares = moments(tables, [local] * len(tables))
    row = lax.broadcasted_iota(jnp.int32, (out_ref.shape[0], LANES), 0)
    table = tail_ref[:, rest:].astype(jnp.float32)
    for place, part in enumerate(in_three(centre) + in_three(squares)):
        table = jnp.where(row == place, part, table)
    out_ref[:, :rest] = tail_ref[:, :rest]
    out_ref[:, rest:] = table.astype(out_ref.dtype)


def merge(tails, local):
    return pl.pallas_call(
        functools.partial(merge_kernel, local),
        out_shape=jax.ShapeDtypeStruct(tails[0].shape, tails[0].dtype),
        compiler_params=pltpu.CompilerParams(vmem_limit_bytes=4 * MIB),
        name="merge",
    )(*tails)


def coded_rows(parts, local, centre, inverse, table):
    rows, blocks = parts[0].shape[0], local // BLOCK_LEN
    unit = 1.0 / math.sqrt(BLOCK_LEN)
    columns = [part[:, c : c + LANES] for part in parts for c in range(0, part.shape[1], LANES)]
    scaling = columns[-1][rows - 2 * blocks :].astype(jnp.float32)
    normal = []
    for b in range(blocks):
        block = columns[b].astype(jnp.float32)
        block = (block - centre) * inverse
        normal.append(block * scaling[b : b + 1] + scaling[blocks + b : blocks + b + 1])
    normal = jnp.concatenate(normal, axis=0)
    first = normal.astype(jnp.bfloat16)
    second = (normal - first.astype(jnp.float32)).astype(jnp.bfloat16)
    coded = jnp.dot(first, table, preferred_element_type=jnp.float32)
    coded = coded + jnp.dot(second, table, preferred_element_type=jnp.float32)
    coded = coded * unit
    largest = jnp.max(jnp.abs(coded), axis=1, keepdims=True)
    scales = (largest / 448.0 + 1e-06).astype(jnp.bfloat16).astype(jnp.float32)
    quanta = (coded * (1.0 / scales)).astype(jnp.bfloat16)
    back = jnp.dot(quanta, table, preferred_element_type=jnp.float32) * (scales * unit)
    return back.astype(jnp.bfloat16)


def finish_kernel(places, splits, lengths, counts, total, *refs):
    pieces = []
    for length in lengths:
        pieces.append(refs[:length])
        refs = refs[length:]
    rows, width = refs[-2].shape[1:]
    if counts:
        tables, (out_ref, columns_ref) = refs[: len(counts)], refs[-4:-2]
        centre, squares = moments(
            [t[0:8, t.shape[1] - LANES :] for t in tables], counts
        )
        inverse = lax.rsqrt(squares / total + 1e-05)
        row = lax.broadcasted_iota(jnp.int32, (LANES, LANES), 0)
        table = jnp.where(row == 0, centre, jnp.where(row == 1, inverse, 0.0))
        columns = jnp.transpose(table)[:rows]
        columns_ref[...] = columns
    else:
        columns, out_ref = refs[0][...], refs[-3]
    done_ref, semaphores = refs[-2:]
    table = signs(BLOCK_LEN)
    me = lax.axis_index("tensor")
    outer, inner = me // splits[1], lax.rem(me, splits[1])
    copies = []
    for p, (k, j) in enumerate(places):
        back = coded_rows(pieces[p], width, columns[:, 0:1], columns[:, 1:2], table)
        for b in range(width // BLOCK_LEN):
            done_ref[p, :, b * BLOCK_LEN : (b + 1) * BLOCK_LEN] = back[
                b * rows : (b + 1) * rows
            ]
        owner = jnp.bitwise_xor(outer, k) * splits[1] + jnp.bitwise_xor(inner, j)
        place = pl.ds(pl.multiple_of(owner * width, LANES), width)
        copy = pltpu.make_async_copy(
            done_ref.at[p], out_ref.at[:, place], semaphores.at[p]
        )
        copy.start()
        copies.append(copy)
    for copy in copies:
        copy.wait()


def finish(places, splits, pieces, local, tables, counts, earlier, total):
    rows = pieces[0][0].shape[0]
    count = len(pieces)
    lengths = [len(parts) for parts in pieces]
    pieces = [part for parts in pieces for part in parts]
    vmem = pl.BlockSpec(memory_space=pltpu.VMEM)
    anywhere = pl.BlockSpec(memory_space=pl.ANY)
    given = pieces + tables + earlier[::-1]
    out_shape = [jax.ShapeDtypeStruct((rows, total), jnp.bfloat16)]
    if not earlier:
        out_shape.append(jax.ShapeDtypeStruct((rows, LANES), jnp.float32))
    return pl.pallas_call(
        functools.partial(finish_kernel, places, splits, lengths, counts, total),
        out_shape=out_shape,
        in_specs=[vmem] * (len(given) - len(earlier) // 2)
        + [anywhere] * (len(earlier) // 2),
        out_specs=[anywhere, vmem][: len(out_shape)],
        scratch_shapes=[
            pltpu.VMEM((count, rows, local), jnp.bfloat16),
            pltpu.SemaphoreType.DMA((count,)),
        ],
        input_output_aliases={len(given) - 1: 0} if earlier else {},
        compiler_params=pltpu.CompilerParams(vmem_limit_bytes=16 * MIB),
        cost_estimate=pl.CostEstimate(
            flops=8 * BLOCK_LEN * rows * local * count,
            bytes_accessed=4 * rows * local * count,
            transcendentals=0,
        ),
        name="finish",
    )(*given)


def body(attended, out_weight, residual, norm_gain, norm_bias):
    n = lax.axis_size("tensor")
    nz, nx = splits = factors(n)
    rows = attended.shape[0]
    local = out_weight.shape[1] // n
    every = [(z, x) for z in range(nz) for x in range(nx)]
    swap = [[(z * nx + x, z * nx + (x ^ j)) for z, x in every] for j in range(nx)]
    jump = [[(z * nx + x, (z ^ k) * nx + x) for z, x in every] for k in range(nz)]

    away = [[(k, j) for j in range(1, nx)] for k in range(nz)]
    here = [[(k, 0)] for k in range(nz)]
    order = list(range(nz - 1, -1, -1))
    calls = [away[order[0]], away[order[1]] + away[order[2]] + here[order[0]]]
    for i in range(2, nz - 1):
        calls.append(away[order[i + 1]] + here[order[i - 1]])
    calls[-1] = calls[-1] + here[1]
    calls.append(here[0])
    joins = [[]] + [[k] for k in order[:-1]] + [[]]
    joins[-3:] = [joins[-3] + joins[-2], []]
    terms = {k: [] for k in range(nz)}
    after, held, released = [], [], []
    for targets, joined in zip(calls, joins):
        results = products(
            attended, out_weight, targets, splits, local, after + released
        )
        after = [results[-1]]
        for (k, j), result in zip(targets, results):
            if j and k:
                result = lax.ppermute(result, "tensor", swap[j])
            if j and not k:
                held.append((result, swap[j]))
            else:
                terms[k].append(result)
        for k in joined:
            bit = k & -k
            total = terms[k][0].astype(jnp.float32)
            for term in terms[k][1:]:
                total = total + term.astype(jnp.float32)
            total = total.astype(jnp.bfloat16)
            after = [total]
            if k == 2:
                for piece, pairs in held:
                    piece = unchanged(piece, total, cost=0)
                    released.append(piece)
                    piece = lax.ppermute(piece, "tensor", pairs)
                    terms[0].append(piece)
            joined_to = lax.ppermute(total, "tensor", jump[bit])
            if k == nz // 2:
                joined_to = unchanged(joined_to)
            terms[k ^ bit].append(joined_to)

    first = local // 2 if local % (2 * LANES) == 0 else 0
    stream_out, sent, tail, *head = own_stream(
        residual, norm_gain, norm_bias, terms[0], first
    )
    crossed, waited = {}, []
    for p in away[0]:
        crossed[p] = [lax.ppermute(part, "tensor", swap[p[1]]) for part in [tail] + head][::-1]
        waited += crossed[p][:-1]
    tails = [crossed[p][-1] for p in away[0]]
    base = [unchanged(part, *tails, cost=0) for part in head]
    base.append(merge([tail] + tails, local))
    top = nz // 2
    near = lax.ppermute(sent, "tensor", jump[1])
    near = unchanged(near, base[-1], *waited, cost=0)
    have = {0: head + [tail], 1: [near]}
    for p in away[1]:
        crossed[p] = [lax.ppermute(near, "tensor", swap[p[1]])]
    far = [lax.ppermute(part, "tensor", jump[top]) for part in base]
    far[:-1] = [unchanged(part, near) for part in far[:-1]]
    far[-1] = unchanged(far[-1], *far[:-1], *[crossed[p][0] for p in away[1]])
    have[top] = far
    for k in sorted(range(2, nz), key=lambda k: (k & (k - 1), k)):
        if k != top:
            rest = k & (k - 1)
            have[k] = [
                lax.ppermute(part, "tensor", jump[k & -k])
                for part in (have[rest] if rest else base)
            ]
    places = [place for k in range(nz) for place in here[k] + away[k]]
    for k, j in places:
        if j and k > 1:
            parts = [lax.ppermute(part, "tensor", swap[j]) for part in have[k]]
            if k in (top, nz - 1):
                parts[:-1] = [unchanged(part) for part in parts[:-1]]
            crossed[k, j] = parts
    pieces = {(k, j): crossed[k, j] if j else have[k] for k, j in places}
    alone = here[1] + away[1]
    tables = [base[-1]] + [have[k][-1] for k in range(2, nz)] + [pieces[p][0] for p in alone]
    counts = [nx * local] * (nz - 1) + [local] * len(alone)
    early, last = places[: 1 - nx], places[1 - nx :]
    result = finish(
        early, splits, [pieces[p] for p in early], local, tables, counts, [], n * local
    )
    result = finish(
        last, splits, [pieces[p] for p in last], local, [], [], list(result), n * local
    )
    return (stream_out, result[0])


def solution(mesh):
    placed = (
        P(("groups", "dp"), "tensor"),
        P("tensor", None),
        P(("groups", "dp"), "tensor"),
        P("tensor"),
        P("tensor"),
    )
    return jax.shard_map(
        body,
        mesh=mesh,
        in_specs=placed,
        out_specs=(P(("groups", "dp"), "tensor"), P(("groups", "dp"), None)),
        check_vma=False,
    )
```

```python
import functools
import math

import jax
import jax.numpy as jnp
from jax import lax
from jax.experimental import pallas as pl
from jax.experimental.pallas import tpu as pltpu
from jax.sharding import PartitionSpec as P

BLOCK_LEN = 128
LANES = 128
MIB = 1024 * 1024


def factors(n):
    inner = 1 << ((n.bit_length() - 1) // 2)
    return n // inner, inner


def tile_width(width, most):
    while width % most:
        most //= 2
    return most


def signs(length):
    rows = lax.broadcasted_iota(jnp.int32, (length, length), 0)
    columns = lax.broadcasted_iota(jnp.int32, (length, length), 1)
    common = jnp.bitwise_and(rows, columns)
    parity = jnp.zeros((length, length), jnp.int32)
    for bit_index in range(length.bit_length() - 1):
        parity = parity + jnp.bitwise_and(jnp.right_shift(common, bit_index), 1)
    return (1 - 2 * jnp.bitwise_and(parity, 1)).astype(jnp.bfloat16)


def product_kernel(targets, splits, local, tile, rows_ref, weight_ref, *refs):
    count = len(targets)
    held, scratch, semaphores = refs[-3:]
    outs = refs[-3 - count : -3]
    nx, per = splits[1], local // tile
    me = lax.axis_index("tensor")
    outer, inner = me // nx, lax.rem(me, nx)
    first = pltpu.make_async_copy(rows_ref, held, semaphores.at[count * per])
    first.start()
    copies = []
    for t, (k, j) in enumerate(targets):
        owner = jnp.bitwise_xor(outer, k) * nx + jnp.bitwise_xor(inner, j)
        for i in range(per):
            start = pl.multiple_of(owner * local + i * tile, LANES)
            copy = pltpu.make_async_copy(
                weight_ref.at[:, pl.ds(start, tile)],
                scratch.at[t * per + i],
                semaphores.at[t * per + i],
            )
            copy.start()
            copies.append(copy)
    first.wait()
    for t in range(count):
        for i in range(per):
            copies[t * per + i].wait()
            outs[t][:, i * tile : (i + 1) * tile] = jnp.dot(
                held[...], scratch[t * per + i], preferred_element_type=jnp.float32
            ).astype(outs[t].dtype)


def products(attended, weight, targets, splits, local, after):
    rows, depth = attended.shape
    tile = tile_width(local, 256)
    slots = len(targets) * (local // tile)
    vmem = pl.BlockSpec(memory_space=pltpu.VMEM)
    return pl.pallas_call(
        functools.partial(product_kernel, targets, splits, local, tile),
        out_shape=[
            jax.ShapeDtypeStruct((rows, local), jnp.bfloat16 if j else jnp.float32)
            for _, j in targets
        ],
        in_specs=[pl.BlockSpec(memory_space=pltpu.HBM)] * 2
        + [pl.BlockSpec(memory_space=pl.ANY)] * len(after),
        out_specs=[vmem] * len(targets),
        scratch_shapes=[
            pltpu.VMEM((rows, depth), jnp.bfloat16),
            pltpu.VMEM((slots, depth, tile), jnp.bfloat16),
            pltpu.SemaphoreType.DMA((slots + 1,)),
        ],
        compiler_params=pltpu.CompilerParams(
            vmem_limit_bytes=40 * MIB
        ),
        cost_estimate=pl.CostEstimate(
            flops=2 * rows * depth * local * len(targets),
            bytes_accessed=2 * depth * local * len(targets),
            transcendentals=0,
        ),
        name="products",
    )(attended, weight, *after)


def in_three(values):
    parts = []
    for _ in range(3):
        part = values.astype(jnp.bfloat16)
        parts.append(part.astype(jnp.float32))
        values = values - parts[-1]
    return parts


def stream_kernel(count, residual_ref, gain_ref, bias_ref, *refs):
    terms, (half_ref, sent_ref, stats_ref) = refs[:count], refs[count:]
    stream = residual_ref[...].astype(jnp.float32)
    for term in terms:
        stream = stream + term[...].astype(jnp.float32)
    rows, width = stream.shape
    half = stream.astype(half_ref.dtype)
    half_ref[...] = half
    sent_ref[:, :width] = half
    mean = jnp.sum(stream, axis=1, keepdims=True) / width
    square = jnp.sum((stream - mean) ** 2, axis=1, keepdims=True)
    lane = lax.broadcasted_iota(jnp.int32, (rows, LANES), 1)
    table = jnp.zeros((rows, LANES), jnp.float32)
    for place, part in enumerate(in_three(mean) + in_three(square)):
        table = jnp.where(lane == place, part, table)
    if rows < LANES:
        table = jnp.concatenate(
            [table, jnp.zeros((LANES - rows, LANES), jnp.float32)], axis=0
        )
    stats = jnp.transpose(table)
    stats_ref[...] = stats[: stats_ref.shape[0]].astype(stats_ref.dtype)
    stats = stats[: rows - 2 * gain_ref.shape[0]]
    sent_ref[:, width:] = jnp.concatenate(
        [stats, gain_ref[...].astype(jnp.float32), bias_ref[...].astype(jnp.float32)],
        axis=0,
    ).astype(sent_ref.dtype)


def own_stream(residual, gain, bias, terms):
    rows, local = residual.shape
    blocks = local // LANES
    return pl.pallas_call(
        functools.partial(stream_kernel, len(terms)),
        out_shape=(
            jax.ShapeDtypeStruct((rows, local), jnp.bfloat16),
            jax.ShapeDtypeStruct((rows, local + LANES), jnp.bfloat16),
            jax.ShapeDtypeStruct((16, LANES), jnp.bfloat16),
        ),
        compiler_params=pltpu.CompilerParams(vmem_limit_bytes=8 * MIB),
        cost_estimate=pl.CostEstimate(
            flops=20 * rows * local, bytes_accessed=16 * rows * local, transcendentals=0
        ),
        name="own_stream",
    )(residual, gain.reshape(blocks, LANES), bias.reshape(blocks, LANES), *terms)


def nothing_kernel(*refs):
    del refs


def unchanged(piece, *after, cost=10**10):
    anywhere = pl.BlockSpec(memory_space=pl.ANY)
    return pl.pallas_call(
        nothing_kernel,
        out_shape=jax.ShapeDtypeStruct(piece.shape, piece.dtype),
        in_specs=[anywhere] * (1 + len(after)),
        out_specs=anywhere,
        input_output_aliases={0: 0},
        compiler_params=pltpu.CompilerParams(vmem_limit_bytes=MIB),
        cost_estimate=pl.CostEstimate(
            flops=cost, bytes_accessed=cost // 100, transcendentals=0
        ),
        name="unchanged",
    )(piece, *after)


def moments(tables, counts):
    whole = sum(counts)
    means, squares = [], jnp.zeros((1, LANES), jnp.float32)
    for table in tables:
        stats = table.astype(jnp.float32)
        means.append(stats[0:1] + stats[1:2] + stats[2:3])
        squares = squares + (stats[3:4] + stats[4:5] + stats[5:6])
    centre = sum(mean * (count / whole) for mean, count in zip(means, counts))
    for mean, count in zip(means, counts):
        squares = squares + count * ((mean - centre) * (mean - centre))
    return centre, squares


def merge_kernel(sent_ref, *refs):
    out_ref = refs[-1]
    rows = out_ref.shape[0]
    local = out_ref.shape[1] - LANES
    tables = [sent_ref[0:8, local:]] + [ref[0:8] for ref in refs[:-1]]
    centre, squares = moments(tables, [local] * len(tables))
    row = lax.broadcasted_iota(jnp.int32, (rows, LANES), 0)
    table = sent_ref[:, local:].astype(jnp.float32)
    for place, part in enumerate(in_three(centre) + in_three(squares)):
        table = jnp.where(row == place, part, table)
    out_ref[:, :local] = sent_ref[:, :local]
    out_ref[:, local:] = table.astype(out_ref.dtype)


def merge(sent, others):
    return pl.pallas_call(
        merge_kernel,
        out_shape=jax.ShapeDtypeStruct(sent.shape, sent.dtype),
        compiler_params=pltpu.CompilerParams(vmem_limit_bytes=4 * MIB),
        name="merge",
    )(sent, *others)


def coded_rows(piece, local, chosen, centre, inverse, table):
    rows, blocks = piece.shape[0], local // BLOCK_LEN
    unit = 1.0 / math.sqrt(BLOCK_LEN)
    scaling = piece[rows - 2 * blocks :, local:].astype(jnp.float32)
    normal = []
    for b in chosen:
        block = piece[:, b * BLOCK_LEN : (b + 1) * BLOCK_LEN].astype(jnp.float32)
        block = (block - centre) * inverse
        normal.append(block * scaling[b : b + 1] + scaling[blocks + b : blocks + b + 1])
    normal = jnp.concatenate(normal, axis=0)
    first = normal.astype(jnp.bfloat16)
    second = (normal - first.astype(jnp.float32)).astype(jnp.bfloat16)
    coded = jnp.dot(first, table, preferred_element_type=jnp.float32)
    coded = coded + jnp.dot(second, table, preferred_element_type=jnp.float32)
    coded = coded * unit
    largest = jnp.max(jnp.abs(coded), axis=1, keepdims=True)
    scales = (largest / 448.0 + 1e-06).astype(jnp.bfloat16).astype(jnp.float32)
    quanta = (coded * (1.0 / scales)).astype(jnp.bfloat16)
    back = jnp.dot(quanta, table, preferred_element_type=jnp.float32) * (scales * unit)
    return back.astype(jnp.bfloat16)


def finish_kernel(places, splits, counts, total, *refs):
    pieces, refs = refs[: len(places)], refs[len(places) :]
    rows = pieces[0].shape[0]
    width = pieces[0].shape[1] - LANES
    if counts:
        tables, (out_ref, columns_ref) = refs[: len(counts)], refs[-4:-2]
        centre, squares = moments([t[0:8, width:] for t in tables], counts)
        inverse = lax.rsqrt(squares / total + 1e-05)
        row = lax.broadcasted_iota(jnp.int32, (LANES, LANES), 0)
        table = jnp.where(row == 0, centre, jnp.where(row == 1, inverse, 0.0))
        columns = jnp.transpose(table)[:rows]
        columns_ref[...] = columns
    else:
        columns, out_ref = refs[0][...], refs[-3]
    done_ref, semaphores = refs[-2:]
    table = signs(BLOCK_LEN)
    me = lax.axis_index("tensor")
    outer, inner = me // splits[1], lax.rem(me, splits[1])
    copies = []
    blocks = width // BLOCK_LEN
    step = blocks // 2 if len(places) == 1 and blocks > 1 else blocks
    for p, (k, j) in enumerate(places):
        owner = jnp.bitwise_xor(outer, k) * splits[1] + jnp.bitwise_xor(inner, j)
        for begin in range(0, blocks, step):
            chosen = range(begin, begin + step)
            back = coded_rows(
                pieces[p], width, chosen, columns[:, 0:1], columns[:, 1:2], table
            )
            for i, b in enumerate(chosen):
                done_ref[p, :, b * BLOCK_LEN : (b + 1) * BLOCK_LEN] = back[
                    i * rows : (i + 1) * rows
                ]
            here = pl.ds(begin * BLOCK_LEN, step * BLOCK_LEN)
            start = pl.multiple_of(owner * width + begin * BLOCK_LEN, LANES)
            copy = pltpu.make_async_copy(
                done_ref.at[p, :, here],
                out_ref.at[:, pl.ds(start, step * BLOCK_LEN)],
                semaphores.at[len(copies)],
            )
            copy.start()
            copies.append(copy)
    for copy in copies:
        copy.wait()


def finish(places, splits, pieces, tables, counts, earlier, total):
    rows, local = pieces[0].shape[0], pieces[0].shape[1] - LANES
    count = len(pieces)
    vmem = pl.BlockSpec(memory_space=pltpu.VMEM)
    anywhere = pl.BlockSpec(memory_space=pl.ANY)
    given = tables + earlier[::-1]
    out_shape = [jax.ShapeDtypeStruct((rows, total), jnp.bfloat16)]
    if not earlier:
        out_shape.append(jax.ShapeDtypeStruct((rows, LANES), jnp.float32))
    return pl.pallas_call(
        functools.partial(finish_kernel, places, splits, counts, total),
        out_shape=out_shape,
        in_specs=[vmem] * (count + len(given) - len(earlier) // 2)
        + [anywhere] * (len(earlier) // 2),
        out_specs=[anywhere, vmem][: len(out_shape)],
        scratch_shapes=[
            pltpu.VMEM((count, rows, local), jnp.bfloat16),
            pltpu.SemaphoreType.DMA((count + 1,)),
        ],
        input_output_aliases={count + len(given) - 1: 0} if earlier else {},
        compiler_params=pltpu.CompilerParams(vmem_limit_bytes=16 * MIB),
        cost_estimate=pl.CostEstimate(
            flops=8 * BLOCK_LEN * rows * local * count,
            bytes_accessed=4 * rows * local * count,
            transcendentals=0,
        ),
        name="finish",
    )(*pieces, *given)


def body(attended, out_weight, residual, norm_gain, norm_bias):
    n = lax.axis_size("tensor")
    nz, nx = splits = factors(n)
    rows = attended.shape[0]
    local = out_weight.shape[1] // n
    every = [(z, x) for z in range(nz) for x in range(nx)]
    swap = [[(z * nx + x, z * nx + (x ^ j)) for z, x in every] for j in range(nx)]
    jump = [[(z * nx + x, (z ^ k) * nx + x) for z, x in every] for k in range(nz)]

    away = [[(k, j) for j in range(1, nx)] for k in range(nz)]
    here = [[(k, 0)] for k in range(nz)]
    order = list(range(nz - 1, -1, -1))
    calls = [away[order[0]], away[order[1]] + away[order[2]] + here[order[0]]]
    for i in range(2, nz - 1):
        calls.append(away[order[i + 1]] + here[order[i - 1]])
    calls[-1] = calls[-1] + here[1]
    calls.append(here[0])
    joins = [[]] + [[k] for k in order[:-1]] + [[]]
    joins[-3:] = [joins[-3] + joins[-2], []]
    terms = {k: [] for k in range(nz)}
    after, held, released = [], [], []
    for targets, joined in zip(calls, joins):
        results = products(
            attended, out_weight, targets, splits, local, after + released
        )
        after = [results[-1]]
        for (k, j), result in zip(targets, results):
            if j and k:
                result = lax.ppermute(result, "tensor", swap[j])
            if j and not k:
                held.append((result, swap[j]))
            else:
                terms[k].append(result)
        for k in joined:
            bit = k & -k
            total = terms[k][0].astype(jnp.float32)
            for term in terms[k][1:]:
                total = total + term.astype(jnp.float32)
            total = total.astype(jnp.bfloat16)
            after = [total]
            if k == 2:
                for piece, pairs in held:
                    piece = unchanged(piece, total, cost=0)
                    released.append(piece)
                    piece = lax.ppermute(piece, "tensor", pairs)
                    terms[0].append(piece)
            joined_to = lax.ppermute(total, "tensor", jump[bit])
            if k == nz // 2:
                joined_to = unchanged(joined_to)
            terms[k ^ bit].append(joined_to)

    stream_out, sent, stats = own_stream(residual, norm_gain, norm_bias, terms[0])
    others = [lax.ppermute(stats, "tensor", swap[j]) for j in range(1, nx)]
    merged = merge(sent, others)
    have = {0: merged, 1: lax.ppermute(sent, "tensor", jump[1])}
    crossed = {}
    top = nz // 2
    have[top] = lax.ppermute(merged, "tensor", jump[top])
    for k, j in away[0] + away[1]:
        crossed[k, j] = lax.ppermute(have[k] if k else sent, "tensor", swap[j])
    have[top] = unchanged(have[top], *crossed.values())
    for k in sorted(range(2, nz), key=lambda k: (k & (k - 1), k)):
        if k != top:
            have[k] = lax.ppermute(have[k ^ (k & -k)], "tensor", jump[k & -k])
    places = [place for k in range(nz) for place in here[k] + away[k]]
    for k, j in places:
        if j and k > 1:
            crossed[k, j] = lax.ppermute(have[k], "tensor", swap[j])
    pieces = {(k, j): crossed[k, j] if j else have[k] for k, j in places}
    alone = here[1] + away[1]
    tables = [have[k] for k in range(nz) if k != 1] + [pieces[p] for p in alone]
    counts = [nx * local] * (nz - 1) + [local] * len(alone)
    first, last = places[: 1 - nx], places[1 - nx :]
    result = finish(first, splits, [pieces[p] for p in first], tables, counts, [], n * local)
    result = finish(last, splits, [pieces[p] for p in last], [], [], list(result), n * local)
    return (stream_out, result[0])


def solution(mesh):
    placed = (
        P(("groups", "dp"), "tensor"),
        P("tensor", None),
        P(("groups", "dp"), "tensor"),
        P("tensor"),
        P("tensor"),
    )
    return jax.shard_map(
        body,
        mesh=mesh,
        in_specs=placed,
        out_specs=(P(("groups", "dp"), "tensor"), P(("groups", "dp"), None)),
        check_vma=False,
    )
```

```python
import functools
import math

import jax
import jax.numpy as jnp
from jax import lax
from jax.experimental import pallas as pl
from jax.experimental.pallas import tpu as pltpu
from jax.sharding import PartitionSpec as P

BLOCK_LEN = 128
LANES = 128
MIB = 1024 * 1024


def factors(n):
    inner = 1 << ((n.bit_length() - 1) // 2)
    return n // inner, inner


def tile_width(width, most):
    while width % most:
        most //= 2
    return most


def signs(length):
    rows = lax.broadcasted_iota(jnp.int32, (length, length), 0)
    columns = lax.broadcasted_iota(jnp.int32, (length, length), 1)
    common = jnp.bitwise_and(rows, columns)
    parity = jnp.zeros((length, length), jnp.int32)
    for bit_index in range(length.bit_length() - 1):
        parity = parity + jnp.bitwise_and(jnp.right_shift(common, bit_index), 1)
    return (1 - 2 * jnp.bitwise_and(parity, 1)).astype(jnp.bfloat16)


def product_kernel(targets, splits, local, tile, rows_ref, weight_ref, *refs):
    count = len(targets)
    held, scratch, semaphores = refs[-3:]
    outs = refs[-3 - count : -3]
    nx, per = splits[1], local // tile
    me = lax.axis_index("tensor")
    outer, inner = me // nx, lax.rem(me, nx)
    first = pltpu.make_async_copy(rows_ref, held, semaphores.at[count * per])
    first.start()
    copies = []
    for t, (k, j) in enumerate(targets):
        owner = jnp.bitwise_xor(outer, k) * nx + jnp.bitwise_xor(inner, j)
        for i in range(per):
            start = pl.multiple_of(owner * local + i * tile, LANES)
            copy = pltpu.make_async_copy(
                weight_ref.at[:, pl.ds(start, tile)],
                scratch.at[t * per + i],
                semaphores.at[t * per + i],
            )
            copy.start()
            copies.append(copy)
    first.wait()
    for t in range(count):
        for i in range(per):
            copies[t * per + i].wait()
            outs[t][:, i * tile : (i + 1) * tile] = jnp.dot(
                held[...], scratch[t * per + i], preferred_element_type=jnp.float32
            ).astype(outs[t].dtype)


def products(attended, weight, targets, splits, local, after):
    rows, depth = attended.shape
    tile = tile_width(local, 1024 if len(targets) > 1 else 512)
    slots = len(targets) * (local // tile)
    vmem = pl.BlockSpec(memory_space=pltpu.VMEM)
    return pl.pallas_call(
        functools.partial(product_kernel, targets, splits, local, tile),
        out_shape=[
            jax.ShapeDtypeStruct((rows, local), jnp.bfloat16 if j else jnp.float32)
            for _, j in targets
        ],
        in_specs=[pl.BlockSpec(memory_space=pltpu.HBM)] * 2
        + [pl.BlockSpec(memory_space=pl.ANY)] * len(after),
        out_specs=[vmem] * len(targets),
        scratch_shapes=[
            pltpu.VMEM((rows, depth), jnp.bfloat16),
            pltpu.VMEM((slots, depth, tile), jnp.bfloat16),
            pltpu.SemaphoreType.DMA((slots + 1,)),
        ],
        compiler_params=pltpu.CompilerParams(
            vmem_limit_bytes=40 * MIB
        ),
        cost_estimate=pl.CostEstimate(
            flops=2 * rows * depth * local * len(targets),
            bytes_accessed=2 * depth * local * len(targets),
            transcendentals=0,
        ),
        name="products",
    )(attended, weight, *after)


def in_three(values):
    parts = []
    for _ in range(3):
        part = values.astype(jnp.bfloat16)
        parts.append(part.astype(jnp.float32))
        values = values - parts[-1]
    return parts


def stream_kernel(count, residual_ref, gain_ref, bias_ref, *refs):
    terms, (half_ref, sent_ref, stats_ref) = refs[:count], refs[count:]
    stream = residual_ref[...].astype(jnp.float32)
    for term in terms:
        stream = stream + term[...].astype(jnp.float32)
    rows, width = stream.shape
    half = stream.astype(half_ref.dtype)
    half_ref[...] = half
    sent_ref[:, :width] = half
    mean = jnp.sum(stream, axis=1, keepdims=True) / width
    square = jnp.sum((stream - mean) ** 2, axis=1, keepdims=True)
    lane = lax.broadcasted_iota(jnp.int32, (rows, LANES), 1)
    table = jnp.zeros((rows, LANES), jnp.float32)
    for place, part in enumerate(in_three(mean) + in_three(square)):
        table = jnp.where(lane == place, part, table)
    if rows < LANES:
        table = jnp.concatenate(
            [table, jnp.zeros((LANES - rows, LANES), jnp.float32)], axis=0
        )
    stats = jnp.transpose(table)
    stats_ref[...] = stats[: stats_ref.shape[0]].astype(stats_ref.dtype)
    stats = stats[: rows - 2 * gain_ref.shape[0]]
    sent_ref[:, width:] = jnp.concatenate(
        [stats, gain_ref[...].astype(jnp.float32), bias_ref[...].astype(jnp.float32)],
        axis=0,
    ).astype(sent_ref.dtype)


def own_stream(residual, gain, bias, terms):
    rows, local = residual.shape
    blocks = local // LANES
    return pl.pallas_call(
        functools.partial(stream_kernel, len(terms)),
        out_shape=(
            jax.ShapeDtypeStruct((rows, local), jnp.bfloat16),
            jax.ShapeDtypeStruct((rows, local + LANES), jnp.bfloat16),
            jax.ShapeDtypeStruct((16, LANES), jnp.bfloat16),
        ),
        compiler_params=pltpu.CompilerParams(vmem_limit_bytes=8 * MIB),
        cost_estimate=pl.CostEstimate(
            flops=20 * rows * local, bytes_accessed=16 * rows * local, transcendentals=0
        ),
        name="own_stream",
    )(residual, gain.reshape(blocks, LANES), bias.reshape(blocks, LANES), *terms)


def nothing_kernel(*refs):
    del refs


def unchanged(piece, *after, cost=10**10):
    anywhere = pl.BlockSpec(memory_space=pl.ANY)
    return pl.pallas_call(
        nothing_kernel,
        out_shape=jax.ShapeDtypeStruct(piece.shape, piece.dtype),
        in_specs=[anywhere] * (1 + len(after)),
        out_specs=anywhere,
        input_output_aliases={0: 0},
        compiler_params=pltpu.CompilerParams(vmem_limit_bytes=MIB),
        cost_estimate=pl.CostEstimate(
            flops=cost, bytes_accessed=cost // 100, transcendentals=0
        ),
        name="unchanged",
    )(piece, *after)


def moments(tables, counts):
    whole = sum(counts)
    means, squares = [], jnp.zeros((1, LANES), jnp.float32)
    for table in tables:
        stats = table.astype(jnp.float32)
        means.append(stats[0:1] + stats[1:2] + stats[2:3])
        squares = squares + (stats[3:4] + stats[4:5] + stats[5:6])
    centre = sum(mean * (count / whole) for mean, count in zip(means, counts))
    for mean, count in zip(means, counts):
        squares = squares + count * ((mean - centre) * (mean - centre))
    return centre, squares


def merge_kernel(sent_ref, *refs):
    out_ref = refs[-1]
    rows = out_ref.shape[0]
    local = out_ref.shape[1] - LANES
    tables = [sent_ref[0:8, local:]] + [ref[0:8] for ref in refs[:-1]]
    centre, squares = moments(tables, [local] * len(tables))
    row = lax.broadcasted_iota(jnp.int32, (rows, LANES), 0)
    table = sent_ref[:, local:].astype(jnp.float32)
    for place, part in enumerate(in_three(centre) + in_three(squares)):
        table = jnp.where(row == place, part, table)
    out_ref[:, :local] = sent_ref[:, :local]
    out_ref[:, local:] = table.astype(out_ref.dtype)


def merge(sent, others):
    return pl.pallas_call(
        merge_kernel,
        out_shape=jax.ShapeDtypeStruct(sent.shape, sent.dtype),
        compiler_params=pltpu.CompilerParams(vmem_limit_bytes=4 * MIB),
        name="merge",
    )(sent, *others)


def coded_rows(piece, local, centre, inverse, table):
    rows, blocks = piece.shape[0], local // BLOCK_LEN
    unit = 1.0 / math.sqrt(BLOCK_LEN)
    scaling = piece[rows - 2 * blocks :, local:].astype(jnp.float32)
    normal = []
    for b in range(blocks):
        block = piece[:, b * BLOCK_LEN : (b + 1) * BLOCK_LEN].astype(jnp.float32)
        block = (block - centre) * inverse
        normal.append(block * scaling[b : b + 1] + scaling[blocks + b : blocks + b + 1])
    normal = jnp.concatenate(normal, axis=0)
    first = normal.astype(jnp.bfloat16)
    second = (normal - first.astype(jnp.float32)).astype(jnp.bfloat16)
    coded = jnp.dot(first, table, preferred_element_type=jnp.float32)
    coded = coded + jnp.dot(second, table, preferred_element_type=jnp.float32)
    coded = coded * unit
    largest = jnp.max(jnp.abs(coded), axis=1, keepdims=True)
    scales = (largest / 448.0 + 1e-06).astype(jnp.bfloat16).astype(jnp.float32)
    quanta = (coded * (1.0 / scales)).astype(jnp.bfloat16)
    back = jnp.dot(quanta, table, preferred_element_type=jnp.float32) * (scales * unit)
    return back.astype(jnp.bfloat16)


def finish_kernel(places, splits, counts, total, *refs):
    pieces, refs = refs[: len(places)], refs[len(places) :]
    rows = pieces[0].shape[0]
    width = pieces[0].shape[1] - LANES
    if counts:
        tables, (out_ref, columns_ref) = refs[: len(counts)], refs[-4:-2]
        centre, squares = moments([t[0:8, width:] for t in tables], counts)
        inverse = lax.rsqrt(squares / total + 1e-05)
        row = lax.broadcasted_iota(jnp.int32, (LANES, LANES), 0)
        table = jnp.where(row == 0, centre, jnp.where(row == 1, inverse, 0.0))
        columns = jnp.transpose(table)[:rows]
        columns_ref[...] = columns
    else:
        columns, out_ref = refs[0][...], refs[-3]
    done_ref, semaphores = refs[-2:]
    table = signs(BLOCK_LEN)
    me = lax.axis_index("tensor")
    outer, inner = me // splits[1], lax.rem(me, splits[1])
    copies = []
    for p, (k, j) in enumerate(places):
        back = coded_rows(pieces[p], width, columns[:, 0:1], columns[:, 1:2], table)
        for b in range(width // BLOCK_LEN):
            done_ref[p, :, b * BLOCK_LEN : (b + 1) * BLOCK_LEN] = back[
                b * rows : (b + 1) * rows
            ]
        owner = jnp.bitwise_xor(outer, k) * splits[1] + jnp.bitwise_xor(inner, j)
        place = pl.ds(pl.multiple_of(owner * width, LANES), width)
        copy = pltpu.make_async_copy(
            done_ref.at[p], out_ref.at[:, place], semaphores.at[p]
        )
        copy.start()
        copies.append(copy)
    for copy in copies:
        copy.wait()


def finish(places, splits, pieces, tables, counts, earlier, total):
    rows, local = pieces[0].shape[0], pieces[0].shape[1] - LANES
    count = len(pieces)
    vmem = pl.BlockSpec(memory_space=pltpu.VMEM)
    anywhere = pl.BlockSpec(memory_space=pl.ANY)
    given = tables + earlier[::-1]
    out_shape = [jax.ShapeDtypeStruct((rows, total), jnp.bfloat16)]
    if not earlier:
        out_shape.append(jax.ShapeDtypeStruct((rows, LANES), jnp.float32))
    return pl.pallas_call(
        functools.partial(finish_kernel, places, splits, counts, total),
        out_shape=out_shape,
        in_specs=[vmem] * (count + len(given) - len(earlier) // 2)
        + [anywhere] * (len(earlier) // 2),
        out_specs=[anywhere, vmem][: len(out_shape)],
        scratch_shapes=[
            pltpu.VMEM((count, rows, local), jnp.bfloat16),
            pltpu.SemaphoreType.DMA((count,)),
        ],
        input_output_aliases={count + len(given) - 1: 0} if earlier else {},
        compiler_params=pltpu.CompilerParams(vmem_limit_bytes=16 * MIB),
        cost_estimate=pl.CostEstimate(
            flops=8 * BLOCK_LEN * rows * local * count,
            bytes_accessed=4 * rows * local * count,
            transcendentals=0,
        ),
        name="finish",
    )(*pieces, *given)


def body(attended, out_weight, residual, norm_gain, norm_bias):
    n = lax.axis_size("tensor")
    nz, nx = splits = factors(n)
    rows = attended.shape[0]
    local = out_weight.shape[1] // n
    every = [(z, x) for z in range(nz) for x in range(nx)]
    swap = [[(z * nx + x, z * nx + (x ^ j)) for z, x in every] for j in range(nx)]
    jump = [[(z * nx + x, (z ^ k) * nx + x) for z, x in every] for k in range(nz)]

    away = [[(k, j) for j in range(1, nx)] for k in range(nz)]
    here = [[(k, 0)] for k in range(nz)]
    order = list(range(nz - 1, -1, -1))
    calls = [away[order[0]], away[order[1]] + away[order[2]] + here[order[0]]]
    for i in range(2, nz - 1):
        calls.append(away[order[i + 1]] + here[order[i - 1]])
    calls[-1] = calls[-1] + here[1]
    calls.append(here[0])
    joins = [[]] + [[k] for k in order[:-1]] + [[]]
    joins[-3:] = [joins[-3] + joins[-2], []]
    terms = {k: [] for k in range(nz)}
    after, held, released = [], [], []
    for targets, joined in zip(calls, joins):
        results = products(
            attended, out_weight, targets, splits, local, after + released
        )
        after = [results[-1]]
        for (k, j), result in zip(targets, results):
            if j and k:
                result = lax.ppermute(result, "tensor", swap[j])
            if j and not k:
                held.append((result, swap[j]))
            else:
                terms[k].append(result)
        for k in joined:
            bit = k & -k
            total = terms[k][0].astype(jnp.float32)
            for term in terms[k][1:]:
                total = total + term.astype(jnp.float32)
            total = total.astype(jnp.bfloat16)
            after = [total]
            if k == 2:
                for piece, pairs in held:
                    piece = unchanged(piece, total, cost=0)
                    released.append(piece)
                    piece = lax.ppermute(piece, "tensor", pairs)
                    terms[0].append(piece)
            joined_to = lax.ppermute(total, "tensor", jump[bit])
            if k == nz // 2:
                joined_to = unchanged(joined_to)
            terms[k ^ bit].append(joined_to)

    stream_out, sent, stats = own_stream(residual, norm_gain, norm_bias, terms[0])
    others = [lax.ppermute(stats, "tensor", swap[j]) for j in range(1, nx)]
    merged = merge(sent, others)
    have = {0: merged, 1: lax.ppermute(sent, "tensor", jump[1])}
    crossed = {}
    top = nz // 2
    have[top] = lax.ppermute(merged, "tensor", jump[top])
    for k, j in away[0] + away[1]:
        crossed[k, j] = lax.ppermute(have[k] if k else sent, "tensor", swap[j])
    have[top] = unchanged(have[top], *crossed.values())
    for k in sorted(range(2, nz), key=lambda k: (k & (k - 1), k)):
        if k != top:
            have[k] = lax.ppermute(have[k ^ (k & -k)], "tensor", jump[k & -k])
    places = [place for k in range(nz) for place in here[k] + away[k]]
    for k, j in places:
        if j and k > 1:
            crossed[k, j] = lax.ppermute(have[k], "tensor", swap[j])
    pieces = {(k, j): crossed[k, j] if j else have[k] for k, j in places}
    alone = here[1] + away[1]
    tables = [have[k] for k in range(nz) if k != 1] + [pieces[p] for p in alone]
    counts = [nx * local] * (nz - 1) + [local] * len(alone)
    first, last = places[: 1 - nx], places[1 - nx :]
    result = finish(first, splits, [pieces[p] for p in first], tables, counts, [], n * local)
    result = finish(last, splits, [pieces[p] for p in last], [], [], list(result), n * local)
    return (stream_out, result[0])


def solution(mesh):
    placed = (
        P(("groups", "dp"), "tensor"),
        P("tensor", None),
        P(("groups", "dp"), "tensor"),
        P("tensor"),
        P("tensor"),
    )
    return jax.shard_map(
        body,
        mesh=mesh,
        in_specs=placed,
        out_specs=(P(("groups", "dp"), "tensor"), P(("groups", "dp"), None)),
        check_vma=False,
    )
```

```python
import functools
import math

import jax
import jax.numpy as jnp
from jax import lax
from jax.experimental import pallas as pl
from jax.experimental.pallas import tpu as pltpu
from jax.sharding import PartitionSpec as P

BLOCK_LEN = 128
LANES = 128
MIB = 1024 * 1024


def factors(n):
    inner = 1 << ((n.bit_length() - 1) // 2)
    return n // inner, inner


def tile_width(width, most):
    while width % most:
        most //= 2
    return most


def signs(length):
    rows = lax.broadcasted_iota(jnp.int32, (length, length), 0)
    columns = lax.broadcasted_iota(jnp.int32, (length, length), 1)
    common = jnp.bitwise_and(rows, columns)
    parity = jnp.zeros((length, length), jnp.int32)
    for bit_index in range(length.bit_length() - 1):
        parity = parity + jnp.bitwise_and(jnp.right_shift(common, bit_index), 1)
    return (1 - 2 * jnp.bitwise_and(parity, 1)).astype(jnp.bfloat16)


def product_kernel(targets, splits, local, tile, rows_ref, weight_ref, *refs):
    count = len(targets)
    held, scratch, semaphores = refs[-3:]
    outs = refs[-3 - count : -3]
    nx, per = splits[1], local // tile
    me = lax.axis_index("tensor")
    outer, inner = me // nx, lax.rem(me, nx)
    first = pltpu.make_async_copy(rows_ref, held, semaphores.at[count * per])
    first.start()
    copies = []
    for t, (k, j) in enumerate(targets):
        owner = jnp.bitwise_xor(outer, k) * nx + jnp.bitwise_xor(inner, j)
        for i in range(per):
            start = pl.multiple_of(owner * local + i * tile, LANES)
            copy = pltpu.make_async_copy(
                weight_ref.at[:, pl.ds(start, tile)],
                scratch.at[t * per + i],
                semaphores.at[t * per + i],
            )
            copy.start()
            copies.append(copy)
    first.wait()
    for t in range(count):
        for i in range(per):
            copies[t * per + i].wait()
            outs[t][:, i * tile : (i + 1) * tile] = jnp.dot(
                held[...], scratch[t * per + i], preferred_element_type=jnp.float32
            ).astype(outs[t].dtype)


def products(attended, weight, targets, splits, local, after):
    rows, depth = attended.shape
    tile = tile_width(local, 512)
    slots = len(targets) * (local // tile)
    vmem = pl.BlockSpec(memory_space=pltpu.VMEM)
    return pl.pallas_call(
        functools.partial(product_kernel, targets, splits, local, tile),
        out_shape=[
            jax.ShapeDtypeStruct((rows, local), jnp.bfloat16 if j else jnp.float32)
            for _, j in targets
        ],
        in_specs=[pl.BlockSpec(memory_space=pltpu.HBM)] * 2
        + [pl.BlockSpec(memory_space=pl.ANY)] * len(after),
        out_specs=[vmem] * len(targets),
        scratch_shapes=[
            pltpu.VMEM((rows, depth), jnp.bfloat16),
            pltpu.VMEM((slots, depth, tile), jnp.bfloat16),
            pltpu.SemaphoreType.DMA((slots + 1,)),
        ],
        compiler_params=pltpu.CompilerParams(
            vmem_limit_bytes=40 * MIB
        ),
        cost_estimate=pl.CostEstimate(
            flops=2 * rows * depth * local * len(targets),
            bytes_accessed=2 * depth * local * len(targets),
            transcendentals=0,
        ),
        name="products",
    )(attended, weight, *after)


def in_three(values):
    parts = []
    for _ in range(3):
        part = values.astype(jnp.bfloat16)
        parts.append(part.astype(jnp.float32))
        values = values - parts[-1]
    return parts


def stream_kernel(count, residual_ref, gain_ref, bias_ref, *refs):
    terms, (half_ref, sent_ref, stats_ref) = refs[:count], refs[count:]
    stream = residual_ref[...].astype(jnp.float32)
    for term in terms:
        stream = stream + term[...].astype(jnp.float32)
    rows, width = stream.shape
    half = stream.astype(half_ref.dtype)
    half_ref[...] = half
    sent_ref[:, :width] = half
    mean = jnp.sum(stream, axis=1, keepdims=True) / width
    square = jnp.sum((stream - mean) ** 2, axis=1, keepdims=True)
    lane = lax.broadcasted_iota(jnp.int32, (rows, LANES), 1)
    table = jnp.zeros((rows, LANES), jnp.float32)
    for place, part in enumerate(in_three(mean) + in_three(square)):
        table = jnp.where(lane == place, part, table)
    if rows < LANES:
        table = jnp.concatenate(
            [table, jnp.zeros((LANES - rows, LANES), jnp.float32)], axis=0
        )
    stats = jnp.transpose(table)
    stats_ref[...] = stats[: stats_ref.shape[0]].astype(stats_ref.dtype)
    stats = stats[: rows - 2 * gain_ref.shape[0]]
    sent_ref[:, width:] = jnp.concatenate(
        [stats, gain_ref[...].astype(jnp.float32), bias_ref[...].astype(jnp.float32)],
        axis=0,
    ).astype(sent_ref.dtype)


def own_stream(residual, gain, bias, terms):
    rows, local = residual.shape
    blocks = local // LANES
    return pl.pallas_call(
        functools.partial(stream_kernel, len(terms)),
        out_shape=(
            jax.ShapeDtypeStruct((rows, local), jnp.bfloat16),
            jax.ShapeDtypeStruct((rows, local + LANES), jnp.bfloat16),
            jax.ShapeDtypeStruct((16, LANES), jnp.bfloat16),
        ),
        compiler_params=pltpu.CompilerParams(vmem_limit_bytes=8 * MIB),
        cost_estimate=pl.CostEstimate(
            flops=20 * rows * local, bytes_accessed=16 * rows * local, transcendentals=0
        ),
        name="own_stream",
    )(residual, gain.reshape(blocks, LANES), bias.reshape(blocks, LANES), *terms)


def nothing_kernel(*refs):
    del refs


def unchanged(piece, *after, cost=10**10):
    anywhere = pl.BlockSpec(memory_space=pl.ANY)
    return pl.pallas_call(
        nothing_kernel,
        out_shape=jax.ShapeDtypeStruct(piece.shape, piece.dtype),
        in_specs=[anywhere] * (1 + len(after)),
        out_specs=anywhere,
        input_output_aliases={0: 0},
        compiler_params=pltpu.CompilerParams(vmem_limit_bytes=MIB),
        cost_estimate=pl.CostEstimate(
            flops=cost, bytes_accessed=cost // 100, transcendentals=0
        ),
        name="unchanged",
    )(piece, *after)


def moments(tables, counts):
    whole = sum(counts)
    means, squares = [], jnp.zeros((1, LANES), jnp.float32)
    for table in tables:
        stats = table.astype(jnp.float32)
        means.append(stats[0:1] + stats[1:2] + stats[2:3])
        squares = squares + (stats[3:4] + stats[4:5] + stats[5:6])
    centre = sum(mean * (count / whole) for mean, count in zip(means, counts))
    for mean, count in zip(means, counts):
        squares = squares + count * ((mean - centre) * (mean - centre))
    return centre, squares


def merge_kernel(sent_ref, *refs):
    out_ref = refs[-1]
    rows = out_ref.shape[0]
    local = out_ref.shape[1] - LANES
    tables = [sent_ref[0:8, local:]] + [ref[0:8] for ref in refs[:-1]]
    centre, squares = moments(tables, [local] * len(tables))
    row = lax.broadcasted_iota(jnp.int32, (rows, LANES), 0)
    table = sent_ref[:, local:].astype(jnp.float32)
    for place, part in enumerate(in_three(centre) + in_three(squares)):
        table = jnp.where(row == place, part, table)
    out_ref[:, :local] = sent_ref[:, :local]
    out_ref[:, local:] = table.astype(out_ref.dtype)


def merge(sent, others):
    return pl.pallas_call(
        merge_kernel,
        out_shape=jax.ShapeDtypeStruct(sent.shape, sent.dtype),
        compiler_params=pltpu.CompilerParams(vmem_limit_bytes=4 * MIB),
        name="merge",
    )(sent, *others)


def coded_rows(piece, local, centre, inverse, table):
    rows, blocks = piece.shape[0], local // BLOCK_LEN
    unit = 1.0 / math.sqrt(BLOCK_LEN)
    scaling = piece[rows - 2 * blocks :, local:].astype(jnp.float32)
    normal = []
    for b in range(blocks):
        block = piece[:, b * BLOCK_LEN : (b + 1) * BLOCK_LEN].astype(jnp.float32)
        block = (block - centre) * inverse
        normal.append(block * scaling[b : b + 1] + scaling[blocks + b : blocks + b + 1])
    normal = jnp.concatenate(normal, axis=0)
    first = normal.astype(jnp.bfloat16)
    second = (normal - first.astype(jnp.float32)).astype(jnp.bfloat16)
    coded = jnp.dot(first, table, preferred_element_type=jnp.float32)
    coded = coded + jnp.dot(second, table, preferred_element_type=jnp.float32)
    coded = coded * unit
    largest = jnp.max(jnp.abs(coded), axis=1, keepdims=True)
    scales = (largest / 448.0 + 1e-06).astype(jnp.bfloat16).astype(jnp.float32)
    quanta = (coded * (1.0 / scales)).astype(jnp.bfloat16)
    back = jnp.dot(quanta, table, preferred_element_type=jnp.float32) * (scales * unit)
    return back.astype(jnp.bfloat16)


def finish_kernel(places, splits, counts, total, *refs):
    pieces, refs = refs[: len(places)], refs[len(places) :]
    rows = pieces[0].shape[0]
    width = pieces[0].shape[1] - LANES
    if counts:
        tables, (out_ref, columns_ref) = refs[: len(counts)], refs[-4:-2]
        centre, squares = moments([t[0:8, width:] for t in tables], counts)
        inverse = lax.rsqrt(squares / total + 1e-05)
        row = lax.broadcasted_iota(jnp.int32, (LANES, LANES), 0)
        table = jnp.where(row == 0, centre, jnp.where(row == 1, inverse, 0.0))
        columns = jnp.transpose(table)[:rows]
        columns_ref[...] = columns
    else:
        columns, out_ref = refs[0][...], refs[-3]
    done_ref, semaphores = refs[-2:]
    table = signs(BLOCK_LEN)
    me = lax.axis_index("tensor")
    outer, inner = me // splits[1], lax.rem(me, splits[1])
    copies = []
    for p, (k, j) in enumerate(places):
        back = coded_rows(pieces[p], width, columns[:, 0:1], columns[:, 1:2], table)
        for b in range(width // BLOCK_LEN):
            done_ref[p, :, b * BLOCK_LEN : (b + 1) * BLOCK_LEN] = back[
                b * rows : (b + 1) * rows
            ]
        owner = jnp.bitwise_xor(outer, k) * splits[1] + jnp.bitwise_xor(inner, j)
        place = pl.ds(pl.multiple_of(owner * width, LANES), width)
        copy = pltpu.make_async_copy(
            done_ref.at[p], out_ref.at[:, place], semaphores.at[p]
        )
        copy.start()
        copies.append(copy)
    for copy in copies:
        copy.wait()


def finish(places, splits, pieces, tables, counts, earlier, total):
    rows, local = pieces[0].shape[0], pieces[0].shape[1] - LANES
    count = len(pieces)
    vmem = pl.BlockSpec(memory_space=pltpu.VMEM)
    anywhere = pl.BlockSpec(memory_space=pl.ANY)
    given = tables + earlier[::-1]
    out_shape = [jax.ShapeDtypeStruct((rows, total), jnp.bfloat16)]
    if not earlier:
        out_shape.append(jax.ShapeDtypeStruct((rows, LANES), jnp.float32))
    return pl.pallas_call(
        functools.partial(finish_kernel, places, splits, counts, total),
        out_shape=out_shape,
        in_specs=[vmem] * (count + len(given) - len(earlier) // 2)
        + [anywhere] * (len(earlier) // 2),
        out_specs=[anywhere, vmem][: len(out_shape)],
        scratch_shapes=[
            pltpu.VMEM((count, rows, local), jnp.bfloat16),
            pltpu.SemaphoreType.DMA((count,)),
        ],
        input_output_aliases={count + len(given) - 1: 0} if earlier else {},
        compiler_params=pltpu.CompilerParams(vmem_limit_bytes=16 * MIB),
        cost_estimate=pl.CostEstimate(
            flops=8 * BLOCK_LEN * rows * local * count,
            bytes_accessed=4 * rows * local * count,
            transcendentals=0,
        ),
        name="finish",
    )(*pieces, *given)


def body(attended, out_weight, residual, norm_gain, norm_bias):
    n = lax.axis_size("tensor")
    nz, nx = splits = factors(n)
    rows = attended.shape[0]
    local = out_weight.shape[1] // n
    every = [(z, x) for z in range(nz) for x in range(nx)]
    swap = [[(z * nx + x, z * nx + (x ^ j)) for z, x in every] for j in range(nx)]
    jump = [[(z * nx + x, (z ^ k) * nx + x) for z, x in every] for k in range(nz)]

    away = [[(k, j) for j in range(1, nx)] for k in range(nz)]
    here = [[(k, 0)] for k in range(nz)]
    order = list(range(nz - 1, -1, -1))
    calls = [away[order[0]], away[order[1]] + away[order[2]] + here[order[0]]]
    for i in range(2, nz - 1):
        calls.append(away[order[i + 1]] + here[order[i - 1]])
    calls[-1] = calls[-1] + here[1]
    calls.append(here[0])
    joins = [[]] + [[k] for k in order[:-1]] + [[]]
    joins[-3:] = [joins[-3] + joins[-2], []]
    terms = {k: [] for k in range(nz)}
    after, held, released = [], [], []
    for targets, joined in zip(calls, joins):
        results = products(
            attended, out_weight, targets, splits, local, after + released
        )
        after = [results[-1]]
        for (k, j), result in zip(targets, results):
            if j and k:
                result = lax.ppermute(result, "tensor", swap[j])
            if j and not k:
                held.append((result, swap[j]))
            else:
                terms[k].append(result)
        for k in joined:
            bit = k & -k
            total = terms[k][0].astype(jnp.float32)
            for term in terms[k][1:]:
                total = total + term.astype(jnp.float32)
            total = total.astype(jnp.bfloat16)
            after = [total]
            if k == 2:
                for piece, pairs in held:
                    piece = unchanged(piece, total, cost=0)
                    released.append(piece)
                    piece = lax.ppermute(piece, "tensor", pairs)
                    terms[0].append(piece)
            joined_to = lax.ppermute(total, "tensor", jump[bit])
            if k == nz // 2:
                joined_to = unchanged(joined_to)
            terms[k ^ bit].append(joined_to)

    stream_out, sent, stats = own_stream(residual, norm_gain, norm_bias, terms[0])
    others = [lax.ppermute(stats, "tensor", swap[j]) for j in range(1, nx)]
    merged = merge(sent, others)
    have = {0: merged, 1: lax.ppermute(sent, "tensor", jump[1])}
    crossed = {}
    top = nz // 2
    have[top] = lax.ppermute(merged, "tensor", jump[top])
    for k, j in away[0] + away[1]:
        crossed[k, j] = lax.ppermute(have[k] if k else sent, "tensor", swap[j])
    have[top] = unchanged(have[top], have[1], *[crossed[p] for p in away[0]])
    for p in away[1]:
        crossed[p] = unchanged(unchanged(crossed[p]))
    for k in sorted(range(2, nz), key=lambda k: (k & (k - 1), k)):
        if k != top:
            have[k] = lax.ppermute(have[k ^ (k & -k)], "tensor", jump[k & -k])
    places = [place for k in range(nz) for place in here[k] + away[k]]
    for k, j in places:
        if j and k > 1:
            crossed[k, j] = lax.ppermute(have[k], "tensor", swap[j])
    pieces = {(k, j): crossed[k, j] if j else have[k] for k, j in places}
    alone = here[1] + away[1]
    tables = [have[k] for k in range(nz) if k != 1] + [pieces[p] for p in alone]
    counts = [nx * local] * (nz - 1) + [local] * len(alone)
    first, last = places[: 1 - nx], places[1 - nx :]
    result = finish(first, splits, [pieces[p] for p in first], tables, counts, [], n * local)
    result = finish(last, splits, [pieces[p] for p in last], [], [], list(result), n * local)
    return (stream_out, result[0])


def solution(mesh):
    placed = (
        P(("groups", "dp"), "tensor"),
        P("tensor", None),
        P(("groups", "dp"), "tensor"),
        P("tensor"),
        P("tensor"),
    )
    return jax.shard_map(
        body,
        mesh=mesh,
        in_specs=placed,
        out_specs=(P(("groups", "dp"), "tensor"), P(("groups", "dp"), None)),
        check_vma=False,
    )
```

```python
import functools
import math

import jax
import jax.numpy as jnp
from jax import lax
from jax.experimental import pallas as pl
from jax.experimental.pallas import tpu as pltpu
from jax.sharding import PartitionSpec as P

BLOCK_LEN = 128
LANES = 128
MIB = 1024 * 1024


def factors(n):
    inner = 1 << ((n.bit_length() - 1) // 2)
    return n // inner, inner


def tile_width(width, most):
    while width % most:
        most //= 2
    return most


def signs(length):
    rows = lax.broadcasted_iota(jnp.int32, (length, length), 0)
    columns = lax.broadcasted_iota(jnp.int32, (length, length), 1)
    common = jnp.bitwise_and(rows, columns)
    parity = jnp.zeros((length, length), jnp.int32)
    for bit_index in range(length.bit_length() - 1):
        parity = parity + jnp.bitwise_and(jnp.right_shift(common, bit_index), 1)
    return (1 - 2 * jnp.bitwise_and(parity, 1)).astype(jnp.bfloat16)


def product_kernel(targets, splits, local, tile, rows_ref, weight_ref, *refs):
    count = len(targets)
    scratch, semaphores = refs[-2:]
    outs = refs[-2 - count : -2]
    nx, per = splits[1], local // tile
    me = lax.axis_index("tensor")
    outer, inner = me // nx, lax.rem(me, nx)
    copies = []
    for t, (k, j) in enumerate(targets):
        owner = jnp.bitwise_xor(outer, k) * nx + jnp.bitwise_xor(inner, j)
        for i in range(per):
            start = pl.multiple_of(owner * local + i * tile, LANES)
            copy = pltpu.make_async_copy(
                weight_ref.at[:, pl.ds(start, tile)],
                scratch.at[t * per + i],
                semaphores.at[t * per + i],
            )
            copy.start()
            copies.append(copy)
    for t in range(count):
        for i in range(per):
            copies[t * per + i].wait()
            outs[t][:, i * tile : (i + 1) * tile] = jnp.dot(
                rows_ref[...], scratch[t * per + i], preferred_element_type=jnp.float32
            ).astype(outs[t].dtype)


def products(attended, weight, targets, splits, local, after):
    rows, depth = attended.shape
    tile = tile_width(local, 512)
    slots = len(targets) * (local // tile)
    vmem = pl.BlockSpec(memory_space=pltpu.VMEM)
    return pl.pallas_call(
        functools.partial(product_kernel, targets, splits, local, tile),
        out_shape=[
            jax.ShapeDtypeStruct((rows, local), jnp.bfloat16 if j else jnp.float32)
            for _, j in targets
        ],
        in_specs=[vmem, pl.BlockSpec(memory_space=pltpu.HBM)]
        + [pl.BlockSpec(memory_space=pl.ANY)] * len(after),
        out_specs=[vmem] * len(targets),
        scratch_shapes=[
            pltpu.VMEM((slots, depth, tile), jnp.bfloat16),
            pltpu.SemaphoreType.DMA((slots,)),
        ],
        compiler_params=pltpu.CompilerParams(
            vmem_limit_bytes=40 * MIB
        ),
        cost_estimate=pl.CostEstimate(
            flops=2 * rows * depth * local * len(targets),
            bytes_accessed=2 * depth * local * len(targets),
            transcendentals=0,
        ),
        name="products",
    )(attended, weight, *after)


def in_three(values):
    parts = []
    for _ in range(3):
        part = values.astype(jnp.bfloat16)
        parts.append(part.astype(jnp.float32))
        values = values - parts[-1]
    return parts


def stream_kernel(count, residual_ref, gain_ref, bias_ref, *refs):
    terms, (half_ref, sent_ref, stats_ref) = refs[:count], refs[count:]
    stream = residual_ref[...].astype(jnp.float32)
    for term in terms:
        stream = stream + term[...].astype(jnp.float32)
    rows, width = stream.shape
    half = stream.astype(half_ref.dtype)
    half_ref[...] = half
    sent_ref[:, :width] = half
    mean = jnp.sum(stream, axis=1, keepdims=True) / width
    square = jnp.sum((stream - mean) ** 2, axis=1, keepdims=True)
    lane = lax.broadcasted_iota(jnp.int32, (rows, LANES), 1)
    table = jnp.zeros((rows, LANES), jnp.float32)
    for place, part in enumerate(in_three(mean) + in_three(square)):
        table = jnp.where(lane == place, part, table)
    if rows < LANES:
        table = jnp.concatenate(
            [table, jnp.zeros((LANES - rows, LANES), jnp.float32)], axis=0
        )
    stats = jnp.transpose(table)
    stats_ref[...] = stats[: stats_ref.shape[0]].astype(stats_ref.dtype)
    stats = stats[: rows - 2 * gain_ref.shape[0]]
    sent_ref[:, width:] = jnp.concatenate(
        [stats, gain_ref[...].astype(jnp.float32), bias_ref[...].astype(jnp.float32)],
        axis=0,
    ).astype(sent_ref.dtype)


def own_stream(residual, gain, bias, terms):
    rows, local = residual.shape
    blocks = local // LANES
    return pl.pallas_call(
        functools.partial(stream_kernel, len(terms)),
        out_shape=(
            jax.ShapeDtypeStruct((rows, local), jnp.bfloat16),
            jax.ShapeDtypeStruct((rows, local + LANES), jnp.bfloat16),
            jax.ShapeDtypeStruct((16, LANES), jnp.bfloat16),
        ),
        compiler_params=pltpu.CompilerParams(vmem_limit_bytes=8 * MIB),
        cost_estimate=pl.CostEstimate(
            flops=20 * rows * local, bytes_accessed=16 * rows * local, transcendentals=0
        ),
        name="own_stream",
    )(residual, gain.reshape(blocks, LANES), bias.reshape(blocks, LANES), *terms)


def nothing_kernel(*refs):
    del refs


def unchanged(piece, *after, cost=10**10):
    anywhere = pl.BlockSpec(memory_space=pl.ANY)
    return pl.pallas_call(
        nothing_kernel,
        out_shape=jax.ShapeDtypeStruct(piece.shape, piece.dtype),
        in_specs=[anywhere] * (1 + len(after)),
        out_specs=anywhere,
        input_output_aliases={0: 0},
        compiler_params=pltpu.CompilerParams(vmem_limit_bytes=MIB),
        cost_estimate=pl.CostEstimate(
            flops=cost, bytes_accessed=cost // 100, transcendentals=0
        ),
        name="unchanged",
    )(piece, *after)


def moments(tables, counts):
    whole = sum(counts)
    means, squares = [], jnp.zeros((1, LANES), jnp.float32)
    for table in tables:
        stats = table.astype(jnp.float32)
        means.append(stats[0:1] + stats[1:2] + stats[2:3])
        squares = squares + (stats[3:4] + stats[4:5] + stats[5:6])
    centre = sum(mean * (count / whole) for mean, count in zip(means, counts))
    for mean, count in zip(means, counts):
        squares = squares + count * ((mean - centre) * (mean - centre))
    return centre, squares


def merge_kernel(sent_ref, *refs):
    out_ref = refs[-1]
    rows = out_ref.shape[0]
    local = out_ref.shape[1] - LANES
    tables = [sent_ref[0:8, local:]] + [ref[0:8] for ref in refs[:-1]]
    centre, squares = moments(tables, [local] * len(tables))
    row = lax.broadcasted_iota(jnp.int32, (rows, LANES), 0)
    table = sent_ref[:, local:].astype(jnp.float32)
    for place, part in enumerate(in_three(centre) + in_three(squares)):
        table = jnp.where(row == place, part, table)
    out_ref[:, :local] = sent_ref[:, :local]
    out_ref[:, local:] = table.astype(out_ref.dtype)


def merge(sent, others):
    return pl.pallas_call(
        merge_kernel,
        out_shape=jax.ShapeDtypeStruct(sent.shape, sent.dtype),
        compiler_params=pltpu.CompilerParams(vmem_limit_bytes=4 * MIB),
        name="merge",
    )(sent, *others)


def coded_rows(piece, local, centre, inverse, table):
    rows, blocks = piece.shape[0], local // BLOCK_LEN
    unit = 1.0 / math.sqrt(BLOCK_LEN)
    scaling = piece[rows - 2 * blocks :, local:].astype(jnp.float32)
    normal = []
    for b in range(blocks):
        block = piece[:, b * BLOCK_LEN : (b + 1) * BLOCK_LEN].astype(jnp.float32)
        block = (block - centre) * inverse
        normal.append(block * scaling[b : b + 1] + scaling[blocks + b : blocks + b + 1])
    normal = jnp.concatenate(normal, axis=0)
    first = normal.astype(jnp.bfloat16)
    second = (normal - first.astype(jnp.float32)).astype(jnp.bfloat16)
    coded = jnp.dot(first, table, preferred_element_type=jnp.float32)
    coded = coded + jnp.dot(second, table, preferred_element_type=jnp.float32)
    coded = coded * unit
    largest = jnp.max(jnp.abs(coded), axis=1, keepdims=True)
    scales = (largest / 448.0 + 1e-06).astype(jnp.bfloat16).astype(jnp.float32)
    quanta = (coded * (1.0 / scales)).astype(jnp.bfloat16)
    back = jnp.dot(quanta, table, preferred_element_type=jnp.float32) * (scales * unit)
    return back.astype(jnp.bfloat16)


def finish_kernel(places, splits, counts, total, *refs):
    pieces, refs = refs[: len(places)], refs[len(places) :]
    rows = pieces[0].shape[0]
    width = pieces[0].shape[1] - LANES
    if counts:
        tables, (out_ref, columns_ref) = refs[: len(counts)], refs[-4:-2]
        centre, squares = moments([t[0:8, width:] for t in tables], counts)
        inverse = lax.rsqrt(squares / total + 1e-05)
        row = lax.broadcasted_iota(jnp.int32, (LANES, LANES), 0)
        table = jnp.where(row == 0, centre, jnp.where(row == 1, inverse, 0.0))
        columns = jnp.transpose(table)[:rows]
        columns_ref[...] = columns
    else:
        columns, out_ref = refs[0][...], refs[-3]
    done_ref, semaphores = refs[-2:]
    table = signs(BLOCK_LEN)
    me = lax.axis_index("tensor")
    outer, inner = me // splits[1], lax.rem(me, splits[1])
    copies = []
    for p, (k, j) in enumerate(places):
        back = coded_rows(pieces[p], width, columns[:, 0:1], columns[:, 1:2], table)
        for b in range(width // BLOCK_LEN):
            done_ref[p, :, b * BLOCK_LEN : (b + 1) * BLOCK_LEN] = back[
                b * rows : (b + 1) * rows
            ]
        owner = jnp.bitwise_xor(outer, k) * splits[1] + jnp.bitwise_xor(inner, j)
        place = pl.ds(pl.multiple_of(owner * width, LANES), width)
        copy = pltpu.make_async_copy(
            done_ref.at[p], out_ref.at[:, place], semaphores.at[p]
        )
        copy.start()
        copies.append(copy)
    for copy in copies:
        copy.wait()


def finish(places, splits, pieces, tables, counts, earlier, total):
    rows, local = pieces[0].shape[0], pieces[0].shape[1] - LANES
    count = len(pieces)
    vmem = pl.BlockSpec(memory_space=pltpu.VMEM)
    anywhere = pl.BlockSpec(memory_space=pl.ANY)
    given = tables + earlier[::-1]
    out_shape = [jax.ShapeDtypeStruct((rows, total), jnp.bfloat16)]
    if not earlier:
        out_shape.append(jax.ShapeDtypeStruct((rows, LANES), jnp.float32))
    return pl.pallas_call(
        functools.partial(finish_kernel, places, splits, counts, total),
        out_shape=out_shape,
        in_specs=[vmem] * (count + len(given) - len(earlier) // 2)
        + [anywhere] * (len(earlier) // 2),
        out_specs=[anywhere, vmem][: len(out_shape)],
        scratch_shapes=[
            pltpu.VMEM((count, rows, local), jnp.bfloat16),
            pltpu.SemaphoreType.DMA((count,)),
        ],
        input_output_aliases={count + len(given) - 1: 0} if earlier else {},
        compiler_params=pltpu.CompilerParams(vmem_limit_bytes=16 * MIB),
        cost_estimate=pl.CostEstimate(
            flops=8 * BLOCK_LEN * rows * local * count,
            bytes_accessed=4 * rows * local * count,
            transcendentals=0,
        ),
        name="finish",
    )(*pieces, *given)


def body(attended, out_weight, residual, norm_gain, norm_bias):
    n = lax.axis_size("tensor")
    nz, nx = splits = factors(n)
    rows = attended.shape[0]
    local = out_weight.shape[1] // n
    every = [(z, x) for z in range(nz) for x in range(nx)]
    swap = [[(z * nx + x, z * nx + (x ^ j)) for z, x in every] for j in range(nx)]
    jump = [[(z * nx + x, (z ^ k) * nx + x) for z, x in every] for k in range(nz)]

    away = [[(k, j) for j in range(1, nx)] for k in range(nz)]
    here = [[(k, 0)] for k in range(nz)]
    order = list(range(nz - 1, -1, -1))
    calls = [away[order[0]], away[order[1]] + away[order[2]] + here[order[0]]]
    for i in range(2, nz - 1):
        calls.append(away[order[i + 1]] + here[order[i - 1]])
    calls[-1] = calls[-1] + here[1]
    calls.append(here[0])
    joins = [[]] + [[k] for k in order[:-1]] + [[]]
    joins[-3:] = [joins[-3] + joins[-2], []]
    terms = {k: [] for k in range(nz)}
    after, held, released = [], [], []
    for targets, joined in zip(calls, joins):
        results = products(
            attended, out_weight, targets, splits, local, after + released
        )
        after = [results[-1]]
        for (k, j), result in zip(targets, results):
            if j and k:
                result = lax.ppermute(result, "tensor", swap[j])
            if j and not k:
                held.append((result, swap[j]))
            else:
                terms[k].append(result)
        for k in joined:
            bit = k & -k
            total = terms[k][0].astype(jnp.float32)
            for term in terms[k][1:]:
                total = total + term.astype(jnp.float32)
            total = total.astype(jnp.bfloat16)
            after = [total]
            if k == 2:
                for piece, pairs in held:
                    piece = unchanged(piece, total, cost=0)
                    released.append(piece)
                    piece = lax.ppermute(piece, "tensor", pairs)
                    terms[0].append(piece)
            joined_to = lax.ppermute(total, "tensor", jump[bit])
            if k == nz // 2:
                joined_to = unchanged(joined_to)
            terms[k ^ bit].append(joined_to)

    stream_out, sent, stats = own_stream(residual, norm_gain, norm_bias, terms[0])
    others = [lax.ppermute(stats, "tensor", swap[j]) for j in range(1, nx)]
    merged = merge(sent, others)
    have = {0: merged, 1: lax.ppermute(sent, "tensor", jump[1])}
    crossed = {}
    top = nz // 2
    have[top] = lax.ppermute(merged, "tensor", jump[top])
    for k, j in away[0] + away[1]:
        crossed[k, j] = lax.ppermute(have[k] if k else sent, "tensor", swap[j])
    have[top] = unchanged(have[top], *crossed.values())
    for k in sorted(range(2, nz), key=lambda k: (k & (k - 1), k)):
        if k != top:
            have[k] = lax.ppermute(have[k ^ (k & -k)], "tensor", jump[k & -k])
    places = [place for k in range(nz) for place in here[k] + away[k]]
    for k, j in places:
        if j and k > 1:
            crossed[k, j] = lax.ppermute(have[k], "tensor", swap[j])
    pieces = {(k, j): crossed[k, j] if j else have[k] for k, j in places}
    alone = here[1] + away[1]
    tables = [have[k] for k in range(nz) if k != 1] + [pieces[p] for p in alone]
    counts = [nx * local] * (nz - 1) + [local] * len(alone)
    first, last = places[: 1 - nx], places[1 - nx :]
    result = finish(first, splits, [pieces[p] for p in first], tables, counts, [], n * local)
    result = finish(last, splits, [pieces[p] for p in last], [], [], list(result), n * local)
    return (stream_out, result[0])


def solution(mesh):
    placed = (
        P(("groups", "dp"), "tensor"),
        P("tensor", None),
        P(("groups", "dp"), "tensor"),
        P("tensor"),
        P("tensor"),
    )
    return jax.shard_map(
        body,
        mesh=mesh,
        in_specs=placed,
        out_specs=(P(("groups", "dp"), "tensor"), P(("groups", "dp"), None)),
        check_vma=False,
    )
```
